32 devices in a mesh: tiles: 2 (over y), date: 4 (over z), space: 4 (over x, core).
Axes of the slice: x: 2, y: 2, z: 4, core: 2. Of those that a mesh axis runs over, the one named last changes fastest.
Arguments:
- reflect: float32 [8, 6, 8192], P('date', None, ('tiles', 'space')), parts along dimension 2, may hold values from -0.05 to 1.05
- clear_sky: int32 [8, 8192], P('date', ('tiles', 'space')), parts along dimension 1, may hold values 0 or 1
- live_dates: int32 [4], replicated, may hold values from 1 to 2, as said below
- day_of_year: int32 [8], replicated, may hold values from 1 to 365
- ref_quantile: float32 [6, 256], replicated, may hold values from 0 to 1, as said below
Outputs:
- residual: float32 [8, 6, 8192], P('date', None, ('tiles', 'space')), parts along dimension 2
The draws below stay inside these ranges and needn't reach their ends.
There are 2 independent parts, one for each index of `tiles`. The reference program is written for one: setup_inputs(seed, part) draws one part's arguments, and reference() takes and returns one part's arrays. A program takes and returns all parts, laid end to end along the dimension named above; an argument that names none is the same for every part. Nothing has to cross between parts.
Inputs may be any that keep to these rules, and one draw needn't show every extreme that they name: `live_dates`: some group has all 2 slots live and some group has exactly 1. `ref_quantile`: strictly increasing along the bins.
All inputs are finite; a program needn't handle non-finite values. No bound on the sum of `clear_sky` on one device may be relied on, other than what follows from the above.
Results may differ from the reference program's by a relative error of at most 0.009.
Values sent between devices are 32-bit elements; how exact they have to be, the bound alone decides.
A program may use at most 64 MiB of HBM per device.

```python
import math
import jax
import jax.numpy as jnp
from jax import lax

BANDS = 6
BINS = 256
HARM = 7
DATE_DEV = 2
DATES = 8
PIX = 4096
COEF = 15
DGROUPS = 4


def draw_live_dates(key, part):
    first_key, second_key, third_key = jax.random.split(jax.random.fold_in(key, 11), 3)
    counts = jax.random.randint(first_key, (DGROUPS,), 1, DATE_DEV + 1)
    full_slot = jax.random.randint(second_key, (), 0, DGROUPS)
    offset = jax.random.randint(third_key, (), 1, DGROUPS)
    single_slot = (full_slot + offset) % DGROUPS
    counts = counts.at[full_slot].set(DATE_DEV)
    counts = counts.at[single_slot].set(1)
    return counts.astype(jnp.int32)


def draw_ref_quantile(key, part):
    inner_key = jax.random.fold_in(key, 23)
    steps_up = jnp.exp(jax.random.uniform(inner_key, (BANDS, BINS), jnp.float32, -1.0, 1.0))
    running = jnp.cumsum(steps_up, axis=1) - 0.5 * steps_up
    return (running / jnp.sum(steps_up, axis=1, keepdims=True)).astype(jnp.float32)


def set_ends(drawn, rng, low, largest):
    shape = drawn.shape
    spot = [jax.random.randint(jax.random.fold_in(rng, axis), (), 0, shape[axis]) for axis in range(len(shape))]
    drawn = drawn.at[tuple(spot)].set(low)
    longest = shape.index(max(shape))
    spot[longest] = (spot[longest] + 1) % shape[longest]
    return drawn.at[tuple(spot)].set(largest)


def block_levels(rng, dims, pieces, least, high):
    factor_of, own = 1.0, jax.random.fold_in(rng, 6)
    for dim, blocks in pieces:
        steps = jnp.exp(jax.random.uniform(jax.random.fold_in(own, dim), (blocks,), jnp.float32, least / len(pieces), high / len(pieces)))
        factor_of = factor_of * jnp.repeat(steps, dims[dim] // blocks).reshape([-1 if axis == dim else 1 for axis in range(len(dims))])
    return factor_of


def setup_inputs(seed: int = 0, part: int = 0) -> dict:
    key_of = jax.random.split(jax.random.key(seed), 6)
    part_splits = jax.random.split(jax.random.fold_in(key_of[5], part), 6)
    return {
        "reflect": jnp.clip(-0.05 + 1.09999995 * jax.random.uniform(part_splits[0], (DATES, BANDS, PIX), jnp.float32) ** block_levels(part_splits[0], (DATES, BANDS, PIX), ((0, 4), (2, 4)), -0.2, 0.2), -0.05, 1.05),
        "clear_sky": set_ends((jax.random.randint(part_splits[1], (DATES, PIX), 0, 3) < 2).astype(jnp.int32), jax.random.fold_in(part_splits[1], 1), 0, 1),
        "live_dates": draw_live_dates(jax.random.fold_in(key_of[5], 71), part),
        "day_of_year": set_ends(jax.random.randint(key_of[3], (DATES,), 1, 366), jax.random.fold_in(key_of[3], 1), 1, 365).astype(jnp.int32),
        "ref_quantile": draw_ref_quantile(jax.random.fold_in(key_of[5], 71), part),
    }


ridge_weight = 1.0
year_days = 365.0

def tent_weights(position, bin_count):
    centers = jnp.arange(bin_count, dtype=jnp.float32)
    return jnp.maximum(0.0, 1.0 - jnp.abs(position[..., None] - centers)).astype(jnp.bfloat16)

def harmonic_basis(day_of_year, harmonics):
    angles = 2.0 * math.pi * day_of_year.astype(jnp.float32) / year_days
    orders = jnp.arange(1, harmonics + 1, dtype=jnp.float32)
    phases = angles[:, None] * orders[None, :]
    ones_col = jnp.ones((day_of_year.shape[0], 1), jnp.float32)
    return jnp.concatenate([ones_col, jnp.cos(phases), jnp.sin(phases)], axis=1)

def reference(reflect, clear_sky, live_dates, day_of_year, ref_quantile):
    slot_index = jnp.arange(DATES, dtype=jnp.int32)
    counts_each = jnp.repeat(live_dates, DATE_DEV)
    live_flag = (slot_index % DATE_DEV < counts_each).astype(jnp.float32)
    valid_mask = clear_sky * (slot_index % DATE_DEV < counts_each).astype(jnp.int32)[:, None]
    valid_float = valid_mask.astype(jnp.float32)
    quant_half = ref_quantile.astype(jnp.bfloat16)

    def match_date(inputs):
        values_row, mask_row = inputs
        position = jnp.clip(BINS * values_row - 0.5, 0.0, BINS - 1.0)
        weights = tent_weights(position, BINS)
        histogram = jnp.einsum('bpk,p->bk', weights.astype(jnp.float32), mask_row.astype(jnp.float32))
        grand_total = jnp.maximum(jnp.sum(histogram, axis=-1), 1.0)
        cumulative = ((jnp.cumsum(histogram, axis=-1) - 0.5 * histogram) / grand_total[:, None]).astype(jnp.bfloat16)
        level_pos = jnp.einsum('bpk,bk->bp', weights.astype(jnp.float32), cumulative.astype(jnp.float32))
        level_pos = jnp.clip(BINS * level_pos - 0.5, 0.0, BINS - 1.0)
        second = tent_weights(level_pos, BINS)
        return jnp.einsum('bpk,bk->bp', second.astype(jnp.float32), quant_half.astype(jnp.float32))
    matched = lax.map(match_date, (reflect, valid_float))
    design = harmonic_basis(day_of_year, HARM)
    weighted_design = design * live_flag[:, None]
    normal = jnp.dot(weighted_design.T, design, precision=lax.Precision.HIGHEST) + ridge_weight * jnp.eye(COEF, dtype=jnp.float32)
    projector = jnp.linalg.solve(normal, weighted_design.T)
    valid_count = jnp.sum(valid_float, axis=0)
    fill_mean = jnp.sum(valid_float[:, None, :] * matched, axis=0) / jnp.maximum(valid_count, 1.0)[None, :]
    filled = valid_float[:, None, :] * matched + (1.0 - valid_float[:, None, :]) * fill_mean[None]
    coefficients = jnp.einsum('ct,tbp->cbp', projector, filled, precision=lax.Precision.HIGHEST)
    fitted = jnp.einsum('tc,cbp->tbp', design, coefficients, precision=lax.Precision.HIGHEST)
    return valid_float[:, None, :] * (matched - fitted)
```

```python
import functools
import math

import jax
import jax.numpy as jnp
from jax import lax
from jax.experimental import pallas as pl
from jax.experimental.pallas import tpu as pltpu
from jax.sharding import PartitionSpec as P

MESH = pl.DeviceIdType.MESH
HARMONICS = 7
RIDGE = 1.0
YEAR = 365
LOW = 16
LANES = 128
SUBLANES = 8


def iota(shape, dim):
    return lax.broadcasted_iota(jnp.int32, shape, dim)


def rounded(x):
    return x.astype(jnp.bfloat16).astype(jnp.float32)


def block_histogram(values, valid, bands, bins):
    high_count = bins // LOW
    pixels = values.shape[1]
    position = jnp.clip(bins * values - 0.5, 0.0, bins - 1.0)
    high = jnp.floor(position * (1.0 / LOW))
    local = position - LOW * high
    marked = jnp.where(valid, high, -1.0)
    high_iota = iota((high_count, pixels), 0).astype(jnp.float32)
    low_iota = iota((LOW, pixels), 0).astype(jnp.float32)
    hot, tents = [], []
    for b in range(bands):
        hot.append(jnp.where(high_iota == marked[b : b + 1], 1.0, 0.0).astype(jnp.bfloat16))
        tents.append(
            jnp.maximum(0.0, 1.0 - jnp.abs(local[b : b + 1] - low_iota)).astype(jnp.bfloat16)
        )
    spill = jnp.maximum(0.0, 1.0 - jnp.abs(local - LOW))
    tents.append(jnp.concatenate([spill, jnp.zeros_like(spill)], axis=0).astype(jnp.bfloat16))
    hot.append(jnp.zeros((LANES - bands * high_count, pixels), jnp.bfloat16))
    counts = lax.dot_general(
        jnp.concatenate(tents, axis=0),
        jnp.concatenate(hot, axis=0),
        (((1,), (1,)), ((), ())),
        preferred_element_type=jnp.float32,
    )
    band_lane = iota((LOW, LANES), 1) // high_count
    inner = jnp.zeros((LOW, LANES), jnp.float32)
    for b in range(bands):
        inner += jnp.where(band_lane == b, counts[b * LOW : (b + 1) * LOW], 0.0)
    outer = counts[bands * LOW : bands * LOW + SUBLANES]
    own = iota((SUBLANES, LANES), 0) == band_lane[:SUBLANES]
    return inner, jnp.sum(jnp.where(own, outer, 0.0), axis=0, keepdims=True)


def running_sums(inner, spill, bands, bins):
    high_count = bins // LOW
    dates = len(inner)
    used = bands * high_count
    column = [jnp.sum(inner[d], axis=0, keepdims=True) + spill[d] for d in range(dates)]
    rows = column + spill
    left = jnp.zeros((SUBLANES, LANES), jnp.float32)
    row_of = iota((SUBLANES, LANES), 0)
    for i, row in enumerate(rows):
        left = jnp.where(row_of == i, row, left)
    src, dst = iota((LANES, LANES), 0), iota((LANES, LANES), 1)
    same = (src // high_count == dst // high_count) & (dst < used)
    before = jnp.where((same & (src < dst)) | (dst == used + src // high_count), 1.0, 0.0)
    shift = jnp.where(same & (src + 1 == dst), 0.5, 0.0)
    before = jnp.where(src < used, before, 0.0)
    shift = jnp.where(src < used, shift, 0.0)
    moved = jnp.dot(
        left,
        jnp.concatenate([before, shift], axis=1),
        precision=lax.Precision.HIGHEST,
        preferred_element_type=jnp.float32,
    )
    out_row, in_row = iota((LOW, LOW), 0), iota((LOW, LOW), 1)
    lower = jnp.where(in_row < out_row, 1.0, jnp.where(in_row == out_row, 0.5, 0.0))
    within = jnp.dot(
        lower,
        jnp.concatenate(inner, axis=1),
        precision=lax.Precision.HIGHEST,
        preferred_element_type=jnp.float32,
    )
    first = iota((LOW, LANES), 0) == 0
    sums = []
    for d in range(dates):
        part = within[:, d * LANES : (d + 1) * LANES] + moved[d : d + 1, :LANES]
        back = moved[dates + d : dates + d + 1, LANES:]
        sums.append(part - jnp.where(first, back, 0.0))
    return sums


def flat_table(sums, bands, bins):
    high_count = bins // LOW
    used = bands * high_count
    lane = iota((SUBLANES, LANES), 1)
    total_lane = jnp.minimum(used + lane // high_count, LANES - 1)
    total = jnp.take_along_axis(sums[:SUBLANES], total_lane, axis=1)[:1]
    cumulative = (sums / jnp.maximum(total, 1.0)).astype(jnp.bfloat16).astype(jnp.float32)
    band_lane = iota((LOW, LANES), 1) // high_count
    wide = jnp.concatenate(
        [jnp.where(band_lane == b, cumulative, 0.0) for b in range(bands)], axis=0
    ).astype(jnp.bfloat16)
    src, dst = iota((LANES, bins), 0), iota((LANES, bins), 1)
    spread = jnp.where((src % high_count == dst // LOW) & (src < used), 1.0, 0.0).astype(
        jnp.bfloat16
    )
    placed = jnp.dot(wide, spread, preferred_element_type=jnp.float32)
    rows, cols = iota(placed.shape, 0), iota(placed.shape, 1)
    placed = jnp.where(rows % LOW == cols % LOW, placed, 0.0).astype(jnp.bfloat16)
    pick = jnp.where(
        iota((SUBLANES, bands * LOW), 1) // LOW == iota((SUBLANES, bands * LOW), 0), 1.0, 0.0
    ).astype(jnp.bfloat16)
    return jnp.dot(pick, placed, preferred_element_type=jnp.float32)


def gather_lanes(table, index):
    parts = table.shape[1] // LANES
    inner = index % LANES
    out = jnp.take_along_axis(table[:, :LANES], inner, axis=1)
    for part in range(1, parts):
        other = jnp.take_along_axis(table[:, part * LANES : (part + 1) * LANES], inner, axis=1)
        out = jnp.where(index >= part * LANES, other, out)
    return out


def interpolate(table, position, bins):
    low = jnp.floor(position)
    first = low.astype(jnp.int32)
    second = jnp.minimum(first + 1, bins - 1)
    low_weight = rounded(1.0 - jnp.abs(position - low))
    high_weight = rounded(jnp.maximum(0.0, 1.0 - jnp.abs(position - (low + 1.0))))
    return low_weight * gather_lanes(table, first) + high_weight * gather_lanes(table, second)


def own_fit_rows(live_ref, day_ref, date_slots, dates, first_date):
    size = max(dates, SUBLANES)
    rows, cols = iota((size, size), 0), iota((size, size), 1)

    def place(t, carry):
        day_r, day_c, live_r, live_c = carry
        day = day_ref[t]
        live = (lax.rem(t, date_slots) < live_ref[lax.div(t, date_slots)]).astype(jnp.int32)
        return (
            jnp.where(rows == t, day, day_r),
            jnp.where(cols == t, day, day_c),
            jnp.where(rows == t, live, live_r),
            jnp.where(cols == t, live, live_c),
        )

    zero = jnp.zeros((size, size), jnp.int32)
    day_r, day_c, live_r, live_c = lax.fori_loop(
        0, dates, place, (zero, zero, zero, zero), unroll=dates <= 16
    )
    base = jnp.cos((2.0 * math.pi / YEAR) * (day_r - day_c).astype(jnp.float32))
    older, newer = jnp.ones_like(base), base
    total = older + newer
    for _ in range(HARMONICS - 1):
        older, newer = newer, 2.0 * base * newer - older
        total = total + newer
    eye = jnp.where(rows == cols, 1.0, 0.0)
    work = jnp.where((live_r * live_c) == 1, total, 0.0) + RIDGE * eye
    inverse = eye
    for k in range(dates):
        pivot = work[k : k + 1, k : k + 1]
        row_w, row_i = work[k : k + 1, :] / pivot, inverse[k : k + 1, :] / pivot
        column = work[:, k : k + 1]
        work = jnp.where(rows == k, row_w, work - column * row_w)
        inverse = jnp.where(rows == k, row_i, inverse - column * row_i)
    return [
        jnp.sum(jnp.where(rows == first_date + d, inverse, 0.0), axis=0, keepdims=True)
        for d in range(date_slots)
    ]


def kernel(
    groups,
    spaces,
    live_ref,
    day_ref,
    reflect_ref,
    clear_ref,
    quantile_ref,
    out_ref,
    padded,
    quant,
    hist_own,
    hist_all,
    mask_all,
    series_all,
    hist_send,
    hist_recv,
    mask_send,
    mask_recv,
    series_send,
    series_recv,
):
    date_slots, bands, pixels = reflect_ref.shape
    bins = quantile_ref.shape[1]
    dates = date_slots * groups
    my_date, my_space = lax.axis_index("date"), lax.axis_index("space")
    date_peers = [lax.rem(my_date + i, groups) for i in range(1, groups)]
    space_peers = [lax.rem(my_space + i, spaces) for i in range(1, spaces)]

    barrier = pltpu.get_barrier_semaphore()
    for peer in space_peers:
        pl.semaphore_signal(barrier, inc=1, device_id={"space": peer}, device_id_type=MESH)
    for peer in date_peers:
        pl.semaphore_signal(barrier, inc=1, device_id={"date": peer}, device_id_type=MESH)

    padded[...] = jnp.zeros_like(padded)
    padded[:, :bands] = reflect_ref[...]
    quant[...] = jnp.zeros_like(quant)
    quant[:bands] = rounded(quantile_ref[...])

    inner, spill = [], []
    for d in range(date_slots):
        live = lax.rem(jnp.int32(d), date_slots) < live_ref[my_date]
        valid = clear_ref[d : d + 1, :] * live.astype(jnp.int32)
        mask_all[my_date, d : d + 1, :] = valid.astype(jnp.float32)
        block, extra = block_histogram(
            padded[d], jnp.broadcast_to(valid, (SUBLANES, pixels)) == 1, bands, bins
        )
        inner.append(block)
        spill.append(extra)
    sums = running_sums(inner, spill, bands, bins)
    for d in range(date_slots):
        hist_own[d] = sums[d]

    pl.semaphore_wait(barrier, groups + spaces - 2)

    copies = []
    for peer in space_peers:
        copy = pltpu.make_async_remote_copy(
            src_ref=hist_own,
            dst_ref=hist_all.at[my_space],
            send_sem=hist_send.at[peer],
            recv_sem=hist_recv.at[my_space],
            device_id={"space": peer},
            device_id_type=MESH,
        )
        copy.start()
        copies.append(copy)
    for peer in date_peers:
        copy = pltpu.make_async_remote_copy(
            src_ref=mask_all.at[my_date],
            dst_ref=mask_all.at[my_date],
            send_sem=mask_send.at[peer],
            recv_sem=mask_recv.at[my_date],
            device_id={"date": peer},
            device_id_type=MESH,
        )
        copy.start()
        copies.append(copy)

    fit_rows = own_fit_rows(live_ref, day_ref, date_slots, dates, my_date * date_slots)

    total = [hist_own[d] for d in range(date_slots)]
    for peer in space_peers:
        pltpu.make_async_remote_copy(
            src_ref=hist_own,
            dst_ref=hist_all.at[peer],
            send_sem=hist_send.at[peer],
            recv_sem=hist_recv.at[peer],
            device_id={"space": peer},
            device_id_type=MESH,
        ).wait_recv()
        for d in range(date_slots):
            total[d] = total[d] + hist_all[peer, d]

    for d in range(date_slots):
        table = flat_table(total[d], bands, bins)
        for start in range(0, pixels, LANES):
            span = slice(start, start + LANES)
            position = jnp.clip(bins * padded[d, :, span] - 0.5, 0.0, bins - 1.0)
            level = interpolate(table, position, bins)
            level = jnp.clip(bins * level - 0.5, 0.0, bins - 1.0)
            matched = interpolate(quant[...], level, bins)
            series_all[my_date, d, :, span] = matched[:bands] * mask_all[my_date, d : d + 1, span]
        for peer in date_peers:
            copy = pltpu.make_async_remote_copy(
                src_ref=series_all.at[my_date, d],
                dst_ref=series_all.at[my_date, d],
                send_sem=series_send.at[peer, d],
                recv_sem=series_recv.at[my_date, d],
                device_id={"date": peer},
                device_id_type=MESH,
            )
            copy.start()
            copies.append(copy)

    for peer in date_peers:
        pltpu.make_async_remote_copy(
            src_ref=mask_all.at[peer],
            dst_ref=mask_all.at[peer],
            send_sem=mask_send.at[peer],
            recv_sem=mask_recv.at[peer],
            device_id={"date": peer},
            device_id_type=MESH,
        ).wait_recv()
    for d in range(date_slots):
        for peer in date_peers:
            pltpu.make_async_remote_copy(
                src_ref=series_all.at[peer, d],
                dst_ref=series_all.at[peer, d],
                send_sem=series_send.at[peer, d],
                recv_sem=series_recv.at[peer, d],
                device_id={"date": peer},
                device_id_type=MESH,
            ).wait_recv()

    count = jnp.zeros((1, pixels), jnp.float32)
    summed = jnp.zeros((bands, pixels), jnp.float32)
    gaps = [jnp.zeros((1, pixels), jnp.float32) for _ in range(date_slots)]
    fits = [jnp.zeros((bands, pixels), jnp.float32) for _ in range(date_slots)]
    for t in range(dates):
        g, s = divmod(t, date_slots)
        mask, series = mask_all[g, s : s + 1, :], series_all[g, s]
        count += mask
        summed += series
        for d in range(date_slots):
            weight = fit_rows[d][:, t : t + 1]
            gaps[d] += weight * (1.0 - mask)
            fits[d] += weight * series
    mean = summed / jnp.maximum(count, 1.0)
    for d in range(date_slots):
        out_ref[d] = mask_all[my_date, d : d + 1, :] * (fits[d] + gaps[d] * mean)

    for copy in copies:
        copy.wait_send()


def per_device(groups, spaces, reflect, clear_sky, live_dates, day_of_year, ref_quantile):
    date_slots, bands, pixels = reflect.shape
    bins = ref_quantile.shape[1]
    vmem, smem = pl.BlockSpec(memory_space=pltpu.VMEM), pl.BlockSpec(memory_space=pltpu.SMEM)
    return pl.pallas_call(
        functools.partial(kernel, groups, spaces),
        out_shape=jax.ShapeDtypeStruct(reflect.shape, jnp.float32),
        in_specs=[smem, smem, vmem, vmem, vmem],
        out_specs=vmem,
        scratch_shapes=[
            pltpu.VMEM((date_slots, SUBLANES, pixels), jnp.float32),
            pltpu.VMEM((SUBLANES, bins), jnp.float32),
            pltpu.VMEM((date_slots, LOW, LANES), jnp.float32),
            pltpu.VMEM((spaces, date_slots, LOW, LANES), jnp.float32),
            pltpu.VMEM((groups, date_slots, pixels), jnp.float32),
            pltpu.VMEM((groups, date_slots, bands, pixels), jnp.float32),
            pltpu.SemaphoreType.DMA((spaces,)),
            pltpu.SemaphoreType.DMA((spaces,)),
            pltpu.SemaphoreType.DMA((groups,)),
            pltpu.SemaphoreType.DMA((groups,)),
            pltpu.SemaphoreType.DMA((groups, date_slots)),
            pltpu.SemaphoreType.DMA((groups, date_slots)),
        ],
        compiler_params=pltpu.CompilerParams(collective_id=0, has_side_effects=True),
    )(live_dates, day_of_year, reflect, clear_sky, ref_quantile)


def solution(mesh):
    return jax.shard_map(
        functools.partial(per_device, mesh.shape["date"], mesh.shape["space"]),
        mesh=mesh,
        in_specs=(
            P("date", None, ("tiles", "space")),
            P("date", ("tiles", "space")),
            P(),
            P(),
            P(),
        ),
        out_specs=P("date", None, ("tiles", "space")),
        check_vma=False,
    )
```

```python
import functools
import math

import jax
import jax.numpy as jnp
from jax import lax
from jax.experimental import pallas as pl
from jax.experimental.pallas import tpu as pltpu
from jax.sharding import PartitionSpec as P

MESH = pl.DeviceIdType.MESH
HARMONICS = 7
RIDGE = 1.0
YEAR = 365
LOW = 16
LANES = 128
SUBLANES = 8


def iota(shape, dim):
    return lax.broadcasted_iota(jnp.int32, shape, dim)


def rounded(x):
    return x.astype(jnp.bfloat16).astype(jnp.float32)


def block_histogram(values, valid, bands, bins):
    high_count = bins // LOW
    pixels = values.shape[1]
    position = jnp.clip(bins * values - 0.5, 0.0, bins - 1.0)
    high = jnp.floor(position * (1.0 / LOW))
    local = position - LOW * high
    marked = jnp.where(valid, high, -1.0)
    high_iota = iota((high_count, pixels), 0).astype(jnp.float32)
    low_iota = iota((LOW, pixels), 0).astype(jnp.float32)
    hot, tents = [], []
    for b in range(bands):
        hot.append(jnp.where(high_iota == marked[b : b + 1], 1.0, 0.0).astype(jnp.bfloat16))
        tents.append(
            jnp.maximum(0.0, 1.0 - jnp.abs(local[b : b + 1] - low_iota)).astype(jnp.bfloat16)
        )
    spill = jnp.maximum(0.0, 1.0 - jnp.abs(local - LOW))
    tents.append(jnp.concatenate([spill, jnp.zeros_like(spill)], axis=0).astype(jnp.bfloat16))
    hot.append(jnp.zeros((LANES - bands * high_count, pixels), jnp.bfloat16))
    counts = lax.dot_general(
        jnp.concatenate(tents, axis=0),
        jnp.concatenate(hot, axis=0),
        (((1,), (1,)), ((), ())),
        preferred_element_type=jnp.float32,
    )
    band_lane = iota((LOW, LANES), 1) // high_count
    inner = jnp.zeros((LOW, LANES), jnp.float32)
    for b in range(bands):
        inner += jnp.where(band_lane == b, counts[b * LOW : (b + 1) * LOW], 0.0)
    outer = counts[bands * LOW : bands * LOW + SUBLANES]
    own = iota((SUBLANES, LANES), 0) == band_lane[:SUBLANES]
    return inner, jnp.sum(jnp.where(own, outer, 0.0), axis=0, keepdims=True)


def running_sums(inner, spill, bands, bins):
    high_count = bins // LOW
    dates = len(inner)
    used = bands * high_count
    column = [jnp.sum(inner[d], axis=0, keepdims=True) + spill[d] for d in range(dates)]
    rows = column + spill
    left = jnp.zeros((SUBLANES, LANES), jnp.float32)
    row_of = iota((SUBLANES, LANES), 0)
    for i, row in enumerate(rows):
        left = jnp.where(row_of == i, row, left)
    src, dst = iota((LANES, LANES), 0), iota((LANES, LANES), 1)
    same = (src // high_count == dst // high_count) & (dst < used)
    before = jnp.where((same & (src < dst)) | (dst == used + src // high_count), 1.0, 0.0)
    shift = jnp.where(same & (src + 1 == dst), 0.5, 0.0)
    before = jnp.where(src < used, before, 0.0)
    shift = jnp.where(src < used, shift, 0.0)
    moved = jnp.dot(
        left,
        jnp.concatenate([before, shift], axis=1),
        precision=lax.Precision.HIGHEST,
        preferred_element_type=jnp.float32,
    )
    out_row, in_row = iota((LOW, LOW), 0), iota((LOW, LOW), 1)
    lower = jnp.where(in_row < out_row, 1.0, jnp.where(in_row == out_row, 0.5, 0.0))
    within = jnp.dot(
        lower,
        jnp.concatenate(inner, axis=1),
        precision=lax.Precision.HIGHEST,
        preferred_element_type=jnp.float32,
    )
    first = iota((LOW, LANES), 0) == 0
    sums = []
    for d in range(dates):
        part = within[:, d * LANES : (d + 1) * LANES] + moved[d : d + 1, :LANES]
        back = moved[dates + d : dates + d + 1, LANES:]
        sums.append(part - jnp.where(first, back, 0.0))
    return sums


def flat_table(sums, bands, bins):
    high_count = bins // LOW
    used = bands * high_count
    lane = iota((SUBLANES, LANES), 1)
    total_lane = jnp.minimum(used + lane // high_count, LANES - 1)
    total = jnp.take_along_axis(sums[:SUBLANES], total_lane, axis=1)[:1]
    cumulative = (sums / jnp.maximum(total, 1.0)).astype(jnp.bfloat16).astype(jnp.float32)
    band_lane = iota((LOW, LANES), 1) // high_count
    wide = jnp.concatenate(
        [jnp.where(band_lane == b, cumulative, 0.0) for b in range(bands)], axis=0
    ).astype(jnp.bfloat16)
    src, dst = iota((LANES, bins), 0), iota((LANES, bins), 1)
    spread = jnp.where((src % high_count == dst // LOW) & (src < used), 1.0, 0.0).astype(
        jnp.bfloat16
    )
    placed = jnp.dot(wide, spread, preferred_element_type=jnp.float32)
    rows, cols = iota(placed.shape, 0), iota(placed.shape, 1)
    placed = jnp.where(rows % LOW == cols % LOW, placed, 0.0).astype(jnp.bfloat16)
    pick = jnp.where(
        iota((SUBLANES, bands * LOW), 1) // LOW == iota((SUBLANES, bands * LOW), 0), 1.0, 0.0
    ).astype(jnp.bfloat16)
    return jnp.dot(pick, placed, preferred_element_type=jnp.float32)


def gather_lanes(table, index):
    parts = table.shape[1] // LANES
    inner = index % LANES
    out = jnp.take_along_axis(table[:, :LANES], inner, axis=1)
    for part in range(1, parts):
        other = jnp.take_along_axis(table[:, part * LANES : (part + 1) * LANES], inner, axis=1)
        out = jnp.where(index >= part * LANES, other, out)
    return out


def interpolate(table, position, bins):
    low = jnp.floor(position)
    first = low.astype(jnp.int32)
    second = jnp.minimum(first + 1, bins - 1)
    low_weight = rounded(1.0 - jnp.abs(position - low))
    high_weight = rounded(jnp.maximum(0.0, 1.0 - jnp.abs(position - (low + 1.0))))
    return low_weight * gather_lanes(table, first) + high_weight * gather_lanes(table, second)


def own_fit_rows(live_ref, day_ref, date_slots, dates, first_date):
    size = max(dates, SUBLANES)
    rows, cols = iota((size, size), 0), iota((size, size), 1)

    def place(t, carry):
        day_r, day_c, live_r, live_c = carry
        day = day_ref[t]
        live = (lax.rem(t, date_slots) < live_ref[lax.div(t, date_slots)]).astype(jnp.int32)
        return (
            jnp.where(rows == t, day, day_r),
            jnp.where(cols == t, day, day_c),
            jnp.where(rows == t, live, live_r),
            jnp.where(cols == t, live, live_c),
        )

    zero = jnp.zeros((size, size), jnp.int32)
    day_r, day_c, live_r, live_c = lax.fori_loop(
        0, dates, place, (zero, zero, zero, zero), unroll=dates <= 16
    )
    base = jnp.cos((2.0 * math.pi / YEAR) * (day_r - day_c).astype(jnp.float32))
    older, newer = jnp.ones_like(base), base
    total = older + newer
    for _ in range(HARMONICS - 1):
        older, newer = newer, 2.0 * base * newer - older
        total = total + newer
    eye = jnp.where(rows == cols, 1.0, 0.0)
    work = jnp.where((live_r * live_c) == 1, total, 0.0) + RIDGE * eye
    inverse = eye
    for k in range(dates):
        pivot = work[k : k + 1, k : k + 1]
        row_w, row_i = work[k : k + 1, :] / pivot, inverse[k : k + 1, :] / pivot
        column = work[:, k : k + 1]
        work = jnp.where(rows == k, row_w, work - column * row_w)
        inverse = jnp.where(rows == k, row_i, inverse - column * row_i)
    return [
        jnp.sum(jnp.where(rows == first_date + d, inverse, 0.0), axis=0, keepdims=True)
        for d in range(date_slots)
    ]


def kernel(
    groups,
    spaces,
    live_hbm,
    day_hbm,
    reflect_hbm,
    clear_hbm,
    quantile_hbm,
    out_ref,
    live_ref,
    day_ref,
    reflect_ref,
    clear_ref,
    quantile_ref,
    in_sems,
    padded,
    quant,
    hist_own,
    hist_all,
    mask_all,
    series_all,
    hist_send,
    hist_recv,
    mask_send,
    mask_recv,
    series_send,
    series_recv,
):
    bands, date_slots, pixels = reflect_ref.shape
    bins = quantile_ref.shape[1]
    dates = date_slots * groups
    my_date, my_space = lax.axis_index("date"), lax.axis_index("space")
    date_peers = [lax.rem(my_date + i, groups) for i in range(1, groups)]
    space_peers = [lax.rem(my_space + i, spaces) for i in range(1, spaces)]

    barrier = pltpu.get_barrier_semaphore()
    for peer in space_peers:
        pl.semaphore_signal(barrier, inc=1, device_id={"space": peer}, device_id_type=MESH)
    for peer in date_peers:
        pl.semaphore_signal(barrier, inc=1, device_id={"date": peer}, device_id_type=MESH)

    loads = [
        pltpu.make_async_copy(src, dst, in_sems.at[i])
        for i, (src, dst) in enumerate(
            (
                (reflect_hbm, reflect_ref),
                (clear_hbm, clear_ref),
                (live_hbm, live_ref),
                (day_hbm, day_ref),
                (quantile_hbm, quantile_ref),
            )
        )
    ]
    for load in loads:
        load.start()
    padded[...] = jnp.zeros_like(padded)
    quant[...] = jnp.zeros_like(quant)
    for load in loads:
        load.wait()
    for b in range(bands):
        for d in range(date_slots):
            padded[d, b : b + 1, :] = reflect_ref[b, d : d + 1, :]
    quant[:bands] = rounded(quantile_ref[...])

    inner, spill = [], []
    for d in range(date_slots):
        live = lax.rem(jnp.int32(d), date_slots) < live_ref[my_date]
        valid = clear_ref[d : d + 1, :] * live.astype(jnp.int32)
        mask_all[my_date, d : d + 1, :] = valid.astype(jnp.float32)
        block, extra = block_histogram(
            padded[d], jnp.broadcast_to(valid, (SUBLANES, pixels)) == 1, bands, bins
        )
        inner.append(block)
        spill.append(extra)
    sums = running_sums(inner, spill, bands, bins)
    for d in range(date_slots):
        hist_own[d] = sums[d]

    pl.semaphore_wait(barrier, groups + spaces - 2)

    copies = []
    for peer in space_peers:
        copy = pltpu.make_async_remote_copy(
            src_ref=hist_own,
            dst_ref=hist_all.at[my_space],
            send_sem=hist_send.at[peer],
            recv_sem=hist_recv.at[my_space],
            device_id={"space": peer},
            device_id_type=MESH,
        )
        copy.start()
        copies.append(copy)
    for peer in date_peers:
        copy = pltpu.make_async_remote_copy(
            src_ref=mask_all.at[my_date],
            dst_ref=mask_all.at[my_date],
            send_sem=mask_send.at[peer],
            recv_sem=mask_recv.at[my_date],
            device_id={"date": peer},
            device_id_type=MESH,
        )
        copy.start()
        copies.append(copy)

    total = [hist_own[d] for d in range(date_slots)]
    for peer in space_peers:
        pltpu.make_async_remote_copy(
            src_ref=hist_own,
            dst_ref=hist_all.at[peer],
            send_sem=hist_send.at[peer],
            recv_sem=hist_recv.at[peer],
            device_id={"space": peer},
            device_id_type=MESH,
        ).wait_recv()
        for d in range(date_slots):
            total[d] = total[d] + hist_all[peer, d]

    for d in range(date_slots):
        table = flat_table(total[d], bands, bins)
        for start in range(0, pixels, LANES):
            span = slice(start, start + LANES)
            position = jnp.clip(bins * padded[d, :, span] - 0.5, 0.0, bins - 1.0)
            level = interpolate(table, position, bins)
            level = jnp.clip(bins * level - 0.5, 0.0, bins - 1.0)
            matched = interpolate(quant[...], level, bins)
            series_all[my_date, d, :, span] = matched[:bands] * mask_all[my_date, d : d + 1, span]
        for peer in date_peers:
            copy = pltpu.make_async_remote_copy(
                src_ref=series_all.at[my_date, d],
                dst_ref=series_all.at[my_date, d],
                send_sem=series_send.at[peer, d],
                recv_sem=series_recv.at[my_date, d],
                device_id={"date": peer},
                device_id_type=MESH,
            )
            copy.start()
            copies.append(copy)

    fit_rows = own_fit_rows(live_ref, day_ref, date_slots, dates, my_date * date_slots)

    for peer in date_peers:
        pltpu.make_async_remote_copy(
            src_ref=mask_all.at[peer],
            dst_ref=mask_all.at[peer],
            send_sem=mask_send.at[peer],
            recv_sem=mask_recv.at[peer],
            device_id={"date": peer},
            device_id_type=MESH,
        ).wait_recv()
    for d in range(date_slots):
        for peer in date_peers:
            pltpu.make_async_remote_copy(
                src_ref=series_all.at[peer, d],
                dst_ref=series_all.at[peer, d],
                send_sem=series_send.at[peer, d],
                recv_sem=series_recv.at[peer, d],
                device_id={"date": peer},
                device_id_type=MESH,
            ).wait_recv()

    count = jnp.zeros((1, pixels), jnp.float32)
    summed = jnp.zeros((bands, pixels), jnp.float32)
    gaps = [jnp.zeros((1, pixels), jnp.float32) for _ in range(date_slots)]
    fits = [jnp.zeros((bands, pixels), jnp.float32) for _ in range(date_slots)]
    for t in range(dates):
        g, s = divmod(t, date_slots)
        mask, series = mask_all[g, s : s + 1, :], series_all[g, s]
        count += mask
        summed += series
        for d in range(date_slots):
            weight = fit_rows[d][:, t : t + 1]
            gaps[d] += weight * (1.0 - mask)
            fits[d] += weight * series
    mean = summed / jnp.maximum(count, 1.0)
    for d in range(date_slots):
        left = mask_all[my_date, d : d + 1, :] * (fits[d] + gaps[d] * mean)
        for b in range(bands):
            out_ref[b, d : d + 1, :] = left[b : b + 1]

    for copy in copies:
        copy.wait_send()


def per_device(groups, spaces, reflect, clear_sky, live_dates, day_of_year, ref_quantile):
    date_slots, bands, pixels = reflect.shape
    bins = ref_quantile.shape[1]
    by_band = jnp.transpose(reflect, (1, 0, 2))
    residual = pl.pallas_call(
        functools.partial(kernel, groups, spaces),
        out_shape=jax.ShapeDtypeStruct(by_band.shape, jnp.float32),
        in_specs=[pl.BlockSpec(memory_space=pl.ANY)] * 5,
        out_specs=pl.BlockSpec(memory_space=pltpu.VMEM),
        scratch_shapes=[
            pltpu.SMEM(live_dates.shape, jnp.int32),
            pltpu.SMEM(day_of_year.shape, jnp.int32),
            pltpu.VMEM(by_band.shape, jnp.float32),
            pltpu.VMEM(clear_sky.shape, jnp.int32),
            pltpu.VMEM(ref_quantile.shape, jnp.float32),
            pltpu.SemaphoreType.DMA((5,)),
            pltpu.VMEM((date_slots, SUBLANES, pixels), jnp.float32),
            pltpu.VMEM((SUBLANES, bins), jnp.float32),
            pltpu.VMEM((date_slots, LOW, LANES), jnp.float32),
            pltpu.VMEM((spaces, date_slots, LOW, LANES), jnp.float32),
            pltpu.VMEM((groups, date_slots, pixels), jnp.float32),
            pltpu.VMEM((groups, date_slots, bands, pixels), jnp.float32),
            pltpu.SemaphoreType.DMA((spaces,)),
            pltpu.SemaphoreType.DMA((spaces,)),
            pltpu.SemaphoreType.DMA((groups,)),
            pltpu.SemaphoreType.DMA((groups,)),
            pltpu.SemaphoreType.DMA((groups, date_slots)),
            pltpu.SemaphoreType.DMA((groups, date_slots)),
        ],
        compiler_params=pltpu.CompilerParams(collective_id=0, has_side_effects=True),
    )(live_dates, day_of_year, by_band, clear_sky, ref_quantile)
    return jnp.transpose(residual, (1, 0, 2))


def solution(mesh):
    return jax.shard_map(
        functools.partial(per_device, mesh.shape["date"], mesh.shape["space"]),
        mesh=mesh,
        in_specs=(
            P("date", None, ("tiles", "space")),
            P("date", ("tiles", "space")),
            P(),
            P(),
            P(),
        ),
        out_specs=P("date", None, ("tiles", "space")),
        check_vma=False,
    )
```

```python
import functools
import math

import jax
import jax.numpy as jnp
from jax import lax
from jax.experimental import pallas as pl
from jax.experimental.pallas import tpu as pltpu
from jax.sharding import PartitionSpec as P

MESH = pl.DeviceIdType.MESH
HARMONICS = 7
RIDGE = 1.0
YEAR = 365
LOW = 16
LANES = 128
SUBLANES = 8


def iota(shape, dim):
    return lax.broadcasted_iota(jnp.int32, shape, dim)


def rounded(x):
    return x.astype(jnp.bfloat16).astype(jnp.float32)


def block_histogram(values, valid, bands, bins):
    high_count = bins // LOW
    pixels = values.shape[1]
    position = jnp.clip(bins * values - 0.5, 0.0, bins - 1.0)
    high = jnp.floor(position * (1.0 / LOW))
    local = position - LOW * high
    marked = jnp.where(valid, high, -1.0)
    high_iota = iota((high_count, pixels), 0).astype(jnp.float32)
    low_iota = iota((LOW, pixels), 0).astype(jnp.float32)
    hot, tents = [], []
    for b in range(bands):
        hot.append(jnp.where(high_iota == marked[b : b + 1], 1.0, 0.0).astype(jnp.bfloat16))
        tents.append(
            jnp.maximum(0.0, 1.0 - jnp.abs(local[b : b + 1] - low_iota)).astype(jnp.bfloat16)
        )
    spill = jnp.maximum(0.0, 1.0 - jnp.abs(local - LOW))
    tents.append(jnp.concatenate([spill, jnp.zeros_like(spill)], axis=0).astype(jnp.bfloat16))
    hot.append(jnp.zeros((LANES - bands * high_count, pixels), jnp.bfloat16))
    counts = lax.dot_general(
        jnp.concatenate(tents, axis=0),
        jnp.concatenate(hot, axis=0),
        (((1,), (1,)), ((), ())),
        preferred_element_type=jnp.float32,
    )
    band_lane = iota((LOW, LANES), 1) // high_count
    inner = jnp.zeros((LOW, LANES), jnp.float32)
    for b in range(bands):
        inner += jnp.where(band_lane == b, counts[b * LOW : (b + 1) * LOW], 0.0)
    outer = counts[bands * LOW : bands * LOW + SUBLANES]
    own = iota((SUBLANES, LANES), 0) == band_lane[:SUBLANES]
    return inner, jnp.sum(jnp.where(own, outer, 0.0), axis=0, keepdims=True)


def running_sums(inner, spill, bands, bins):
    high_count = bins // LOW
    dates = len(inner)
    used = bands * high_count
    column = [jnp.sum(inner[d], axis=0, keepdims=True) + spill[d] for d in range(dates)]
    rows = column + spill
    left = jnp.zeros((SUBLANES, LANES), jnp.float32)
    row_of = iota((SUBLANES, LANES), 0)
    for i, row in enumerate(rows):
        left = jnp.where(row_of == i, row, left)
    src, dst = iota((LANES, LANES), 0), iota((LANES, LANES), 1)
    same = (src // high_count == dst // high_count) & (dst < used)
    before = jnp.where((same & (src < dst)) | (dst == used + src // high_count), 1.0, 0.0)
    shift = jnp.where(same & (src + 1 == dst), 0.5, 0.0)
    before = jnp.where(src < used, before, 0.0)
    shift = jnp.where(src < used, shift, 0.0)
    moved = jnp.dot(
        left,
        jnp.concatenate([before, shift], axis=1),
        precision=lax.Precision.HIGHEST,
        preferred_element_type=jnp.float32,
    )
    out_row, in_row = iota((LOW, LOW), 0), iota((LOW, LOW), 1)
    lower = jnp.where(in_row < out_row, 1.0, jnp.where(in_row == out_row, 0.5, 0.0))
    within = jnp.dot(
        lower,
        jnp.concatenate(inner, axis=1),
        precision=lax.Precision.HIGHEST,
        preferred_element_type=jnp.float32,
    )
    first = iota((LOW, LANES), 0) == 0
    sums = []
    for d in range(dates):
        part = within[:, d * LANES : (d + 1) * LANES] + moved[d : d + 1, :LANES]
        back = moved[dates + d : dates + d + 1, LANES:]
        sums.append(part - jnp.where(first, back, 0.0))
    return sums


def flat_table(sums, bands, bins):
    high_count = bins // LOW
    used = bands * high_count
    lane = iota((SUBLANES, LANES), 1)
    total_lane = jnp.minimum(used + lane // high_count, LANES - 1)
    total = jnp.take_along_axis(sums[:SUBLANES], total_lane, axis=1)[:1]
    cumulative = (sums / jnp.maximum(total, 1.0)).astype(jnp.bfloat16).astype(jnp.float32)
    band_lane = iota((LOW, LANES), 1) // high_count
    wide = jnp.concatenate(
        [jnp.where(band_lane == b, cumulative, 0.0) for b in range(bands)], axis=0
    ).astype(jnp.bfloat16)
    src, dst = iota((LANES, bins), 0), iota((LANES, bins), 1)
    spread = jnp.where((src % high_count == dst // LOW) & (src < used), 1.0, 0.0).astype(
        jnp.bfloat16
    )
    placed = jnp.dot(wide, spread, preferred_element_type=jnp.float32)
    rows, cols = iota(placed.shape, 0), iota(placed.shape, 1)
    placed = jnp.where(rows % LOW == cols % LOW, placed, 0.0).astype(jnp.bfloat16)
    pick = jnp.where(
        iota((SUBLANES, bands * LOW), 1) // LOW == iota((SUBLANES, bands * LOW), 0), 1.0, 0.0
    ).astype(jnp.bfloat16)
    return jnp.dot(pick, placed, preferred_element_type=jnp.float32)


def gather_lanes(table, index):
    parts = table.shape[1] // LANES
    inner = index % LANES
    out = jnp.take_along_axis(table[:, :LANES], inner, axis=1)
    for part in range(1, parts):
        other = jnp.take_along_axis(table[:, part * LANES : (part + 1) * LANES], inner, axis=1)
        out = jnp.where(index >= part * LANES, other, out)
    return out


def interpolate(table, position, bins):
    low = jnp.floor(position)
    first = low.astype(jnp.int32)
    second = jnp.minimum(first + 1, bins - 1)
    low_weight = rounded(1.0 - jnp.abs(position - low))
    high_weight = rounded(jnp.maximum(0.0, 1.0 - jnp.abs(position - (low + 1.0))))
    return low_weight * gather_lanes(table, first) + high_weight * gather_lanes(table, second)


def own_fit_rows(live_ref, day_ref, date_slots, dates, first_date):
    size = max(dates, SUBLANES)
    rows, cols = iota((size, size), 0), iota((size, size), 1)

    def place(t, carry):
        day_r, day_c, live_r, live_c = carry
        day = day_ref[t]
        live = (lax.rem(t, date_slots) < live_ref[lax.div(t, date_slots)]).astype(jnp.int32)
        return (
            jnp.where(rows == t, day, day_r),
            jnp.where(cols == t, day, day_c),
            jnp.where(rows == t, live, live_r),
            jnp.where(cols == t, live, live_c),
        )

    zero = jnp.zeros((size, size), jnp.int32)
    day_r, day_c, live_r, live_c = lax.fori_loop(
        0, dates, place, (zero, zero, zero, zero), unroll=dates <= 16
    )
    base = jnp.cos((2.0 * math.pi / YEAR) * (day_r - day_c).astype(jnp.float32))
    older, newer = jnp.ones_like(base), base
    total = older + newer
    for _ in range(HARMONICS - 1):
        older, newer = newer, 2.0 * base * newer - older
        total = total + newer
    eye = jnp.where(rows == cols, 1.0, 0.0)
    work = jnp.where((live_r * live_c) == 1, total, 0.0) + RIDGE * eye
    inverse = eye
    for k in range(dates):
        pivot = work[k : k + 1, k : k + 1]
        row_w, row_i = work[k : k + 1, :] / pivot, inverse[k : k + 1, :] / pivot
        column = work[:, k : k + 1]
        work = jnp.where(rows == k, row_w, work - column * row_w)
        inverse = jnp.where(rows == k, row_i, inverse - column * row_i)
    return [
        jnp.sum(jnp.where(rows == first_date + d, inverse, 0.0), axis=0, keepdims=True)
        for d in range(date_slots)
    ]


def kernel(
    groups,
    spaces,
    live_hbm,
    day_hbm,
    reflect_hbm,
    clear_hbm,
    quantile_hbm,
    out_ref,
    live_ref,
    day_ref,
    reflect_ref,
    clear_ref,
    quantile_ref,
    in_sems,
    padded,
    quant,
    hist_own,
    hist_all,
    mask_all,
    series_all,
    hist_send,
    hist_recv,
    mask_send,
    mask_recv,
    series_send,
    series_recv,
):
    bands, date_slots, pixels = reflect_ref.shape
    bins = quantile_ref.shape[1]
    dates = date_slots * groups
    my_date, my_space = lax.axis_index("date"), lax.axis_index("space")
    date_peers = [lax.rem(my_date + i, groups) for i in range(1, groups)]
    space_peers = [lax.rem(my_space + i, spaces) for i in range(1, spaces)]

    barrier = pltpu.get_barrier_semaphore()
    for peer in space_peers:
        pl.semaphore_signal(barrier, inc=1, device_id={"space": peer}, device_id_type=MESH)
    for peer in date_peers:
        pl.semaphore_signal(barrier, inc=1, device_id={"date": peer}, device_id_type=MESH)

    loads = [
        pltpu.make_async_copy(src, dst, in_sems.at[i])
        for i, (src, dst) in enumerate(
            (
                (reflect_hbm, reflect_ref),
                (clear_hbm, clear_ref),
                (live_hbm, live_ref),
                (day_hbm, day_ref),
                (quantile_hbm, quantile_ref),
            )
        )
    ]
    for load in loads:
        load.start()
    padded[...] = jnp.zeros_like(padded)
    quant[...] = jnp.zeros_like(quant)
    for load in loads:
        load.wait()
    for b in range(bands):
        for d in range(date_slots):
            padded[d, b : b + 1, :] = reflect_ref[b, d : d + 1, :]
    quant[:bands] = rounded(quantile_ref[...])

    inner, spill = [], []
    for d in range(date_slots):
        live = lax.rem(jnp.int32(d), date_slots) < live_ref[my_date]
        valid = clear_ref[d : d + 1, :] * live.astype(jnp.int32)
        mask_all[my_date, d : d + 1, :] = valid.astype(jnp.float32)
        block, extra = block_histogram(
            padded[d], jnp.broadcast_to(valid, (SUBLANES, pixels)) == 1, bands, bins
        )
        inner.append(block)
        spill.append(extra)
    sums = running_sums(inner, spill, bands, bins)
    for d in range(date_slots):
        hist_own[d] = sums[d]

    pl.semaphore_wait(barrier, groups + spaces - 2)

    copies = []
    for peer in space_peers:
        copy = pltpu.make_async_remote_copy(
            src_ref=hist_own,
            dst_ref=hist_all.at[my_space],
            send_sem=hist_send.at[peer],
            recv_sem=hist_recv.at[my_space],
            device_id={"space": peer},
            device_id_type=MESH,
        )
        copy.start()
        copies.append(copy)
    for peer in date_peers:
        copy = pltpu.make_async_remote_copy(
            src_ref=mask_all.at[my_date],
            dst_ref=mask_all.at[my_date],
            send_sem=mask_send.at[peer],
            recv_sem=mask_recv.at[my_date],
            device_id={"date": peer},
            device_id_type=MESH,
        )
        copy.start()
        copies.append(copy)

    total = [hist_own[d] for d in range(date_slots)]
    for peer in space_peers:
        pltpu.make_async_remote_copy(
            src_ref=hist_own,
            dst_ref=hist_all.at[peer],
            send_sem=hist_send.at[peer],
            recv_sem=hist_recv.at[peer],
            device_id={"space": peer},
            device_id_type=MESH,
        ).wait_recv()
        for d in range(date_slots):
            total[d] = total[d] + hist_all[peer, d]

    for d in range(date_slots):
        table = flat_table(total[d], bands, bins)
        for start in range(0, pixels, LANES):
            span = slice(start, start + LANES)
            position = jnp.clip(bins * padded[d, :, span] - 0.5, 0.0, bins - 1.0)
            level = interpolate(table, position, bins)
            level = jnp.clip(bins * level - 0.5, 0.0, bins - 1.0)
            matched = interpolate(quant[...], level, bins)
            series_all[my_date, d, :, span] = matched[:bands] * mask_all[my_date, d : d + 1, span]
        for peer in date_peers:
            copy = pltpu.make_async_remote_copy(
                src_ref=series_all.at[my_date, d],
                dst_ref=series_all.at[my_date, d],
                send_sem=series_send.at[peer, d],
                recv_sem=series_recv.at[my_date, d],
                device_id={"date": peer},
                device_id_type=MESH,
            )
            copy.start()
            copies.append(copy)

    fit_rows = own_fit_rows(live_ref, day_ref, date_slots, dates, my_date * date_slots)

    for peer in date_peers:
        pltpu.make_async_remote_copy(
            src_ref=mask_all.at[peer],
            dst_ref=mask_all.at[peer],
            send_sem=mask_send.at[peer],
            recv_sem=mask_recv.at[peer],
            device_id={"date": peer},
            device_id_type=MESH,
        ).wait_recv()
    for d in range(date_slots):
        for peer in date_peers:
            pltpu.make_async_remote_copy(
                src_ref=series_all.at[peer, d],
                dst_ref=series_all.at[peer, d],
                send_sem=series_send.at[peer, d],
                recv_sem=series_recv.at[peer, d],
                device_id={"date": peer},
                device_id_type=MESH,
            ).wait_recv()

    count = jnp.zeros((1, pixels), jnp.float32)
    summed = jnp.zeros((bands, pixels), jnp.float32)
    gaps = [jnp.zeros((1, pixels), jnp.float32) for _ in range(date_slots)]
    fits = [jnp.zeros((bands, pixels), jnp.float32) for _ in range(date_slots)]
    for t in range(dates):
        g, s = divmod(t, date_slots)
        mask, series = mask_all[g, s : s + 1, :], series_all[g, s]
        count += mask
        summed += series
        for d in range(date_slots):
            weight = fit_rows[d][:, t : t + 1]
            gaps[d] += weight * (1.0 - mask)
            fits[d] += weight * series
    mean = summed / jnp.maximum(count, 1.0)
    for d in range(date_slots):
        left = mask_all[my_date, d : d + 1, :] * (fits[d] + gaps[d] * mean)
        for b in range(bands):
            out_ref[b, d : d + 1, :] = left[b : b + 1]

    for copy in copies:
        copy.wait_send()


def per_device(groups, spaces, reflect, clear_sky, live_dates, day_of_year, ref_quantile):
    date_slots, bands, pixels = reflect.shape
    bins = ref_quantile.shape[1]
    by_band = jnp.transpose(reflect, (1, 0, 2))
    residual = pl.pallas_call(
        functools.partial(kernel, groups, spaces),
        out_shape=jax.ShapeDtypeStruct(by_band.shape, jnp.float32),
        in_specs=[pl.BlockSpec(memory_space=pltpu.HBM)] * 5,
        out_specs=pl.BlockSpec(memory_space=pltpu.VMEM),
        scratch_shapes=[
            pltpu.SMEM(live_dates.shape, jnp.int32),
            pltpu.SMEM(day_of_year.shape, jnp.int32),
            pltpu.VMEM(by_band.shape, jnp.float32),
            pltpu.VMEM(clear_sky.shape, jnp.int32),
            pltpu.VMEM(ref_quantile.shape, jnp.float32),
            pltpu.SemaphoreType.DMA((5,)),
            pltpu.VMEM((date_slots, SUBLANES, pixels), jnp.float32),
            pltpu.VMEM((SUBLANES, bins), jnp.float32),
            pltpu.VMEM((date_slots, LOW, LANES), jnp.float32),
            pltpu.VMEM((spaces, date_slots, LOW, LANES), jnp.float32),
            pltpu.VMEM((groups, date_slots, pixels), jnp.float32),
            pltpu.VMEM((groups, date_slots, bands, pixels), jnp.float32),
            pltpu.SemaphoreType.DMA((spaces,)),
            pltpu.SemaphoreType.DMA((spaces,)),
            pltpu.SemaphoreType.DMA((groups,)),
            pltpu.SemaphoreType.DMA((groups,)),
            pltpu.SemaphoreType.DMA((groups, date_slots)),
            pltpu.SemaphoreType.DMA((groups, date_slots)),
        ],
        compiler_params=pltpu.CompilerParams(
            collective_id=0, has_side_effects=True, vmem_limit_bytes=16 * 2**20
        ),
    )(live_dates, day_of_year, by_band, clear_sky, ref_quantile)
    return jnp.transpose(residual, (1, 0, 2))


def solution(mesh):
    return jax.shard_map(
        functools.partial(per_device, mesh.shape["date"], mesh.shape["space"]),
        mesh=mesh,
        in_specs=(
            P("date", None, ("tiles", "space")),
            P("date", ("tiles", "space")),
            P(),
            P(),
            P(),
        ),
        out_specs=P("date", None, ("tiles", "space")),
        check_vma=False,
    )
```

```python
import functools
import math

import jax
import jax.numpy as jnp
from jax import lax
from jax.experimental import pallas as pl
from jax.experimental.pallas import tpu as pltpu
from jax.sharding import PartitionSpec as P

MESH = pl.DeviceIdType.MESH
HARMONICS = 7
RIDGE = 1.0
YEAR = 365
LOW = 16
LANES = 128
SUBLANES = 8


def iota(shape, dim):
    return lax.broadcasted_iota(jnp.int32, shape, dim)


def rounded(x):
    return x.astype(jnp.bfloat16).astype(jnp.float32)


def block_histogram(values, valid, bands, bins):
    high_count = bins // LOW
    pixels = values.shape[1]
    position = jnp.clip(bins * values - 0.5, 0.0, bins - 1.0)
    high = jnp.floor(position * (1.0 / LOW))
    local = position - LOW * high
    marked = jnp.where(valid, high, -1.0)
    high_iota = iota((high_count, pixels), 0).astype(jnp.float32)
    low_iota = iota((LOW, pixels), 0).astype(jnp.float32)
    hot, tents = [], []
    for b in range(bands):
        hot.append(jnp.where(high_iota == marked[b : b + 1], 1.0, 0.0).astype(jnp.bfloat16))
        tents.append(
            jnp.maximum(0.0, 1.0 - jnp.abs(local[b : b + 1] - low_iota)).astype(jnp.bfloat16)
        )
    spill = jnp.maximum(0.0, 1.0 - jnp.abs(local - LOW))
    tents.append(jnp.concatenate([spill, jnp.zeros_like(spill)], axis=0).astype(jnp.bfloat16))
    hot.append(jnp.zeros((LANES - bands * high_count, pixels), jnp.bfloat16))
    counts = lax.dot_general(
        jnp.concatenate(tents, axis=0),
        jnp.concatenate(hot, axis=0),
        (((1,), (1,)), ((), ())),
        preferred_element_type=jnp.float32,
    )
    band_lane = iota((LOW, LANES), 1) // high_count
    inner = jnp.zeros((LOW, LANES), jnp.float32)
    for b in range(bands):
        inner += jnp.where(band_lane == b, counts[b * LOW : (b + 1) * LOW], 0.0)
    outer = counts[bands * LOW : bands * LOW + SUBLANES]
    own = iota((SUBLANES, LANES), 0) == band_lane[:SUBLANES]
    return inner, jnp.sum(jnp.where(own, outer, 0.0), axis=0, keepdims=True)


def running_sums(inner, spill, bands, bins):
    high_count = bins // LOW
    dates = len(inner)
    used = bands * high_count
    column = [jnp.sum(inner[d], axis=0, keepdims=True) + spill[d] for d in range(dates)]
    rows = column + spill
    left = jnp.zeros((SUBLANES, LANES), jnp.float32)
    row_of = iota((SUBLANES, LANES), 0)
    for i, row in enumerate(rows):
        left = jnp.where(row_of == i, row, left)
    src, dst = iota((LANES, LANES), 0), iota((LANES, LANES), 1)
    same = (src // high_count == dst // high_count) & (dst < used)
    before = jnp.where((same & (src < dst)) | (dst == used + src // high_count), 1.0, 0.0)
    shift = jnp.where(same & (src + 1 == dst), 0.5, 0.0)
    before = jnp.where(src < used, before, 0.0)
    shift = jnp.where(src < used, shift, 0.0)
    moved = jnp.dot(
        left,
        jnp.concatenate([before, shift], axis=1),
        precision=lax.Precision.HIGHEST,
        preferred_element_type=jnp.float32,
    )
    out_row, in_row = iota((LOW, LOW), 0), iota((LOW, LOW), 1)
    lower = jnp.where(in_row < out_row, 1.0, jnp.where(in_row == out_row, 0.5, 0.0))
    within = jnp.dot(
        lower,
        jnp.concatenate(inner, axis=1),
        precision=lax.Precision.HIGHEST,
        preferred_element_type=jnp.float32,
    )
    first = iota((LOW, LANES), 0) == 0
    sums = []
    for d in range(dates):
        part = within[:, d * LANES : (d + 1) * LANES] + moved[d : d + 1, :LANES]
        back = moved[dates + d : dates + d + 1, LANES:]
        sums.append(part - jnp.where(first, back, 0.0))
    return sums


def flat_table(sums, bands, bins):
    high_count = bins // LOW
    used = bands * high_count
    lane = iota((SUBLANES, LANES), 1)
    total_lane = jnp.minimum(used + lane // high_count, LANES - 1)
    total = jnp.take_along_axis(sums[:SUBLANES], total_lane, axis=1)[:1]
    cumulative = (sums / jnp.maximum(total, 1.0)).astype(jnp.bfloat16).astype(jnp.float32)
    band_lane = iota((LOW, LANES), 1) // high_count
    wide = jnp.concatenate(
        [jnp.where(band_lane == b, cumulative, 0.0) for b in range(bands)], axis=0
    ).astype(jnp.bfloat16)
    src, dst = iota((LANES, bins), 0), iota((LANES, bins), 1)
    spread = jnp.where((src % high_count == dst // LOW) & (src < used), 1.0, 0.0).astype(
        jnp.bfloat16
    )
    placed = jnp.dot(wide, spread, preferred_element_type=jnp.float32)
    rows, cols = iota(placed.shape, 0), iota(placed.shape, 1)
    placed = jnp.where(rows % LOW == cols % LOW, placed, 0.0).astype(jnp.bfloat16)
    pick = jnp.where(
        iota((SUBLANES, bands * LOW), 1) // LOW == iota((SUBLANES, bands * LOW), 0), 1.0, 0.0
    ).astype(jnp.bfloat16)
    return jnp.dot(pick, placed, preferred_element_type=jnp.float32)


def gather_lanes(table, index):
    parts = table.shape[1] // LANES
    inner = index % LANES
    out = jnp.take_along_axis(table[:, :LANES], inner, axis=1)
    for part in range(1, parts):
        other = jnp.take_along_axis(table[:, part * LANES : (part + 1) * LANES], inner, axis=1)
        out = jnp.where(index >= part * LANES, other, out)
    return out


def interpolate(table, position, bins):
    low = jnp.floor(position)
    first = low.astype(jnp.int32)
    second = jnp.minimum(first + 1, bins - 1)
    low_weight = rounded(1.0 - jnp.abs(position - low))
    high_weight = rounded(jnp.maximum(0.0, 1.0 - jnp.abs(position - (low + 1.0))))
    return low_weight * gather_lanes(table, first) + high_weight * gather_lanes(table, second)


def own_fit_rows(live_ref, day_ref, date_slots, dates, first_date):
    size = max(dates, SUBLANES)
    rows, cols = iota((size, size), 0), iota((size, size), 1)

    def place(t, carry):
        day_r, day_c, live_r, live_c = carry
        day = day_ref[t]
        live = (lax.rem(t, date_slots) < live_ref[lax.div(t, date_slots)]).astype(jnp.int32)
        return (
            jnp.where(rows == t, day, day_r),
            jnp.where(cols == t, day, day_c),
            jnp.where(rows == t, live, live_r),
            jnp.where(cols == t, live, live_c),
        )

    zero = jnp.zeros((size, size), jnp.int32)
    day_r, day_c, live_r, live_c = lax.fori_loop(
        0, dates, place, (zero, zero, zero, zero), unroll=dates <= 16
    )
    base = jnp.cos((2.0 * math.pi / YEAR) * (day_r - day_c).astype(jnp.float32))
    older, newer = jnp.ones_like(base), base
    total = older + newer
    for _ in range(HARMONICS - 1):
        older, newer = newer, 2.0 * base * newer - older
        total = total + newer
    eye = jnp.where(rows == cols, 1.0, 0.0)
    work = jnp.where((live_r * live_c) == 1, total, 0.0) + RIDGE * eye
    inverse = eye
    for k in range(dates):
        pivot = work[k : k + 1, k : k + 1]
        row_w, row_i = work[k : k + 1, :] / pivot, inverse[k : k + 1, :] / pivot
        column = work[:, k : k + 1]
        work = jnp.where(rows == k, row_w, work - column * row_w)
        inverse = jnp.where(rows == k, row_i, inverse - column * row_i)
    return [
        jnp.sum(jnp.where(rows == first_date + d, inverse, 0.0), axis=0, keepdims=True)
        for d in range(date_slots)
    ]


def kernel(
    groups,
    spaces,
    live_hbm,
    day_hbm,
    reflect_hbm,
    clear_hbm,
    quantile_hbm,
    out_ref,
    live_ref,
    day_ref,
    reflect_ref,
    clear_ref,
    quantile_ref,
    in_sems,
    padded,
    quant,
    hist_own,
    hist_all,
    mask_all,
    series_all,
    hist_send,
    hist_recv,
    mask_send,
    mask_recv,
    series_send,
    series_recv,
):
    bands, date_slots, pixels = reflect_ref.shape
    bins = quantile_ref.shape[1]
    dates = date_slots * groups
    my_date, my_space = lax.axis_index("date"), lax.axis_index("space")
    date_peers = [lax.rem(my_date + i, groups) for i in range(1, groups)]
    space_peers = [lax.rem(my_space + i, spaces) for i in range(1, spaces)]

    barrier = pltpu.get_barrier_semaphore()
    for peer in space_peers:
        pl.semaphore_signal(barrier, inc=1, device_id={"space": peer}, device_id_type=MESH)
    for peer in date_peers:
        pl.semaphore_signal(barrier, inc=1, device_id={"date": peer}, device_id_type=MESH)

    loads = [
        pltpu.make_async_copy(src, dst, in_sems.at[i])
        for i, (src, dst) in enumerate(
            (
                (reflect_hbm, reflect_ref),
                (clear_hbm, clear_ref),
                (live_hbm, live_ref),
                (day_hbm, day_ref),
                (quantile_hbm, quantile_ref),
            )
        )
    ]
    for load in loads:
        load.start()
    padded[...] = jnp.zeros_like(padded)
    quant[...] = jnp.zeros_like(quant)
    for load in loads:
        load.wait()
    for b in range(bands):
        for d in range(date_slots):
            padded[d, b : b + 1, :] = reflect_ref[b, d : d + 1, :]
    quant[:bands] = rounded(quantile_ref[...])

    inner, spill = [], []
    for d in range(date_slots):
        live = lax.rem(jnp.int32(d), date_slots) < live_ref[my_date]
        valid = clear_ref[d : d + 1, :] * live.astype(jnp.int32)
        mask_all[my_date, d : d + 1, :] = valid.astype(jnp.float32)
        block, extra = block_histogram(
            padded[d], jnp.broadcast_to(valid, (SUBLANES, pixels)) == 1, bands, bins
        )
        inner.append(block)
        spill.append(extra)
    sums = running_sums(inner, spill, bands, bins)
    for d in range(date_slots):
        hist_own[d] = sums[d]

    pl.semaphore_wait(barrier, groups + spaces - 2)

    copies = []
    for peer in space_peers:
        copy = pltpu.make_async_remote_copy(
            src_ref=hist_own,
            dst_ref=hist_all.at[my_space],
            send_sem=hist_send.at[peer],
            recv_sem=hist_recv.at[my_space],
            device_id={"space": peer},
            device_id_type=MESH,
        )
        copy.start()
        copies.append(copy)
    for peer in date_peers:
        copy = pltpu.make_async_remote_copy(
            src_ref=mask_all.at[my_date],
            dst_ref=mask_all.at[my_date],
            send_sem=mask_send.at[peer],
            recv_sem=mask_recv.at[my_date],
            device_id={"date": peer},
            device_id_type=MESH,
        )
        copy.start()
        copies.append(copy)

    total = [hist_own[d] for d in range(date_slots)]
    for peer in space_peers:
        pltpu.make_async_remote_copy(
            src_ref=hist_own,
            dst_ref=hist_all.at[peer],
            send_sem=hist_send.at[peer],
            recv_sem=hist_recv.at[peer],
            device_id={"space": peer},
            device_id_type=MESH,
        ).wait_recv()
        for d in range(date_slots):
            total[d] = total[d] + hist_all[peer, d]

    for d in range(date_slots):
        table = flat_table(total[d], bands, bins)
        for start in range(0, pixels, LANES):
            span = slice(start, start + LANES)
            position = jnp.clip(bins * padded[d, :, span] - 0.5, 0.0, bins - 1.0)
            level = interpolate(table, position, bins)
            level = jnp.clip(bins * level - 0.5, 0.0, bins - 1.0)
            matched = interpolate(quant[...], level, bins)
            series_all[my_date, d, :, span] = matched[:bands] * mask_all[my_date, d : d + 1, span]
        for peer in date_peers:
            copy = pltpu.make_async_remote_copy(
                src_ref=series_all.at[my_date, d],
                dst_ref=series_all.at[my_date, d],
                send_sem=series_send.at[peer, d],
                recv_sem=series_recv.at[my_date, d],
                device_id={"date": peer},
                device_id_type=MESH,
            )
            copy.start()
            copies.append(copy)

    fit_rows = own_fit_rows(live_ref, day_ref, date_slots, dates, my_date * date_slots)

    for peer in date_peers:
        pltpu.make_async_remote_copy(
            src_ref=mask_all.at[peer],
            dst_ref=mask_all.at[peer],
            send_sem=mask_send.at[peer],
            recv_sem=mask_recv.at[peer],
            device_id={"date": peer},
            device_id_type=MESH,
        ).wait_recv()
    for d in range(date_slots):
        for peer in date_peers:
            pltpu.make_async_remote_copy(
                src_ref=series_all.at[peer, d],
                dst_ref=series_all.at[peer, d],
                send_sem=series_send.at[peer, d],
                recv_sem=series_recv.at[peer, d],
                device_id={"date": peer},
                device_id_type=MESH,
            ).wait_recv()

    count = jnp.zeros((1, pixels), jnp.float32)
    summed = jnp.zeros((bands, pixels), jnp.float32)
    gaps = [jnp.zeros((1, pixels), jnp.float32) for _ in range(date_slots)]
    fits = [jnp.zeros((bands, pixels), jnp.float32) for _ in range(date_slots)]
    for t in range(dates):
        g, s = divmod(t, date_slots)
        mask, series = mask_all[g, s : s + 1, :], series_all[g, s]
        count += mask
        summed += series
        for d in range(date_slots):
            weight = fit_rows[d][:, t : t + 1]
            gaps[d] += weight * (1.0 - mask)
            fits[d] += weight * series
    mean = summed / jnp.maximum(count, 1.0)
    for d in range(date_slots):
        left = mask_all[my_date, d : d + 1, :] * (fits[d] + gaps[d] * mean)
        for b in range(bands):
            out_ref[b, d : d + 1, :] = left[b : b + 1]

    for copy in copies:
        copy.wait_send()


def per_device(groups, spaces, reflect, clear_sky, live_dates, day_of_year, ref_quantile):
    date_slots, bands, pixels = reflect.shape
    bins = ref_quantile.shape[1]
    by_band = jnp.transpose(reflect, (1, 0, 2))
    residual = pl.pallas_call(
        functools.partial(kernel, groups, spaces),
        out_shape=jax.ShapeDtypeStruct(by_band.shape, jnp.float32),
        in_specs=[pl.BlockSpec(memory_space=pltpu.HBM)] * 5,
        out_specs=pl.BlockSpec(memory_space=pltpu.VMEM),
        scratch_shapes=[
            pltpu.SMEM(live_dates.shape, jnp.int32),
            pltpu.SMEM(day_of_year.shape, jnp.int32),
            pltpu.VMEM(by_band.shape, jnp.float32),
            pltpu.VMEM(clear_sky.shape, jnp.int32),
            pltpu.VMEM(ref_quantile.shape, jnp.float32),
            pltpu.SemaphoreType.DMA((5,)),
            pltpu.VMEM((date_slots, SUBLANES, pixels), jnp.float32),
            pltpu.VMEM((SUBLANES, bins), jnp.float32),
            pltpu.VMEM((date_slots, LOW, LANES), jnp.float32),
            pltpu.VMEM((spaces, date_slots, LOW, LANES), jnp.float32),
            pltpu.VMEM((groups, date_slots, pixels), jnp.float32),
            pltpu.VMEM((groups, date_slots, bands, pixels), jnp.float32),
            pltpu.SemaphoreType.DMA((spaces,)),
            pltpu.SemaphoreType.DMA((spaces,)),
            pltpu.SemaphoreType.DMA((groups,)),
            pltpu.SemaphoreType.DMA((groups,)),
            pltpu.SemaphoreType.DMA((groups, date_slots)),
            pltpu.SemaphoreType.DMA((groups, date_slots)),
        ],
        compiler_params=pltpu.CompilerParams(
            collective_id=0, has_side_effects=True, vmem_limit_bytes=16 * 2**20
        ),
    )(
        *(
            pltpu.with_memory_space_constraint(x, pltpu.HBM)
            for x in (live_dates, day_of_year, by_band, clear_sky, ref_quantile)
        )
    )
    return jnp.transpose(residual, (1, 0, 2))


def solution(mesh):
    return jax.shard_map(
        functools.partial(per_device, mesh.shape["date"], mesh.shape["space"]),
        mesh=mesh,
        in_specs=(
            P("date", None, ("tiles", "space")),
            P("date", ("tiles", "space")),
            P(),
            P(),
            P(),
        ),
        out_specs=P("date", None, ("tiles", "space")),
        check_vma=False,
    )
```

```python
import functools
import math

import jax
import jax.numpy as jnp
from jax import lax
from jax.experimental import pallas as pl
from jax.experimental.pallas import tpu as pltpu
from jax.sharding import PartitionSpec as P

MESH = pl.DeviceIdType.MESH
HARMONICS = 7
RIDGE = 1.0
YEAR = 365
LOW = 16
LANES = 128
SUBLANES = 8


def iota(shape, dim):
    return lax.broadcasted_iota(jnp.int32, shape, dim)


def rounded(x):
    return x.astype(jnp.bfloat16).astype(jnp.float32)


def block_histogram(values, valid, bands, bins):
    high_count = bins // LOW
    pixels = values.shape[1]
    position = jnp.clip(bins * values - 0.5, 0.0, bins - 1.0)
    high = jnp.floor(position * (1.0 / LOW))
    local = position - LOW * high
    marked = jnp.where(valid, high, -1.0)
    high_iota = iota((high_count, pixels), 0).astype(jnp.float32)
    low_iota = iota((LOW, pixels), 0).astype(jnp.float32)
    hot, tents = [], []
    for b in range(bands):
        hot.append(jnp.where(high_iota == marked[b : b + 1], 1.0, 0.0).astype(jnp.bfloat16))
        tents.append(
            jnp.maximum(0.0, 1.0 - jnp.abs(local[b : b + 1] - low_iota)).astype(jnp.bfloat16)
        )
    spill = jnp.maximum(0.0, 1.0 - jnp.abs(local - LOW))
    tents.append(jnp.concatenate([spill, jnp.zeros_like(spill)], axis=0).astype(jnp.bfloat16))
    hot.append(jnp.zeros((LANES - bands * high_count, pixels), jnp.bfloat16))
    counts = lax.dot_general(
        jnp.concatenate(tents, axis=0),
        jnp.concatenate(hot, axis=0),
        (((1,), (1,)), ((), ())),
        preferred_element_type=jnp.float32,
    )
    band_lane = iota((LOW, LANES), 1) // high_count
    inner = jnp.zeros((LOW, LANES), jnp.float32)
    for b in range(bands):
        inner += jnp.where(band_lane == b, counts[b * LOW : (b + 1) * LOW], 0.0)
    outer = counts[bands * LOW : bands * LOW + SUBLANES]
    own = iota((SUBLANES, LANES), 0) == band_lane[:SUBLANES]
    return inner, jnp.sum(jnp.where(own, outer, 0.0), axis=0, keepdims=True)


def running_sums(inner, spill, bands, bins):
    high_count = bins // LOW
    dates = len(inner)
    used = bands * high_count
    column = [jnp.sum(inner[d], axis=0, keepdims=True) + spill[d] for d in range(dates)]
    rows = column + spill
    left = jnp.zeros((SUBLANES, LANES), jnp.float32)
    row_of = iota((SUBLANES, LANES), 0)
    for i, row in enumerate(rows):
        left = jnp.where(row_of == i, row, left)
    src, dst = iota((LANES, LANES), 0), iota((LANES, LANES), 1)
    same = (src // high_count == dst // high_count) & (dst < used)
    before = jnp.where((same & (src < dst)) | (dst == used + src // high_count), 1.0, 0.0)
    shift = jnp.where(same & (src + 1 == dst), 0.5, 0.0)
    before = jnp.where(src < used, before, 0.0)
    shift = jnp.where(src < used, shift, 0.0)
    moved = jnp.dot(
        left,
        jnp.concatenate([before, shift], axis=1),
        precision=lax.Precision.HIGHEST,
        preferred_element_type=jnp.float32,
    )
    out_row, in_row = iota((LOW, LOW), 0), iota((LOW, LOW), 1)
    lower = jnp.where(in_row < out_row, 1.0, jnp.where(in_row == out_row, 0.5, 0.0))
    within = jnp.dot(
        lower,
        jnp.concatenate(inner, axis=1),
        precision=lax.Precision.HIGHEST,
        preferred_element_type=jnp.float32,
    )
    first = iota((LOW, LANES), 0) == 0
    sums = []
    for d in range(dates):
        part = within[:, d * LANES : (d + 1) * LANES] + moved[d : d + 1, :LANES]
        back = moved[dates + d : dates + d + 1, LANES:]
        sums.append(part - jnp.where(first, back, 0.0))
    return sums


def flat_table(sums, bands, bins):
    high_count = bins // LOW
    used = bands * high_count
    lane = iota((SUBLANES, LANES), 1)
    total_lane = jnp.minimum(used + lane // high_count, LANES - 1)
    total = jnp.take_along_axis(sums[:SUBLANES], total_lane, axis=1)[:1]
    cumulative = (sums / jnp.maximum(total, 1.0)).astype(jnp.bfloat16).astype(jnp.float32)
    band_lane = iota((LOW, LANES), 1) // high_count
    wide = jnp.concatenate(
        [jnp.where(band_lane == b, cumulative, 0.0) for b in range(bands)], axis=0
    ).astype(jnp.bfloat16)
    src, dst = iota((LANES, bins), 0), iota((LANES, bins), 1)
    spread = jnp.where((src % high_count == dst // LOW) & (src < used), 1.0, 0.0).astype(
        jnp.bfloat16
    )
    placed = jnp.dot(wide, spread, preferred_element_type=jnp.float32)
    rows, cols = iota(placed.shape, 0), iota(placed.shape, 1)
    placed = jnp.where(rows % LOW == cols % LOW, placed, 0.0).astype(jnp.bfloat16)
    pick = jnp.where(
        iota((SUBLANES, bands * LOW), 1) // LOW == iota((SUBLANES, bands * LOW), 0), 1.0, 0.0
    ).astype(jnp.bfloat16)
    return jnp.dot(pick, placed, preferred_element_type=jnp.float32)


def gather_lanes(table, index):
    parts = table.shape[1] // LANES
    inner = index % LANES
    out = jnp.take_along_axis(table[:, :LANES], inner, axis=1)
    for part in range(1, parts):
        other = jnp.take_along_axis(table[:, part * LANES : (part + 1) * LANES], inner, axis=1)
        out = jnp.where(index >= part * LANES, other, out)
    return out


def interpolate(table, position, bins):
    low = jnp.floor(position)
    first = low.astype(jnp.int32)
    second = jnp.minimum(first + 1, bins - 1)
    low_weight = rounded(1.0 - jnp.abs(position - low))
    high_weight = rounded(jnp.maximum(0.0, 1.0 - jnp.abs(position - (low + 1.0))))
    return low_weight * gather_lanes(table, first) + high_weight * gather_lanes(table, second)


def own_fit_rows(live_ref, day_ref, date_slots, dates, first_date):
    size = max(dates, SUBLANES)
    rows, cols = iota((size, size), 0), iota((size, size), 1)

    def place(t, carry):
        day_r, day_c, live_r, live_c = carry
        day = day_ref[t]
        live = (lax.rem(t, date_slots) < live_ref[lax.div(t, date_slots)]).astype(jnp.int32)
        return (
            jnp.where(rows == t, day, day_r),
            jnp.where(cols == t, day, day_c),
            jnp.where(rows == t, live, live_r),
            jnp.where(cols == t, live, live_c),
        )

    zero = jnp.zeros((size, size), jnp.int32)
    day_r, day_c, live_r, live_c = lax.fori_loop(
        0, dates, place, (zero, zero, zero, zero), unroll=dates <= 16
    )
    base = jnp.cos((2.0 * math.pi / YEAR) * (day_r - day_c).astype(jnp.float32))
    older, newer = jnp.ones_like(base), base
    total = older + newer
    for _ in range(HARMONICS - 1):
        older, newer = newer, 2.0 * base * newer - older
        total = total + newer
    eye = jnp.where(rows == cols, 1.0, 0.0)
    work = jnp.where((live_r * live_c) == 1, total, 0.0) + RIDGE * eye
    inverse = eye
    for k in range(dates):
        pivot = work[k : k + 1, k : k + 1]
        row_w, row_i = work[k : k + 1, :] / pivot, inverse[k : k + 1, :] / pivot
        column = work[:, k : k + 1]
        work = jnp.where(rows == k, row_w, work - column * row_w)
        inverse = jnp.where(rows == k, row_i, inverse - column * row_i)
    return [
        jnp.sum(jnp.where(rows == first_date + d, inverse, 0.0), axis=0, keepdims=True)
        for d in range(date_slots)
    ]


def kernel(
    groups,
    spaces,
    early,
    live_hbm,
    day_hbm,
    reflect_hbm,
    clear_hbm,
    quantile_hbm,
    out_ref,
    live_ref,
    day_ref,
    reflect_ref,
    clear_ref,
    quantile_ref,
    in_sems,
    padded,
    quant,
    hist_own,
    hist_all,
    mask_all,
    raw_all,
    table_all,
    early_all,
    late_all,
    hist_send,
    hist_recv,
    mask_send,
    mask_recv,
    raw_send,
    raw_recv,
    table_send,
    table_recv,
    late_send,
    late_recv,
):
    bands, date_slots, pixels = reflect_ref.shape
    bins = quantile_ref.shape[1]
    dates = date_slots * groups
    my_date, my_space = lax.axis_index("date"), lax.axis_index("space")
    space_peers = [lax.rem(my_space + i, spaces) for i in range(1, spaces)]

    def each_date_peer(body):
        def step(i, carry):
            body(lax.rem(my_date + i, groups))
            return carry

        if groups <= 8:
            for i in range(1, groups):
                step(i, 0)
        else:
            lax.fori_loop(1, groups, step, 0)

    def to_date(src, dst, send, recv, peer):
        return pltpu.make_async_remote_copy(
            src_ref=src,
            dst_ref=dst,
            send_sem=send,
            recv_sem=recv,
            device_id={"date": peer},
            device_id_type=MESH,
        )

    def mask_copy(peer, slot):
        return to_date(
            mask_all.at[slot], mask_all.at[slot], mask_send.at[peer], mask_recv.at[slot], peer
        )

    def raw_copy(peer, slot):
        return to_date(
            raw_all.at[slot], raw_all.at[slot], raw_send.at[peer], raw_recv.at[slot], peer
        )

    def table_copy(peer, slot):
        return to_date(
            table_all.at[slot], table_all.at[slot], table_send.at[peer], table_recv.at[slot], peer
        )

    def late_copy(peer, slot, d):
        return to_date(
            late_all.at[slot, d],
            late_all.at[slot, d],
            late_send.at[peer, d],
            late_recv.at[slot, d],
            peer,
        )

    barrier = pltpu.get_barrier_semaphore()
    for peer in space_peers:
        pl.semaphore_signal(barrier, inc=1, device_id={"space": peer}, device_id_type=MESH)
    each_date_peer(
        lambda peer: pl.semaphore_signal(
            barrier, inc=1, device_id={"date": peer}, device_id_type=MESH
        )
    )

    loads = [
        pltpu.make_async_copy(src, dst, in_sems.at[i])
        for i, (src, dst) in enumerate(
            (
                (reflect_hbm, reflect_ref),
                (clear_hbm, clear_ref),
                (live_hbm, live_ref),
                (day_hbm, day_ref),
                (quantile_hbm, quantile_ref),
            )
        )
    ]
    for load in loads:
        load.start()
    padded[...] = jnp.zeros_like(padded)
    quant[...] = jnp.zeros_like(quant)
    for load in loads:
        load.wait()
    for b in range(bands):
        for d in range(date_slots):
            row = reflect_ref[b, d : d + 1, :]
            padded[d, b : b + 1, :] = row
            if d < early:
                raw_all[my_date, d, b : b + 1, :] = row
    quant[:bands] = rounded(quantile_ref[...])

    inner, spill = [], []
    for d in range(date_slots):
        live = lax.rem(jnp.int32(d), date_slots) < live_ref[my_date]
        valid = clear_ref[d : d + 1, :] * live.astype(jnp.int32)
        mask_all[my_date, d : d + 1, :] = valid.astype(jnp.float32)
        block, extra = block_histogram(
            padded[d], jnp.broadcast_to(valid, (SUBLANES, pixels)) == 1, bands, bins
        )
        inner.append(block)
        spill.append(extra)
    sums = running_sums(inner, spill, bands, bins)
    for d in range(date_slots):
        hist_own[d] = sums[d]

    pl.semaphore_wait(barrier, groups + spaces - 2)

    hist_copies = []
    for peer in space_peers:
        copy = pltpu.make_async_remote_copy(
            src_ref=hist_own,
            dst_ref=hist_all.at[my_space],
            send_sem=hist_send.at[peer],
            recv_sem=hist_recv.at[my_space],
            device_id={"space": peer},
            device_id_type=MESH,
        )
        copy.start()
        hist_copies.append(copy)
    each_date_peer(lambda peer: raw_copy(peer, my_date).start())
    each_date_peer(lambda peer: mask_copy(peer, my_date).start())

    total = [hist_own[d] for d in range(date_slots)]
    for peer in space_peers:
        pltpu.make_async_remote_copy(
            src_ref=hist_own,
            dst_ref=hist_all.at[peer],
            send_sem=hist_send.at[peer],
            recv_sem=hist_recv.at[peer],
            device_id={"space": peer},
            device_id_type=MESH,
        ).wait_recv()
        for d in range(date_slots):
            total[d] = total[d] + hist_all[peer, d]

    tables = [flat_table(total[d], bands, bins) for d in range(date_slots)]
    for d in range(early):
        table_all[my_date, d] = tables[d]
    each_date_peer(lambda peer: table_copy(peer, my_date).start())

    def match(table, values):
        position = jnp.clip(bins * values - 0.5, 0.0, bins - 1.0)
        level = interpolate(table, position, bins)
        level = jnp.clip(bins * level - 0.5, 0.0, bins - 1.0)
        return interpolate(quant[...], level, bins)[:bands]

    def match_early(slot):
        for d in range(early):
            for start in range(0, pixels, LANES):
                span = slice(start, start + LANES)
                matched = match(table_all[slot, d], padded[d, :, span])
                early_all[slot, d, :, span] = matched * mask_all[slot, d : d + 1, span]

    for d in range(early, date_slots):
        for start in range(0, pixels, LANES):
            span = slice(start, start + LANES)
            matched = match(tables[d], padded[d, :, span])
            late_all[my_date, d - early, :, span] = matched * mask_all[my_date, d : d + 1, span]
        each_date_peer(lambda peer: late_copy(peer, my_date, d - early).start())

    match_early(my_date)
    fit_rows = own_fit_rows(live_ref, day_ref, date_slots, dates, my_date * date_slots)

    def arrived(peer):
        mask_copy(peer, peer).wait_recv()
        raw_copy(peer, peer).wait_recv()
        table_copy(peer, peer).wait_recv()
        for d in range(early):
            padded[d, :bands] = raw_all[peer, d]
        match_early(peer)

    each_date_peer(arrived)

    count = jnp.zeros((1, pixels), jnp.float32)
    summed = jnp.zeros((bands, pixels), jnp.float32)
    gaps = [jnp.zeros((1, pixels), jnp.float32) for _ in range(date_slots)]
    fits = [jnp.zeros((bands, pixels), jnp.float32) for _ in range(date_slots)]
    for g in range(groups):
        for s in range(date_slots):
            t = g * date_slots + s
            mask = mask_all[g, s : s + 1, :]
            count += mask
            for d in range(date_slots):
                gaps[d] += fit_rows[d][:, t : t + 1] * (1.0 - mask)
            if s < early:
                series = early_all[g, s]
                summed += series
                for d in range(date_slots):
                    fits[d] += fit_rows[d][:, t : t + 1] * series
    share = 1.0 / jnp.maximum(count, 1.0)

    def late_arrived(peer):
        for d in range(date_slots - early):
            late_copy(peer, peer, d).wait_recv()

    each_date_peer(late_arrived)
    for g in range(groups):
        for s in range(early, date_slots):
            t = g * date_slots + s
            series = late_all[g, s - early]
            summed += series
            for d in range(date_slots):
                fits[d] += fit_rows[d][:, t : t + 1] * series
    mean = summed * share
    for d in range(date_slots):
        left = mask_all[my_date, d : d + 1, :] * (fits[d] + gaps[d] * mean)
        for b in range(bands):
            out_ref[b, d : d + 1, :] = left[b : b + 1]

    for copy in hist_copies:
        copy.wait_send()

    def sent(peer):
        raw_copy(peer, my_date).wait_send()
        mask_copy(peer, my_date).wait_send()
        table_copy(peer, my_date).wait_send()
        for d in range(date_slots - early):
            late_copy(peer, my_date, d).wait_send()

    each_date_peer(sent)


def per_device(groups, spaces, reflect, clear_sky, live_dates, day_of_year, ref_quantile):
    date_slots, bands, pixels = reflect.shape
    bins = ref_quantile.shape[1]
    early = max(1, date_slots // 2)
    by_band = jnp.transpose(reflect, (1, 0, 2))
    residual = pl.pallas_call(
        functools.partial(kernel, groups, spaces, early),
        out_shape=jax.ShapeDtypeStruct(by_band.shape, jnp.float32),
        in_specs=[pl.BlockSpec(memory_space=pltpu.HBM)] * 5,
        out_specs=pl.BlockSpec(memory_space=pltpu.VMEM),
        scratch_shapes=[
            pltpu.SMEM(live_dates.shape, jnp.int32),
            pltpu.SMEM(day_of_year.shape, jnp.int32),
            pltpu.VMEM(by_band.shape, jnp.float32),
            pltpu.VMEM(clear_sky.shape, jnp.int32),
            pltpu.VMEM(ref_quantile.shape, jnp.float32),
            pltpu.SemaphoreType.DMA((5,)),
            pltpu.VMEM((date_slots, SUBLANES, pixels), jnp.float32),
            pltpu.VMEM((SUBLANES, bins), jnp.float32),
            pltpu.VMEM((date_slots, LOW, LANES), jnp.float32),
            pltpu.VMEM((spaces, date_slots, LOW, LANES), jnp.float32),
            pltpu.VMEM((groups, date_slots, pixels), jnp.float32),
            pltpu.VMEM((groups, early, bands, pixels), jnp.float32),
            pltpu.VMEM((groups, early, SUBLANES, bins), jnp.float32),
            pltpu.VMEM((groups, early, bands, pixels), jnp.float32),
            pltpu.VMEM((groups, date_slots - early, bands, pixels), jnp.float32),
            pltpu.SemaphoreType.DMA((spaces,)),
            pltpu.SemaphoreType.DMA((spaces,)),
            pltpu.SemaphoreType.DMA((groups,)),
            pltpu.SemaphoreType.DMA((groups,)),
            pltpu.SemaphoreType.DMA((groups,)),
            pltpu.SemaphoreType.DMA((groups,)),
            pltpu.SemaphoreType.DMA((groups,)),
            pltpu.SemaphoreType.DMA((groups,)),
            pltpu.SemaphoreType.DMA((groups, date_slots - early)),
            pltpu.SemaphoreType.DMA((groups, date_slots - early)),
        ],
        compiler_params=pltpu.CompilerParams(
            collective_id=0, has_side_effects=True, vmem_limit_bytes=16 * 2**20
        ),
    )(
        *(
            pltpu.with_memory_space_constraint(x, pltpu.HBM)
            for x in (live_dates, day_of_year, by_band, clear_sky, ref_quantile)
        )
    )
    return jnp.transpose(residual, (1, 0, 2))


def solution(mesh):
    return jax.shard_map(
        functools.partial(per_device, mesh.shape["date"], mesh.shape["space"]),
        mesh=mesh,
        in_specs=(
            P("date", None, ("tiles", "space")),
            P("date", ("tiles", "space")),
            P(),
            P(),
            P(),
        ),
        out_specs=P("date", None, ("tiles", "space")),
        check_vma=False,
    )
```

```python
import functools
import math

import jax
import jax.numpy as jnp
from jax import lax
from jax.experimental import pallas as pl
from jax.experimental.pallas import tpu as pltpu
from jax.sharding import PartitionSpec as P

MESH = pl.DeviceIdType.MESH
HARMONICS = 7
RIDGE = 1.0
YEAR = 365
LOW = 16
LANES = 128
SUBLANES = 8


def iota(shape, dim):
    return lax.broadcasted_iota(jnp.int32, shape, dim)


def rounded(x):
    return x.astype(jnp.bfloat16).astype(jnp.float32)


def three_parts(x):
    first = x.astype(jnp.bfloat16)
    rest = x - first.astype(jnp.float32)
    second = rest.astype(jnp.bfloat16)
    return first, second, (rest - second.astype(jnp.float32)).astype(jnp.bfloat16)


def block_histogram(values, valid, bands, bins):
    high_count = bins // LOW
    pixels = values.shape[1]
    position = jnp.clip(bins * values - 0.5, 0.0, bins - 1.0)
    high = jnp.floor(position * (1.0 / LOW))
    local = position - LOW * high
    marked = jnp.where(valid, high, -1.0)
    high_iota = iota((high_count, pixels), 0).astype(jnp.float32)
    low_iota = iota((LOW, pixels), 0).astype(jnp.float32)
    hot, tents = [], []
    for b in range(bands):
        hot.append(jnp.where(high_iota == marked[b : b + 1], 1.0, 0.0).astype(jnp.bfloat16))
        tents.append(
            jnp.maximum(0.0, 1.0 - jnp.abs(local[b : b + 1] - low_iota)).astype(jnp.bfloat16)
        )
    spill = jnp.maximum(0.0, 1.0 - jnp.abs(local - LOW))
    tents.append(jnp.concatenate([spill, jnp.zeros_like(spill)], axis=0).astype(jnp.bfloat16))
    hot.append(jnp.zeros((LANES - bands * high_count, pixels), jnp.bfloat16))
    counts = lax.dot_general(
        jnp.concatenate(tents, axis=0),
        jnp.concatenate(hot, axis=0),
        (((1,), (1,)), ((), ())),
        preferred_element_type=jnp.float32,
    )
    band_lane = iota((LOW, LANES), 1) // high_count
    inner = jnp.zeros((LOW, LANES), jnp.float32)
    for b in range(bands):
        inner += jnp.where(band_lane == b, counts[b * LOW : (b + 1) * LOW], 0.0)
    outer = counts[bands * LOW : bands * LOW + SUBLANES]
    own = iota((SUBLANES, LANES), 0) == band_lane[:SUBLANES]
    return inner, jnp.sum(jnp.where(own, outer, 0.0), axis=0, keepdims=True)


def running_sums(inner, spill, bands, bins):
    high_count = bins // LOW
    dates = len(inner)
    used = bands * high_count
    column = [jnp.sum(inner[d], axis=0, keepdims=True) + spill[d] for d in range(dates)]
    rows = column + spill
    left = jnp.zeros((SUBLANES, LANES), jnp.float32)
    row_of = iota((SUBLANES, LANES), 0)
    for i, row in enumerate(rows):
        left = jnp.where(row_of == i, row, left)
    src, dst = iota((LANES, LANES), 0), iota((LANES, LANES), 1)
    same = (src // high_count == dst // high_count) & (dst < used)
    before = jnp.where((same & (src < dst)) | (dst == used + src // high_count), 1.0, 0.0)
    shift = jnp.where(same & (src + 1 == dst), 0.5, 0.0)
    before = jnp.where(src < used, before, 0.0)
    shift = jnp.where(src < used, shift, 0.0)
    parts = [part.astype(jnp.float32) for part in three_parts(left)] + [jnp.zeros_like(left)]
    moved = jnp.dot(
        jnp.concatenate(parts, axis=0).astype(jnp.bfloat16),
        jnp.concatenate([before, shift], axis=1).astype(jnp.bfloat16),
        preferred_element_type=jnp.float32,
    )
    moved = sum(moved[i * SUBLANES : (i + 1) * SUBLANES] for i in range(3))
    out_row, in_row = iota((LOW, 3 * LOW), 0), iota((LOW, 3 * LOW), 1) % LOW
    lower = jnp.where(in_row < out_row, 1.0, jnp.where(in_row == out_row, 0.5, 0.0))
    within = jnp.dot(
        lower.astype(jnp.bfloat16),
        jnp.concatenate(three_parts(jnp.concatenate(inner, axis=1)), axis=0),
        preferred_element_type=jnp.float32,
    )
    first = iota((LOW, LANES), 0) == 0
    sums = []
    for d in range(dates):
        part = within[:, d * LANES : (d + 1) * LANES] + moved[d : d + 1, :LANES]
        back = moved[dates + d : dates + d + 1, LANES:]
        sums.append(part - jnp.where(first, back, 0.0))
    return sums


def flat_table(sums, bands, bins):
    high_count = bins // LOW
    used = bands * high_count
    lane = iota((SUBLANES, LANES), 1)
    total_lane = jnp.minimum(used + lane // high_count, LANES - 1)
    total = jnp.take_along_axis(sums[:SUBLANES], total_lane, axis=1)[:1]
    cumulative = (sums / jnp.maximum(total, 1.0)).astype(jnp.bfloat16).astype(jnp.float32)
    band_lane = iota((LOW, LANES), 1) // high_count
    wide = jnp.concatenate(
        [jnp.where(band_lane == b, cumulative, 0.0) for b in range(bands)], axis=0
    ).astype(jnp.bfloat16)
    src, dst = iota((LANES, bins), 0), iota((LANES, bins), 1)
    spread = jnp.where((src % high_count == dst // LOW) & (src < used), 1.0, 0.0).astype(
        jnp.bfloat16
    )
    placed = jnp.dot(wide, spread, preferred_element_type=jnp.float32)
    rows, cols = iota(placed.shape, 0), iota(placed.shape, 1)
    placed = jnp.where(rows % LOW == cols % LOW, placed, 0.0).astype(jnp.bfloat16)
    pick = jnp.where(
        iota((SUBLANES, bands * LOW), 1) // LOW == iota((SUBLANES, bands * LOW), 0), 1.0, 0.0
    ).astype(jnp.bfloat16)
    return jnp.dot(pick, placed, preferred_element_type=jnp.float32)


def gather_lanes(table, index):
    parts = table.shape[1] // LANES
    inner = index % LANES
    out = jnp.take_along_axis(table[:, :LANES], inner, axis=1)
    for part in range(1, parts):
        other = jnp.take_along_axis(table[:, part * LANES : (part + 1) * LANES], inner, axis=1)
        out = jnp.where(index >= part * LANES, other, out)
    return out


def interpolate(table, position, bins):
    low = jnp.floor(position)
    first = low.astype(jnp.int32)
    second = jnp.minimum(first + 1, bins - 1)
    low_weight = rounded(1.0 - jnp.abs(position - low))
    high_weight = rounded(jnp.maximum(0.0, 1.0 - jnp.abs(position - (low + 1.0))))
    return low_weight * gather_lanes(table, first) + high_weight * gather_lanes(table, second)


def own_fit_rows(live_ref, day_ref, date_slots, dates, first_date):
    size = max(dates, SUBLANES)
    rows, cols = iota((size, size), 0), iota((size, size), 1)

    def place(t, carry):
        day_r, day_c, live_r, live_c = carry
        day = day_ref[t]
        live = (lax.rem(t, date_slots) < live_ref[lax.div(t, date_slots)]).astype(jnp.int32)
        return (
            jnp.where(rows == t, day, day_r),
            jnp.where(cols == t, day, day_c),
            jnp.where(rows == t, live, live_r),
            jnp.where(cols == t, live, live_c),
        )

    zero = jnp.zeros((size, size), jnp.int32)
    day_r, day_c, live_r, live_c = lax.fori_loop(
        0, dates, place, (zero, zero, zero, zero), unroll=dates <= 16
    )
    base = jnp.cos((2.0 * math.pi / YEAR) * (day_r - day_c).astype(jnp.float32))
    older, newer = jnp.ones_like(base), base
    total = older + newer
    for _ in range(HARMONICS - 1):
        older, newer = newer, 2.0 * base * newer - older
        total = total + newer
    eye = jnp.where(rows == cols, 1.0, 0.0)
    work = jnp.where((live_r * live_c) == 1, total, 0.0) + RIDGE * eye
    inverse = eye
    for k in range(dates):
        pivot = work[k : k + 1, k : k + 1]
        row_w, row_i = work[k : k + 1, :] / pivot, inverse[k : k + 1, :] / pivot
        column = work[:, k : k + 1]
        work = jnp.where(rows == k, row_w, work - column * row_w)
        inverse = jnp.where(rows == k, row_i, inverse - column * row_i)
    return [
        jnp.sum(jnp.where(rows == first_date + d, inverse, 0.0), axis=0, keepdims=True)
        for d in range(date_slots)
    ]


def kernel(
    groups,
    spaces,
    early,
    live_hbm,
    day_hbm,
    reflect_hbm,
    clear_hbm,
    quantile_hbm,
    out_ref,
    live_ref,
    day_ref,
    reflect_ref,
    clear_ref,
    quantile_ref,
    in_sems,
    padded,
    quant,
    hist_own,
    hist_all,
    mask_all,
    raw_all,
    table_all,
    early_all,
    late_all,
    hist_send,
    hist_recv,
    mask_send,
    mask_recv,
    raw_send,
    raw_recv,
    table_send,
    table_recv,
    late_send,
    late_recv,
):
    bands, date_slots, pixels = reflect_ref.shape
    bins = quantile_ref.shape[1]
    dates = date_slots * groups
    my_date, my_space = lax.axis_index("date"), lax.axis_index("space")
    space_peers = [lax.rem(my_space + i, spaces) for i in range(1, spaces)]

    def each_date_peer(body):
        def step(i, carry):
            body(lax.rem(my_date + i, groups))
            return carry

        if groups <= 8:
            for i in range(1, groups):
                step(i, 0)
        else:
            lax.fori_loop(1, groups, step, 0)

    def to_date(src, dst, send, recv, peer):
        return pltpu.make_async_remote_copy(
            src_ref=src,
            dst_ref=dst,
            send_sem=send,
            recv_sem=recv,
            device_id={"date": peer},
            device_id_type=MESH,
        )

    def mask_copy(peer, slot):
        return to_date(
            mask_all.at[slot], mask_all.at[slot], mask_send.at[peer], mask_recv.at[slot], peer
        )

    def raw_copy(peer, slot):
        return to_date(
            raw_all.at[slot], raw_all.at[slot], raw_send.at[peer], raw_recv.at[slot], peer
        )

    def table_copy(peer, slot):
        return to_date(
            table_all.at[slot], table_all.at[slot], table_send.at[peer], table_recv.at[slot], peer
        )

    def late_copy(peer, slot, d):
        return to_date(
            late_all.at[slot, d],
            late_all.at[slot, d],
            late_send.at[peer, d],
            late_recv.at[slot, d],
            peer,
        )

    barrier = pltpu.get_barrier_semaphore()
    for peer in space_peers:
        pl.semaphore_signal(barrier, inc=1, device_id={"space": peer}, device_id_type=MESH)
    each_date_peer(
        lambda peer: pl.semaphore_signal(
            barrier, inc=1, device_id={"date": peer}, device_id_type=MESH
        )
    )

    loads = [
        pltpu.make_async_copy(src, dst, in_sems.at[i])
        for i, (src, dst) in enumerate(
            (
                (reflect_hbm, reflect_ref),
                (clear_hbm, clear_ref),
                (live_hbm, live_ref),
                (day_hbm, day_ref),
                (quantile_hbm, quantile_ref),
            )
        )
    ]
    for load in loads:
        load.start()
    padded[...] = jnp.zeros_like(padded)
    quant[...] = jnp.zeros_like(quant)
    for load in loads:
        load.wait()
    for b in range(bands):
        for d in range(date_slots):
            row = reflect_ref[b, d : d + 1, :]
            padded[d, b : b + 1, :] = row
            if d < early:
                raw_all[my_date, d, b : b + 1, :] = row
    quant[:bands] = rounded(quantile_ref[...])

    inner, spill = [], []
    for d in range(date_slots):
        live = lax.rem(jnp.int32(d), date_slots) < live_ref[my_date]
        valid = clear_ref[d : d + 1, :] * live.astype(jnp.int32)
        mask_all[my_date, d : d + 1, :] = valid.astype(jnp.float32)
        block, extra = block_histogram(
            padded[d], jnp.broadcast_to(valid, (SUBLANES, pixels)) == 1, bands, bins
        )
        inner.append(block)
        spill.append(extra)
    sums = running_sums(inner, spill, bands, bins)
    for d in range(date_slots):
        hist_own[d] = sums[d]

    pl.semaphore_wait(barrier, groups + spaces - 2)

    hist_copies = []
    for peer in space_peers:
        copy = pltpu.make_async_remote_copy(
            src_ref=hist_own,
            dst_ref=hist_all.at[my_space],
            send_sem=hist_send.at[peer],
            recv_sem=hist_recv.at[my_space],
            device_id={"space": peer},
            device_id_type=MESH,
        )
        copy.start()
        hist_copies.append(copy)
    each_date_peer(lambda peer: raw_copy(peer, my_date).start())
    each_date_peer(lambda peer: mask_copy(peer, my_date).start())

    fit_rows = own_fit_rows(live_ref, day_ref, date_slots, dates, my_date * date_slots)

    total = [hist_own[d] for d in range(date_slots)]
    for peer in space_peers:
        pltpu.make_async_remote_copy(
            src_ref=hist_own,
            dst_ref=hist_all.at[peer],
            send_sem=hist_send.at[peer],
            recv_sem=hist_recv.at[peer],
            device_id={"space": peer},
            device_id_type=MESH,
        ).wait_recv()
        for d in range(date_slots):
            total[d] = total[d] + hist_all[peer, d]

    tables = [flat_table(total[d], bands, bins) for d in range(date_slots)]
    for d in range(early):
        table_all[my_date, d] = tables[d]
    each_date_peer(lambda peer: table_copy(peer, my_date).start())

    def match(table, values):
        position = jnp.clip(bins * values - 0.5, 0.0, bins - 1.0)
        level = interpolate(table, position, bins)
        level = jnp.clip(bins * level - 0.5, 0.0, bins - 1.0)
        return interpolate(quant[...], level, bins)[:bands]

    def match_early(slot):
        for d in range(early):
            for start in range(0, pixels, LANES):
                span = slice(start, start + LANES)
                matched = match(table_all[slot, d], padded[d, :, span])
                early_all[slot, d, :, span] = matched * mask_all[slot, d : d + 1, span]

    for d in range(early, date_slots):
        for start in range(0, pixels, LANES):
            span = slice(start, start + LANES)
            matched = match(tables[d], padded[d, :, span])
            late_all[my_date, d - early, :, span] = matched * mask_all[my_date, d : d + 1, span]
        each_date_peer(lambda peer: late_copy(peer, my_date, d - early).start())

    match_early(my_date)

    def arrived(peer):
        mask_copy(peer, peer).wait_recv()
        raw_copy(peer, peer).wait_recv()
        table_copy(peer, peer).wait_recv()
        for d in range(early):
            padded[d, :bands] = raw_all[peer, d]
        match_early(peer)

    each_date_peer(arrived)

    count = jnp.zeros((1, pixels), jnp.float32)
    summed = jnp.zeros((bands, pixels), jnp.float32)
    gaps = [jnp.zeros((1, pixels), jnp.float32) for _ in range(date_slots)]
    fits = [jnp.zeros((bands, pixels), jnp.float32) for _ in range(date_slots)]
    for g in range(groups):
        for s in range(date_slots):
            t = g * date_slots + s
            mask = mask_all[g, s : s + 1, :]
            count += mask
            for d in range(date_slots):
                gaps[d] += fit_rows[d][:, t : t + 1] * (1.0 - mask)
            if s < early:
                series = early_all[g, s]
                summed += series
                for d in range(date_slots):
                    fits[d] += fit_rows[d][:, t : t + 1] * series
    share = 1.0 / jnp.maximum(count, 1.0)

    def late_arrived(peer):
        for d in range(date_slots - early):
            late_copy(peer, peer, d).wait_recv()

    each_date_peer(late_arrived)
    for g in range(groups):
        for s in range(early, date_slots):
            t = g * date_slots + s
            series = late_all[g, s - early]
            summed += series
            for d in range(date_slots):
                fits[d] += fit_rows[d][:, t : t + 1] * series
    mean = summed * share
    for d in range(date_slots):
        left = mask_all[my_date, d : d + 1, :] * (fits[d] + gaps[d] * mean)
        for b in range(bands):
            out_ref[b, d : d + 1, :] = left[b : b + 1]

    for copy in hist_copies:
        copy.wait_send()

    def sent(peer):
        raw_copy(peer, my_date).wait_send()
        mask_copy(peer, my_date).wait_send()
        table_copy(peer, my_date).wait_send()
        for d in range(date_slots - early):
            late_copy(peer, my_date, d).wait_send()

    each_date_peer(sent)


def per_device(groups, spaces, reflect, clear_sky, live_dates, day_of_year, ref_quantile):
    date_slots, bands, pixels = reflect.shape
    bins = ref_quantile.shape[1]
    early = max(1, date_slots // 2)
    by_band = jnp.transpose(reflect, (1, 0, 2))
    residual = pl.pallas_call(
        functools.partial(kernel, groups, spaces, early),
        out_shape=jax.ShapeDtypeStruct(by_band.shape, jnp.float32),
        in_specs=[pl.BlockSpec(memory_space=pltpu.HBM)] * 5,
        out_specs=pl.BlockSpec(memory_space=pltpu.VMEM),
        scratch_shapes=[
            pltpu.SMEM(live_dates.shape, jnp.int32),
            pltpu.SMEM(day_of_year.shape, jnp.int32),
            pltpu.VMEM(by_band.shape, jnp.float32),
            pltpu.VMEM(clear_sky.shape, jnp.int32),
            pltpu.VMEM(ref_quantile.shape, jnp.float32),
            pltpu.SemaphoreType.DMA((5,)),
            pltpu.VMEM((date_slots, SUBLANES, pixels), jnp.float32),
            pltpu.VMEM((SUBLANES, bins), jnp.float32),
            pltpu.VMEM((date_slots, LOW, LANES), jnp.float32),
            pltpu.VMEM((spaces, date_slots, LOW, LANES), jnp.float32),
            pltpu.VMEM((groups, date_slots, pixels), jnp.float32),
            pltpu.VMEM((groups, early, bands, pixels), jnp.float32),
            pltpu.VMEM((groups, early, SUBLANES, bins), jnp.float32),
            pltpu.VMEM((groups, early, bands, pixels), jnp.float32),
            pltpu.VMEM((groups, date_slots - early, bands, pixels), jnp.float32),
            pltpu.SemaphoreType.DMA((spaces,)),
            pltpu.SemaphoreType.DMA((spaces,)),
            pltpu.SemaphoreType.DMA((groups,)),
            pltpu.SemaphoreType.DMA((groups,)),
            pltpu.SemaphoreType.DMA((groups,)),
            pltpu.SemaphoreType.DMA((groups,)),
            pltpu.SemaphoreType.DMA((groups,)),
            pltpu.SemaphoreType.DMA((groups,)),
            pltpu.SemaphoreType.DMA((groups, date_slots - early)),
            pltpu.SemaphoreType.DMA((groups, date_slots - early)),
        ],
        compiler_params=pltpu.CompilerParams(
            collective_id=0, has_side_effects=True, vmem_limit_bytes=16 * 2**20
        ),
    )(
        *(
            pltpu.with_memory_space_constraint(x, pltpu.HBM)
            for x in (live_dates, day_of_year, by_band, clear_sky, ref_quantile)
        )
    )
    return jnp.transpose(residual, (1, 0, 2))


def solution(mesh):
    return jax.shard_map(
        functools.partial(per_device, mesh.shape["date"], mesh.shape["space"]),
        mesh=mesh,
        in_specs=(
            P("date", None, ("tiles", "space")),
            P("date", ("tiles", "space")),
            P(),
            P(),
            P(),
        ),
        out_specs=P("date", None, ("tiles", "space")),
        check_vma=False,
    )
```

```python
import functools
import math

import jax
import jax.numpy as jnp
from jax import lax
from jax.experimental import pallas as pl
from jax.experimental.pallas import tpu as pltpu
from jax.sharding import PartitionSpec as P

MESH = pl.DeviceIdType.MESH
HARMONICS = 7
RIDGE = 1.0
YEAR = 365
LOW = 16
LANES = 128
SUBLANES = 8


def iota(shape, dim):
    return lax.broadcasted_iota(jnp.int32, shape, dim)


def rounded(x):
    return x.astype(jnp.bfloat16).astype(jnp.float32)


def three_parts(x):
    first = x.astype(jnp.bfloat16)
    rest = x - first.astype(jnp.float32)
    second = rest.astype(jnp.bfloat16)
    return first, second, (rest - second.astype(jnp.float32)).astype(jnp.bfloat16)


def row_slot_band(row, bands):
    whole = SUBLANES - bands
    slot = (row >= bands).astype(jnp.int32)
    band = jnp.where(
        row < bands, row, jnp.where(row < SUBLANES, row - bands + (bands - whole), row - SUBLANES)
    )
    return slot, band


def find_row(slot, band, bands):
    rest = 2 * bands - SUBLANES
    if slot == 0:
        return 0, band
    return (1, band) if band < rest else (0, bands + band - rest)


def block_histograms(values, valid, bands, bins):
    high_count = bins // LOW
    pixels = values[0].shape[1]
    high_iota = iota((high_count, pixels), 0).astype(jnp.float32)
    low_iota = iota((LOW, pixels), 0).astype(jnp.float32)
    marked, local, spill = [], [], []
    for group in range(2):
        position = jnp.clip(bins * values[group] - 0.5, 0.0, bins - 1.0)
        high = jnp.floor(position * (1.0 / LOW))
        local.append(position - LOW * high)
        marked.append(jnp.where(valid[group] > 0.5, high, -1.0))
        spill.append(jnp.maximum(0.0, 1.0 - jnp.abs(local[group] - LOW)))
    spill = jnp.concatenate(spill, axis=0).astype(jnp.bfloat16)
    band_lane = iota((LOW, LANES), 1) // high_count
    row_slot, row_band = row_slot_band(iota((2 * SUBLANES, LANES), 0), bands)
    own_lane = iota((2 * SUBLANES, LANES), 1) // high_count
    inners, outers = [], []
    for slot in range(2):
        hot, tents = [], []
        for band in range(bands):
            group, row = find_row(slot, band, bands)
            one = marked[group][row : row + 1]
            hot.append(jnp.where(high_iota == one, 1.0, 0.0).astype(jnp.bfloat16))
            near = 1.0 - jnp.abs(local[group][row : row + 1] - low_iota)
            tents.append(jnp.maximum(0.0, near).astype(jnp.bfloat16))
        hot.append(jnp.zeros((LANES - bands * high_count, pixels), jnp.bfloat16))
        counts = lax.dot_general(
            jnp.concatenate(tents + [spill], axis=0),
            jnp.concatenate(hot, axis=0),
            (((1,), (1,)), ((), ())),
            preferred_element_type=jnp.float32,
        )
        inner = jnp.zeros((LOW, LANES), jnp.float32)
        for band in range(bands):
            inner += jnp.where(band_lane == band, counts[band * LOW : (band + 1) * LOW], 0.0)
        own = (row_slot == slot) & (row_band == own_lane)
        outer = jnp.where(own, counts[bands * LOW : bands * LOW + 2 * SUBLANES], 0.0)
        inners.append(inner)
        outers.append(jnp.sum(outer, axis=0, keepdims=True))
    return inners, outers


def running_sums(inner, spill, bands, bins):
    high_count = bins // LOW
    dates = len(inner)
    used = bands * high_count
    column = [jnp.sum(inner[d], axis=0, keepdims=True) + spill[d] for d in range(dates)]
    rows = column + spill
    left = jnp.zeros((SUBLANES, LANES), jnp.float32)
    row_of = iota((SUBLANES, LANES), 0)
    for i, row in enumerate(rows):
        left = jnp.where(row_of == i, row, left)
    src, dst = iota((LANES, LANES), 0), iota((LANES, LANES), 1)
    same = (src // high_count == dst // high_count) & (dst < used)
    before = jnp.where((same & (src < dst)) | (dst == used + src // high_count), 1.0, 0.0)
    shift = jnp.where(same & (src + 1 == dst), 0.5, 0.0)
    before = jnp.where(src < used, before, 0.0)
    shift = jnp.where(src < used, shift, 0.0)
    parts = [part.astype(jnp.float32) for part in three_parts(left)] + [jnp.zeros_like(left)]
    moved = jnp.dot(
        jnp.concatenate(parts, axis=0).astype(jnp.bfloat16),
        jnp.concatenate([before, shift], axis=1).astype(jnp.bfloat16),
        preferred_element_type=jnp.float32,
    )
    moved = sum(moved[i * SUBLANES : (i + 1) * SUBLANES] for i in range(3))
    out_row, in_row = iota((LOW, 3 * LOW), 0), iota((LOW, 3 * LOW), 1) % LOW
    lower = jnp.where(in_row < out_row, 1.0, jnp.where(in_row == out_row, 0.5, 0.0))
    within = jnp.dot(
        lower.astype(jnp.bfloat16),
        jnp.concatenate(three_parts(jnp.concatenate(inner, axis=1)), axis=0),
        preferred_element_type=jnp.float32,
    )
    first = iota((LOW, LANES), 0) == 0
    sums = []
    for d in range(dates):
        part = within[:, d * LANES : (d + 1) * LANES] + moved[d : d + 1, :LANES]
        back = moved[dates + d : dates + d + 1, LANES:]
        sums.append(part - jnp.where(first, back, 0.0))
    return sums


def flat_tables(sums, bands, bins):
    high_count = bins // LOW
    used = bands * high_count
    lane = iota((SUBLANES, LANES), 1)
    total_lane = jnp.minimum(used + lane // high_count, LANES - 1)
    band_lane = iota((LOW, LANES), 1) // high_count
    wide = []
    for part in sums:
        total = jnp.take_along_axis(part[:SUBLANES], total_lane, axis=1)[:1]
        cumulative = (part / jnp.maximum(total, 1.0)).astype(jnp.bfloat16).astype(jnp.float32)
        wide += [jnp.where(band_lane == band, cumulative, 0.0) for band in range(bands)]
    src, dst = iota((LANES, bins), 0), iota((LANES, bins), 1)
    spread = jnp.where((src % high_count == dst // LOW) & (src < used), 1.0, 0.0)
    placed = jnp.dot(
        jnp.concatenate(wide, axis=0).astype(jnp.bfloat16),
        spread.astype(jnp.bfloat16),
        preferred_element_type=jnp.float32,
    )
    rows, cols = iota(placed.shape, 0), iota(placed.shape, 1)
    placed = jnp.where(rows % LOW == cols % LOW, placed, 0.0).astype(jnp.bfloat16)
    shape = (2 * SUBLANES, 2 * bands * LOW)
    slot, band = row_slot_band(iota(shape, 0), bands)
    pick = jnp.where((iota(shape, 1) // LOW == slot * bands + band) & (band < bands), 1.0, 0.0)
    tables = jnp.dot(pick.astype(jnp.bfloat16), placed, preferred_element_type=jnp.float32)
    return tables[:SUBLANES], tables[SUBLANES:]


def gather_lanes(table, index):
    parts = table.shape[1] // LANES
    inner = index % LANES
    out = jnp.take_along_axis(table[:, :LANES], inner, axis=1)
    for part in range(1, parts):
        other = jnp.take_along_axis(table[:, part * LANES : (part + 1) * LANES], inner, axis=1)
        out = jnp.where(index >= part * LANES, other, out)
    return out


def interpolate(table, position, bins):
    low = jnp.floor(position)
    first = low.astype(jnp.int32)
    second = jnp.minimum(first + 1, bins - 1)
    low_weight = rounded(1.0 - jnp.abs(position - low))
    high_weight = rounded(jnp.maximum(0.0, 1.0 - jnp.abs(position - (low + 1.0))))
    return low_weight * gather_lanes(table, first) + high_weight * gather_lanes(table, second)


def own_fit_rows(live_ref, day_ref, date_slots, dates, first_date):
    size = max(dates, SUBLANES)
    rows, cols = iota((size, size), 0), iota((size, size), 1)

    def place(t, carry):
        day_r, day_c, live_r, live_c = carry
        day = day_ref[t]
        live = (lax.rem(t, date_slots) < live_ref[lax.div(t, date_slots)]).astype(jnp.int32)
        return (
            jnp.where(rows == t, day, day_r),
            jnp.where(cols == t, day, day_c),
            jnp.where(rows == t, live, live_r),
            jnp.where(cols == t, live, live_c),
        )

    zero = jnp.zeros((size, size), jnp.int32)
    day_r, day_c, live_r, live_c = lax.fori_loop(
        0, dates, place, (zero, zero, zero, zero), unroll=dates <= 16
    )
    base = jnp.cos((2.0 * math.pi / YEAR) * (day_r - day_c).astype(jnp.float32))
    older, newer = jnp.ones_like(base), base
    total = older + newer
    for _ in range(HARMONICS - 1):
        older, newer = newer, 2.0 * base * newer - older
        total = total + newer
    eye = jnp.where(rows == cols, 1.0, 0.0)
    work = jnp.where((live_r * live_c) == 1, total, 0.0) + RIDGE * eye
    inverse = eye
    for k in range(dates):
        pivot = work[k : k + 1, k : k + 1]
        row_w, row_i = work[k : k + 1, :] / pivot, inverse[k : k + 1, :] / pivot
        column = work[:, k : k + 1]
        work = jnp.where(rows == k, row_w, work - column * row_w)
        inverse = jnp.where(rows == k, row_i, inverse - column * row_i)
    return [
        jnp.sum(jnp.where(rows == first_date + d, inverse, 0.0), axis=0, keepdims=True)
        for d in range(date_slots)
    ]


def kernel(
    groups,
    spaces,
    live_hbm,
    day_hbm,
    reflect_hbm,
    clear_hbm,
    quantile_hbm,
    out_ref,
    live_ref,
    day_ref,
    reflect_ref,
    clear_ref,
    quantile_ref,
    in_sems,
    late_raw,
    quant,
    hist_own,
    hist_all,
    mask_all,
    raw_all,
    table_all,
    early_all,
    late_all,
    hist_send,
    hist_recv,
    mask_send,
    mask_recv,
    raw_send,
    raw_recv,
    table_send,
    table_recv,
    late_send,
    late_recv,
):
    bands, date_slots, pixels = reflect_ref.shape
    bins = quantile_ref.shape[1]
    dates = date_slots * groups
    rest = 2 * bands - SUBLANES
    my_date, my_space = lax.axis_index("date"), lax.axis_index("space")
    space_peers = [lax.rem(my_space + i, spaces) for i in range(1, spaces)]

    def each_date_peer(body):
        def step(i, carry):
            body(lax.rem(my_date + i, groups))
            return carry

        if groups <= 8:
            for i in range(1, groups):
                step(i, 0)
        else:
            lax.fori_loop(1, groups, step, 0)

    def to_date(src, dst, send, recv, peer):
        return pltpu.make_async_remote_copy(
            src_ref=src,
            dst_ref=dst,
            send_sem=send,
            recv_sem=recv,
            device_id={"date": peer},
            device_id_type=MESH,
        )

    def mask_copy(peer, slot):
        return to_date(
            mask_all.at[slot], mask_all.at[slot], mask_send.at[peer], mask_recv.at[slot], peer
        )

    def raw_copy(peer, slot):
        return to_date(
            raw_all.at[slot], raw_all.at[slot], raw_send.at[peer], raw_recv.at[slot], peer
        )

    def table_copy(peer, slot):
        return to_date(
            table_all.at[slot], table_all.at[slot], table_send.at[peer], table_recv.at[slot], peer
        )

    def late_copy(peer, slot):
        return to_date(
            late_all.at[slot], late_all.at[slot], late_send.at[peer], late_recv.at[slot], peer
        )

    barrier = pltpu.get_barrier_semaphore()
    for peer in space_peers:
        pl.semaphore_signal(barrier, inc=1, device_id={"space": peer}, device_id_type=MESH)
    each_date_peer(
        lambda peer: pl.semaphore_signal(
            barrier, inc=1, device_id={"date": peer}, device_id_type=MESH
        )
    )

    loads = [
        pltpu.make_async_copy(src, dst, in_sems.at[i])
        for i, (src, dst) in enumerate(
            (
                (reflect_hbm, reflect_ref),
                (clear_hbm, clear_ref),
                (live_hbm, live_ref),
                (day_hbm, day_ref),
                (quantile_hbm, quantile_ref),
            )
        )
    ]
    for load in loads:
        load.start()
    late_raw[...] = jnp.zeros_like(late_raw)
    quant[...] = jnp.zeros_like(quant)
    for load in loads:
        load.wait()
    for d in range(date_slots):
        for b in range(bands):
            group, row = find_row(d, b, bands)
            values = reflect_ref[b, d : d + 1, :]
            if group == 0:
                raw_all[my_date, row : row + 1, :] = values
            else:
                late_raw[row : row + 1, :] = values
            quant[group, row : row + 1, :] = rounded(quantile_ref[b : b + 1, :])

    for d in range(date_slots):
        live = lax.rem(jnp.int32(d), date_slots) < live_ref[my_date]
        valid = clear_ref[d : d + 1, :] * live.astype(jnp.int32)
        mask_all[my_date, d : d + 1, :] = valid.astype(jnp.float32)

    def row_mask(slot, span):
        size = span.stop - span.start
        slots, _ = row_slot_band(iota((SUBLANES, size), 0), bands)
        return jnp.where(slots == 0, mask_all[slot, 0:1, span], mask_all[slot, 1:2, span])

    everything = slice(0, pixels)
    inner, spill = block_histograms(
        (raw_all[my_date], late_raw[...]),
        (
            row_mask(my_date, everything),
            jnp.broadcast_to(mask_all[my_date, 1:2, :], (SUBLANES, pixels)),
        ),
        bands,
        bins,
    )
    sums = running_sums(inner, spill, bands, bins)
    for d in range(date_slots):
        hist_own[d] = sums[d]

    pl.semaphore_wait(barrier, groups + spaces - 2)

    hist_copies = []
    for peer in space_peers:
        copy = pltpu.make_async_remote_copy(
            src_ref=hist_own,
            dst_ref=hist_all.at[my_space],
            send_sem=hist_send.at[peer],
            recv_sem=hist_recv.at[my_space],
            device_id={"space": peer},
            device_id_type=MESH,
        )
        copy.start()
        hist_copies.append(copy)
    each_date_peer(lambda peer: raw_copy(peer, my_date).start())
    each_date_peer(lambda peer: mask_copy(peer, my_date).start())

    fit_rows = own_fit_rows(live_ref, day_ref, date_slots, dates, my_date * date_slots)

    total = [hist_own[d] for d in range(date_slots)]
    for peer in space_peers:
        pltpu.make_async_remote_copy(
            src_ref=hist_own,
            dst_ref=hist_all.at[peer],
            send_sem=hist_send.at[peer],
            recv_sem=hist_recv.at[peer],
            device_id={"space": peer},
            device_id_type=MESH,
        ).wait_recv()
        for d in range(date_slots):
            total[d] = total[d] + hist_all[peer, d]

    early_table, late_table = flat_tables(total, bands, bins)
    table_all[my_date] = early_table
    each_date_peer(lambda peer: table_copy(peer, my_date).start())

    def match(table, values, group):
        position = jnp.clip(bins * values - 0.5, 0.0, bins - 1.0)
        level = interpolate(table, position, bins)
        level = jnp.clip(bins * level - 0.5, 0.0, bins - 1.0)
        return interpolate(quant[group], level, bins)

    def match_early(slot):
        for start in range(0, pixels, LANES):
            span = slice(start, start + LANES)
            matched = match(table_all[slot], raw_all[slot, :, span], 0)
            early_all[slot, :, span] = matched * row_mask(slot, span)

    for start in range(0, pixels, LANES):
        span = slice(start, start + LANES)
        matched = match(late_table, late_raw[:, span], 1)[:rest]
        late_all[my_date, :, span] = matched * mask_all[my_date, 1:2, span]
    each_date_peer(lambda peer: late_copy(peer, my_date).start())

    match_early(my_date)

    def arrived(peer):
        mask_copy(peer, peer).wait_recv()
        raw_copy(peer, peer).wait_recv()
        table_copy(peer, peer).wait_recv()
        match_early(peer)

    each_date_peer(arrived)

    row_slot, _ = row_slot_band(iota((SUBLANES, 1), 0), bands)
    count = jnp.zeros((1, pixels), jnp.float32)
    gaps = [jnp.zeros((1, pixels), jnp.float32) for _ in range(date_slots)]
    summed = jnp.zeros((SUBLANES, pixels), jnp.float32)
    fits = [jnp.zeros((SUBLANES, pixels), jnp.float32) for _ in range(date_slots)]
    for g in range(groups):
        series = early_all[g]
        summed += series
        for d in range(date_slots):
            first, second = (fit_rows[d][:, 2 * g + s : 2 * g + s + 1] for s in range(2))
            fits[d] += jnp.where(row_slot == 0, first, second) * series
        for s in range(date_slots):
            mask = mask_all[g, s : s + 1, :]
            count += mask
            for d in range(date_slots):
                gaps[d] += fit_rows[d][:, 2 * g + s : 2 * g + s + 1] * (1.0 - mask)
    share = 1.0 / jnp.maximum(count, 1.0)
    gaps = [gap * share for gap in gaps]

    def finish(d, row, value):
        out_ref[row, d : d + 1, :] = value

    for b in range(rest, bands):
        other = bands + b - rest
        mean = summed[b : b + 1] + summed[other : other + 1]
        for d in range(date_slots):
            fit = fits[d][b : b + 1] + fits[d][other : other + 1] + gaps[d] * mean
            finish(d, b, mask_all[my_date, d : d + 1, :] * fit)

    each_date_peer(lambda peer: late_copy(peer, peer).wait_recv())
    summed = summed[:rest]
    fits = [fit[:rest] for fit in fits]
    for g in range(groups):
        series = late_all[g]
        summed += series
        for d in range(date_slots):
            fits[d] += fit_rows[d][:, 2 * g + 1 : 2 * g + 2] * series
    for d in range(date_slots):
        left = mask_all[my_date, d : d + 1, :] * (fits[d] + gaps[d] * summed)
        for b in range(rest):
            finish(d, b, left[b : b + 1])

    for copy in hist_copies:
        copy.wait_send()

    def sent(peer):
        raw_copy(peer, my_date).wait_send()
        mask_copy(peer, my_date).wait_send()
        table_copy(peer, my_date).wait_send()
        late_copy(peer, my_date).wait_send()

    each_date_peer(sent)


def per_device(groups, spaces, reflect, clear_sky, live_dates, day_of_year, ref_quantile):
    date_slots, bands, pixels = reflect.shape
    bins = ref_quantile.shape[1]
    rest = 2 * bands - SUBLANES
    by_band = jnp.transpose(reflect, (1, 0, 2))
    residual = pl.pallas_call(
        functools.partial(kernel, groups, spaces),
        out_shape=jax.ShapeDtypeStruct(by_band.shape, jnp.float32),
        in_specs=[pl.BlockSpec(memory_space=pltpu.HBM)] * 5,
        out_specs=pl.BlockSpec(memory_space=pltpu.VMEM),
        scratch_shapes=[
            pltpu.SMEM(live_dates.shape, jnp.int32),
            pltpu.SMEM(day_of_year.shape, jnp.int32),
            pltpu.VMEM(by_band.shape, jnp.float32),
            pltpu.VMEM(clear_sky.shape, jnp.int32),
            pltpu.VMEM(ref_quantile.shape, jnp.float32),
            pltpu.SemaphoreType.DMA((5,)),
            pltpu.VMEM((SUBLANES, pixels), jnp.float32),
            pltpu.VMEM((2, SUBLANES, bins), jnp.float32),
            pltpu.VMEM((date_slots, LOW, LANES), jnp.float32),
            pltpu.VMEM((spaces, date_slots, LOW, LANES), jnp.float32),
            pltpu.VMEM((groups, date_slots, pixels), jnp.float32),
            pltpu.VMEM((groups, SUBLANES, pixels), jnp.float32),
            pltpu.VMEM((groups, SUBLANES, bins), jnp.float32),
            pltpu.VMEM((groups, SUBLANES, pixels), jnp.float32),
            pltpu.VMEM((groups, rest, pixels), jnp.float32),
            pltpu.SemaphoreType.DMA((spaces,)),
            pltpu.SemaphoreType.DMA((spaces,)),
            pltpu.SemaphoreType.DMA((groups,)),
            pltpu.SemaphoreType.DMA((groups,)),
            pltpu.SemaphoreType.DMA((groups,)),
            pltpu.SemaphoreType.DMA((groups,)),
            pltpu.SemaphoreType.DMA((groups,)),
            pltpu.SemaphoreType.DMA((groups,)),
            pltpu.SemaphoreType.DMA((groups,)),
            pltpu.SemaphoreType.DMA((groups,)),
        ],
        compiler_params=pltpu.CompilerParams(
            collective_id=0, has_side_effects=True, vmem_limit_bytes=16 * 2**20
        ),
    )(
        *(
            pltpu.with_memory_space_constraint(x, pltpu.HBM)
            for x in (live_dates, day_of_year, by_band, clear_sky, ref_quantile)
        )
    )
    return jnp.transpose(residual, (1, 0, 2))


def solution(mesh):
    return jax.shard_map(
        functools.partial(per_device, mesh.shape["date"], mesh.shape["space"]),
        mesh=mesh,
        in_specs=(
            P("date", None, ("tiles", "space")),
            P("date", ("tiles", "space")),
            P(),
            P(),
            P(),
        ),
        out_specs=P("date", None, ("tiles", "space")),
        check_vma=False,
    )
```

```python
import functools
import math

import jax
import jax.numpy as jnp
from jax import lax
from jax.experimental import pallas as pl
from jax.experimental.pallas import tpu as pltpu
from jax.sharding import PartitionSpec as P

MESH = pl.DeviceIdType.MESH
HARMONICS = 7
RIDGE = 1.0
YEAR = 365
LOW = 16
LANES = 128
SUBLANES = 8


def iota(shape, dim):
    return lax.broadcasted_iota(jnp.int32, shape, dim)


def rounded(x):
    return x.astype(jnp.bfloat16).astype(jnp.float32)


def three_parts(x):
    first = x.astype(jnp.bfloat16)
    rest = x - first.astype(jnp.float32)
    second = rest.astype(jnp.bfloat16)
    return first, second, (rest - second.astype(jnp.float32)).astype(jnp.bfloat16)


def row_slot_band(row, bands):
    whole = SUBLANES - bands
    slot = (row >= bands).astype(jnp.int32)
    band = jnp.where(
        row < bands, row, jnp.where(row < SUBLANES, row - bands + (bands - whole), row - SUBLANES)
    )
    return slot, band


def find_row(slot, band, bands):
    rest = 2 * bands - SUBLANES
    if slot == 0:
        return 0, band
    return (1, band) if band < rest else (0, bands + band - rest)


def block_histograms(values, valid, bands, bins):
    high_count = bins // LOW
    pixels = values[0].shape[1]
    high_iota = iota((high_count, pixels), 0).astype(jnp.float32)
    low_iota = iota((LOW, pixels), 0).astype(jnp.float32)
    marked, local, spill = [], [], []
    for group in range(2):
        position = jnp.clip(bins * values[group] - 0.5, 0.0, bins - 1.0)
        high = jnp.floor(position * (1.0 / LOW))
        local.append(position - LOW * high)
        marked.append(jnp.where(valid[group] > 0.5, high, -1.0))
        spill.append(jnp.maximum(0.0, 1.0 - jnp.abs(local[group] - LOW)))
    spill = jnp.concatenate(spill, axis=0).astype(jnp.bfloat16)
    band_lane = iota((LOW, LANES), 1) // high_count
    row_slot, row_band = row_slot_band(iota((2 * SUBLANES, LANES), 0), bands)
    own_lane = iota((2 * SUBLANES, LANES), 1) // high_count
    inners, outers = [], []
    for slot in range(2):
        hot, tents = [], []
        for band in range(bands):
            group, row = find_row(slot, band, bands)
            one = marked[group][row : row + 1]
            hot.append(jnp.where(high_iota == one, 1.0, 0.0).astype(jnp.bfloat16))
            near = 1.0 - jnp.abs(local[group][row : row + 1] - low_iota)
            tents.append(jnp.maximum(0.0, near).astype(jnp.bfloat16))
        hot.append(jnp.zeros((LANES - bands * high_count, pixels), jnp.bfloat16))
        counts = lax.dot_general(
            jnp.concatenate(tents + [spill], axis=0),
            jnp.concatenate(hot, axis=0),
            (((1,), (1,)), ((), ())),
            preferred_element_type=jnp.float32,
        )
        inner = jnp.zeros((LOW, LANES), jnp.float32)
        for band in range(bands):
            inner += jnp.where(band_lane == band, counts[band * LOW : (band + 1) * LOW], 0.0)
        own = (row_slot == slot) & (row_band == own_lane)
        outer = jnp.where(own, counts[bands * LOW : bands * LOW + 2 * SUBLANES], 0.0)
        inners.append(inner)
        outers.append(jnp.sum(outer, axis=0, keepdims=True))
    return inners, outers


def running_sums(inner, spill, bands, bins):
    high_count = bins // LOW
    dates = len(inner)
    used = bands * high_count
    column = [jnp.sum(inner[d], axis=0, keepdims=True) + spill[d] for d in range(dates)]
    rows = column + spill
    left = jnp.zeros((SUBLANES, LANES), jnp.float32)
    row_of = iota((SUBLANES, LANES), 0)
    for i, row in enumerate(rows):
        left = jnp.where(row_of == i, row, left)
    src, dst = iota((LANES, LANES), 0), iota((LANES, LANES), 1)
    same = (src // high_count == dst // high_count) & (dst < used)
    before = jnp.where((same & (src < dst)) | (dst == used + src // high_count), 1.0, 0.0)
    shift = jnp.where(same & (src + 1 == dst), 0.5, 0.0)
    before = jnp.where(src < used, before, 0.0)
    shift = jnp.where(src < used, shift, 0.0)
    parts = [part.astype(jnp.float32) for part in three_parts(left)] + [jnp.zeros_like(left)]
    moved = jnp.dot(
        jnp.concatenate(parts, axis=0).astype(jnp.bfloat16),
        jnp.concatenate([before, shift], axis=1).astype(jnp.bfloat16),
        preferred_element_type=jnp.float32,
    )
    moved = sum(moved[i * SUBLANES : (i + 1) * SUBLANES] for i in range(3))
    out_row, in_row = iota((LOW, 3 * LOW), 0), iota((LOW, 3 * LOW), 1) % LOW
    lower = jnp.where(in_row < out_row, 1.0, jnp.where(in_row == out_row, 0.5, 0.0))
    within = jnp.dot(
        lower.astype(jnp.bfloat16),
        jnp.concatenate(three_parts(jnp.concatenate(inner, axis=1)), axis=0),
        preferred_element_type=jnp.float32,
    )
    first = iota((LOW, LANES), 0) == 0
    sums = []
    for d in range(dates):
        part = within[:, d * LANES : (d + 1) * LANES] + moved[d : d + 1, :LANES]
        back = moved[dates + d : dates + d + 1, LANES:]
        sums.append(part - jnp.where(first, back, 0.0))
    return sums


def flat_tables(sums, bands, bins):
    high_count = bins // LOW
    used = bands * high_count
    lane = iota((SUBLANES, LANES), 1)
    total_lane = jnp.minimum(used + lane // high_count, LANES - 1)
    band_lane = iota((LOW, LANES), 1) // high_count
    wide = []
    for part in sums:
        total = jnp.take_along_axis(part[:SUBLANES], total_lane, axis=1)[:1]
        cumulative = (part / jnp.maximum(total, 1.0)).astype(jnp.bfloat16).astype(jnp.float32)
        wide += [jnp.where(band_lane == band, cumulative, 0.0) for band in range(bands)]
    src, dst = iota((LANES, bins), 0), iota((LANES, bins), 1)
    spread = jnp.where((src % high_count == dst // LOW) & (src < used), 1.0, 0.0)
    placed = jnp.dot(
        jnp.concatenate(wide, axis=0).astype(jnp.bfloat16),
        spread.astype(jnp.bfloat16),
        preferred_element_type=jnp.float32,
    )
    rows, cols = iota(placed.shape, 0), iota(placed.shape, 1)
    placed = jnp.where(rows % LOW == cols % LOW, placed, 0.0).astype(jnp.bfloat16)
    shape = (2 * SUBLANES, 2 * bands * LOW)
    slot, band = row_slot_band(iota(shape, 0), bands)
    pick = jnp.where((iota(shape, 1) // LOW == slot * bands + band) & (band < bands), 1.0, 0.0)
    tables = jnp.dot(pick.astype(jnp.bfloat16), placed, preferred_element_type=jnp.float32)
    return tables[:SUBLANES], tables[SUBLANES:]


def gather_lanes(table, index):
    parts = table.shape[1] // LANES
    inner = index % LANES
    out = jnp.take_along_axis(table[:, :LANES], inner, axis=1)
    for part in range(1, parts):
        other = jnp.take_along_axis(table[:, part * LANES : (part + 1) * LANES], inner, axis=1)
        out = jnp.where(index >= part * LANES, other, out)
    return out


def interpolate(table, position, bins):
    low = jnp.floor(position)
    first = low.astype(jnp.int32)
    second = jnp.minimum(first + 1, bins - 1)
    low_weight = rounded(1.0 - jnp.abs(position - low))
    high_weight = rounded(jnp.maximum(0.0, 1.0 - jnp.abs(position - (low + 1.0))))
    return low_weight * gather_lanes(table, first) + high_weight * gather_lanes(table, second)


def own_fit_rows(live_ref, day_ref, date_slots, dates, first_date):
    size = max(dates, SUBLANES)
    rows, cols = iota((size, size), 0), iota((size, size), 1)

    def place(t, carry):
        day_r, day_c, live_r, live_c = carry
        day = day_ref[t]
        live = (lax.rem(t, date_slots) < live_ref[lax.div(t, date_slots)]).astype(jnp.int32)
        return (
            jnp.where(rows == t, day, day_r),
            jnp.where(cols == t, day, day_c),
            jnp.where(rows == t, live, live_r),
            jnp.where(cols == t, live, live_c),
        )

    zero = jnp.zeros((size, size), jnp.int32)
    day_r, day_c, live_r, live_c = lax.fori_loop(
        0, dates, place, (zero, zero, zero, zero), unroll=dates <= 16
    )
    base = jnp.cos((2.0 * math.pi / YEAR) * (day_r - day_c).astype(jnp.float32))
    older, newer = jnp.ones_like(base), base
    total = older + newer
    for _ in range(HARMONICS - 1):
        older, newer = newer, 2.0 * base * newer - older
        total = total + newer
    eye = jnp.where(rows == cols, 1.0, 0.0)
    work = jnp.where((live_r * live_c) == 1, total, 0.0) + RIDGE * eye
    inverse = eye
    for k in range(dates):
        pivot = work[k : k + 1, k : k + 1]
        row_w, row_i = work[k : k + 1, :] / pivot, inverse[k : k + 1, :] / pivot
        column = work[:, k : k + 1]
        work = jnp.where(rows == k, row_w, work - column * row_w)
        inverse = jnp.where(rows == k, row_i, inverse - column * row_i)
    return [
        jnp.sum(jnp.where(rows == first_date + d, inverse, 0.0), axis=0, keepdims=True)
        for d in range(date_slots)
    ]


def kernel(
    groups,
    spaces,
    live_hbm,
    day_hbm,
    reflect_hbm,
    clear_hbm,
    quantile_hbm,
    out_ref,
    live_ref,
    day_ref,
    reflect_ref,
    clear_ref,
    quantile_ref,
    in_sems,
    late_raw,
    quant,
    hist_own,
    hist_all,
    mask_all,
    raw_all,
    table_all,
    early_all,
    late_all,
    hist_send,
    hist_recv,
    mask_send,
    mask_recv,
    raw_send,
    raw_recv,
    table_send,
    table_recv,
    late_send,
    late_recv,
):
    bands, date_slots, pixels = reflect_ref.shape
    bins = quantile_ref.shape[1]
    dates = date_slots * groups
    rest = 2 * bands - SUBLANES
    my_date, my_space = lax.axis_index("date"), lax.axis_index("space")
    space_peers = [lax.rem(my_space + i, spaces) for i in range(1, spaces)]

    def each_date_peer(body):
        def step(i, carry):
            body(lax.rem(my_date + i, groups))
            return carry

        if groups <= 8:
            for i in range(1, groups):
                step(i, 0)
        else:
            lax.fori_loop(1, groups, step, 0)

    def to_date(src, dst, send, recv, peer):
        return pltpu.make_async_remote_copy(
            src_ref=src,
            dst_ref=dst,
            send_sem=send,
            recv_sem=recv,
            device_id={"date": peer},
            device_id_type=MESH,
        )

    def mask_copy(peer, slot):
        return to_date(
            mask_all.at[slot], mask_all.at[slot], mask_send.at[peer], mask_recv.at[slot], peer
        )

    def raw_copy(peer, slot):
        return to_date(
            raw_all.at[slot], raw_all.at[slot], raw_send.at[peer], raw_recv.at[slot], peer
        )

    def table_copy(peer, slot):
        return to_date(
            table_all.at[slot], table_all.at[slot], table_send.at[peer], table_recv.at[slot], peer
        )

    def late_copy(peer, slot):
        return to_date(
            late_all.at[slot], late_all.at[slot], late_send.at[peer], late_recv.at[slot], peer
        )

    barrier = pltpu.get_barrier_semaphore()
    for peer in space_peers:
        pl.semaphore_signal(barrier, inc=1, device_id={"space": peer}, device_id_type=MESH)
    each_date_peer(
        lambda peer: pl.semaphore_signal(
            barrier, inc=1, device_id={"date": peer}, device_id_type=MESH
        )
    )

    loads = [
        pltpu.make_async_copy(src, dst, in_sems.at[i])
        for i, (src, dst) in enumerate(
            (
                (reflect_hbm, reflect_ref),
                (clear_hbm, clear_ref),
                (live_hbm, live_ref),
                (day_hbm, day_ref),
                (quantile_hbm, quantile_ref),
            )
        )
    ]
    for load in loads:
        load.start()
    late_raw[...] = jnp.zeros_like(late_raw)
    quant[...] = jnp.zeros_like(quant)
    for load in loads:
        load.wait()
    for d in range(date_slots):
        for b in range(bands):
            group, row = find_row(d, b, bands)
            values = reflect_ref[b, d : d + 1, :]
            if group == 0:
                raw_all[my_date, row : row + 1, :] = values
            else:
                late_raw[row : row + 1, :] = values
            quant[group, row : row + 1, :] = rounded(quantile_ref[b : b + 1, :])

    for d in range(date_slots):
        live = lax.rem(jnp.int32(d), date_slots) < live_ref[my_date]
        valid = clear_ref[d : d + 1, :] * live.astype(jnp.int32)
        mask_all[my_date, d : d + 1, :] = valid.astype(jnp.float32)

    pl.semaphore_wait(barrier, groups + spaces - 2)

    each_date_peer(lambda peer: raw_copy(peer, my_date).start())
    each_date_peer(lambda peer: mask_copy(peer, my_date).start())

    def row_mask(slot, span):
        size = span.stop - span.start
        slots, _ = row_slot_band(iota((SUBLANES, size), 0), bands)
        return jnp.where(slots == 0, mask_all[slot, 0:1, span], mask_all[slot, 1:2, span])

    everything = slice(0, pixels)
    inner, spill = block_histograms(
        (raw_all[my_date], late_raw[...]),
        (
            row_mask(my_date, everything),
            jnp.broadcast_to(mask_all[my_date, 1:2, :], (SUBLANES, pixels)),
        ),
        bands,
        bins,
    )
    sums = running_sums(inner, spill, bands, bins)
    for d in range(date_slots):
        hist_own[d] = sums[d]

    hist_copies = []
    for peer in space_peers:
        copy = pltpu.make_async_remote_copy(
            src_ref=hist_own,
            dst_ref=hist_all.at[my_space],
            send_sem=hist_send.at[peer],
            recv_sem=hist_recv.at[my_space],
            device_id={"space": peer},
            device_id_type=MESH,
        )
        copy.start()
        hist_copies.append(copy)

    fit_rows = own_fit_rows(live_ref, day_ref, date_slots, dates, my_date * date_slots)

    total = [hist_own[d] for d in range(date_slots)]
    for peer in space_peers:
        pltpu.make_async_remote_copy(
            src_ref=hist_own,
            dst_ref=hist_all.at[peer],
            send_sem=hist_send.at[peer],
            recv_sem=hist_recv.at[peer],
            device_id={"space": peer},
            device_id_type=MESH,
        ).wait_recv()
        for d in range(date_slots):
            total[d] = total[d] + hist_all[peer, d]

    early_table, late_table = flat_tables(total, bands, bins)
    table_all[my_date] = early_table
    each_date_peer(lambda peer: table_copy(peer, my_date).start())

    def match(table, values, group):
        position = jnp.clip(bins * values - 0.5, 0.0, bins - 1.0)
        level = interpolate(table, position, bins)
        level = jnp.clip(bins * level - 0.5, 0.0, bins - 1.0)
        return interpolate(quant[group], level, bins)

    def match_early(slot):
        for start in range(0, pixels, LANES):
            span = slice(start, start + LANES)
            matched = match(table_all[slot], raw_all[slot, :, span], 0)
            early_all[slot, :, span] = matched * row_mask(slot, span)

    for start in range(0, pixels, LANES):
        span = slice(start, start + LANES)
        matched = match(late_table, late_raw[:, span], 1)[:rest]
        late_all[my_date, :, span] = matched * mask_all[my_date, 1:2, span]
    each_date_peer(lambda peer: late_copy(peer, my_date).start())

    match_early(my_date)

    def arrived(peer):
        mask_copy(peer, peer).wait_recv()
        raw_copy(peer, peer).wait_recv()
        table_copy(peer, peer).wait_recv()
        match_early(peer)

    each_date_peer(arrived)

    row_slot, _ = row_slot_band(iota((SUBLANES, 1), 0), bands)
    count = jnp.zeros((1, pixels), jnp.float32)
    gaps = [jnp.zeros((1, pixels), jnp.float32) for _ in range(date_slots)]
    summed = jnp.zeros((SUBLANES, pixels), jnp.float32)
    fits = [jnp.zeros((SUBLANES, pixels), jnp.float32) for _ in range(date_slots)]
    for g in range(groups):
        series = early_all[g]
        summed += series
        for d in range(date_slots):
            first, second = (fit_rows[d][:, 2 * g + s : 2 * g + s + 1] for s in range(2))
            fits[d] += jnp.where(row_slot == 0, first, second) * series
        for s in range(date_slots):
            mask = mask_all[g, s : s + 1, :]
            count += mask
            for d in range(date_slots):
                gaps[d] += fit_rows[d][:, 2 * g + s : 2 * g + s + 1] * (1.0 - mask)
    share = 1.0 / jnp.maximum(count, 1.0)
    gaps = [gap * share for gap in gaps]

    def finish(d, row, value):
        out_ref[row, d : d + 1, :] = value

    for b in range(rest, bands):
        other = bands + b - rest
        mean = summed[b : b + 1] + summed[other : other + 1]
        for d in range(date_slots):
            fit = fits[d][b : b + 1] + fits[d][other : other + 1] + gaps[d] * mean
            finish(d, b, mask_all[my_date, d : d + 1, :] * fit)

    each_date_peer(lambda peer: late_copy(peer, peer).wait_recv())
    summed = summed[:rest]
    fits = [fit[:rest] for fit in fits]
    for g in range(groups):
        series = late_all[g]
        summed += series
        for d in range(date_slots):
            fits[d] += fit_rows[d][:, 2 * g + 1 : 2 * g + 2] * series
    for d in range(date_slots):
        left = mask_all[my_date, d : d + 1, :] * (fits[d] + gaps[d] * summed)
        for b in range(rest):
            finish(d, b, left[b : b + 1])

    for copy in hist_copies:
        copy.wait_send()

    def sent(peer):
        raw_copy(peer, my_date).wait_send()
        mask_copy(peer, my_date).wait_send()
        table_copy(peer, my_date).wait_send()
        late_copy(peer, my_date).wait_send()

    each_date_peer(sent)


def per_device(groups, spaces, reflect, clear_sky, live_dates, day_of_year, ref_quantile):
    date_slots, bands, pixels = reflect.shape
    bins = ref_quantile.shape[1]
    rest = 2 * bands - SUBLANES
    by_band = jnp.transpose(reflect, (1, 0, 2))
    residual = pl.pallas_call(
        functools.partial(kernel, groups, spaces),
        out_shape=jax.ShapeDtypeStruct(by_band.shape, jnp.float32),
        in_specs=[pl.BlockSpec(memory_space=pltpu.HBM)] * 5,
        out_specs=pl.BlockSpec(memory_space=pltpu.VMEM),
        scratch_shapes=[
            pltpu.SMEM(live_dates.shape, jnp.int32),
            pltpu.SMEM(day_of_year.shape, jnp.int32),
            pltpu.VMEM(by_band.shape, jnp.float32),
            pltpu.VMEM(clear_sky.shape, jnp.int32),
            pltpu.VMEM(ref_quantile.shape, jnp.float32),
            pltpu.SemaphoreType.DMA((5,)),
            pltpu.VMEM((SUBLANES, pixels), jnp.float32),
            pltpu.VMEM((2, SUBLANES, bins), jnp.float32),
            pltpu.VMEM((date_slots, LOW, LANES), jnp.float32),
            pltpu.VMEM((spaces, date_slots, LOW, LANES), jnp.float32),
            pltpu.VMEM((groups, date_slots, pixels), jnp.float32),
            pltpu.VMEM((groups, SUBLANES, pixels), jnp.float32),
            pltpu.VMEM((groups, SUBLANES, bins), jnp.float32),
            pltpu.VMEM((groups, SUBLANES, pixels), jnp.float32),
            pltpu.VMEM((groups, rest, pixels), jnp.float32),
            pltpu.SemaphoreType.DMA((spaces,)),
            pltpu.SemaphoreType.DMA((spaces,)),
            pltpu.SemaphoreType.DMA((groups,)),
            pltpu.SemaphoreType.DMA((groups,)),
            pltpu.SemaphoreType.DMA((groups,)),
            pltpu.SemaphoreType.DMA((groups,)),
            pltpu.SemaphoreType.DMA((groups,)),
            pltpu.SemaphoreType.DMA((groups,)),
            pltpu.SemaphoreType.DMA((groups,)),
            pltpu.SemaphoreType.DMA((groups,)),
        ],
        compiler_params=pltpu.CompilerParams(
            collective_id=0, has_side_effects=True, vmem_limit_bytes=16 * 2**20
        ),
    )(
        *(
            pltpu.with_memory_space_constraint(x, pltpu.HBM)
            for x in (live_dates, day_of_year, by_band, clear_sky, ref_quantile)
        )
    )
    return jnp.transpose(residual, (1, 0, 2))


def solution(mesh):
    return jax.shard_map(
        functools.partial(per_device, mesh.shape["date"], mesh.shape["space"]),
        mesh=mesh,
        in_specs=(
            P("date", None, ("tiles", "space")),
            P("date", ("tiles", "space")),
            P(),
            P(),
            P(),
        ),
        out_specs=P("date", None, ("tiles", "space")),
        check_vma=False,
    )
```

```python
import functools
import math

import jax
import jax.numpy as jnp
from jax import lax
from jax.experimental import pallas as pl
from jax.experimental.pallas import tpu as pltpu
from jax.sharding import PartitionSpec as P

MESH = pl.DeviceIdType.MESH
HARMONICS = 7
RIDGE = 1.0
YEAR = 365
LOW = 16
LANES = 128
SUBLANES = 8


def iota(shape, dim):
    return lax.broadcasted_iota(jnp.int32, shape, dim)


def rounded(x):
    return x.astype(jnp.bfloat16).astype(jnp.float32)


def three_parts(x):
    first = x.astype(jnp.bfloat16)
    rest = x - first.astype(jnp.float32)
    second = rest.astype(jnp.bfloat16)
    return first, second, (rest - second.astype(jnp.float32)).astype(jnp.bfloat16)


def row_slot_band(row, bands):
    whole = SUBLANES - bands
    slot = (row >= bands).astype(jnp.int32)
    band = jnp.where(
        row < bands, row, jnp.where(row < SUBLANES, row - bands + (bands - whole), row - SUBLANES)
    )
    return slot, band


def find_row(slot, band, bands):
    rest = 2 * bands - SUBLANES
    if slot == 0:
        return 0, band
    return (1, band) if band < rest else (0, bands + band - rest)


def block_histograms(values, valid, bands, bins):
    high_count = bins // LOW
    pixels = values[0].shape[1]
    high_iota = iota((high_count, pixels), 0).astype(jnp.float32)
    low_iota = iota((LOW, pixels), 0).astype(jnp.float32)
    marked, local, spill = [], [], []
    for group in range(2):
        position = jnp.clip(bins * values[group] - 0.5, 0.0, bins - 1.0)
        high = jnp.floor(position * (1.0 / LOW))
        local.append(position - LOW * high)
        marked.append(jnp.where(valid[group] > 0.5, high, -1.0))
        spill.append(jnp.maximum(0.0, 1.0 - jnp.abs(local[group] - LOW)))
    spill = jnp.concatenate(spill, axis=0).astype(jnp.bfloat16)
    band_lane = iota((LOW, LANES), 1) // high_count
    row_slot, row_band = row_slot_band(iota((2 * SUBLANES, LANES), 0), bands)
    own_lane = iota((2 * SUBLANES, LANES), 1) // high_count
    hot, tents = [], []
    for slot in range(2):
        for band in range(bands):
            group, row = find_row(slot, band, bands)
            one = marked[group][row : row + 1]
            hot.append(jnp.where(high_iota == one, 1.0, 0.0).astype(jnp.bfloat16))
            near = 1.0 - jnp.abs(local[group][row : row + 1] - low_iota)
            tents.append(jnp.maximum(0.0, near).astype(jnp.bfloat16))
        hot.append(jnp.zeros((LANES - bands * high_count, pixels), jnp.bfloat16))
    counts = lax.dot_general(
        jnp.concatenate(tents + [spill], axis=0),
        jnp.concatenate(hot, axis=0),
        (((1,), (1,)), ((), ())),
        preferred_element_type=jnp.float32,
    )
    inners, outers = [], []
    for slot in range(2):
        part = counts[:, slot * LANES : (slot + 1) * LANES]
        inner = jnp.zeros((LOW, LANES), jnp.float32)
        for band in range(bands):
            start = (slot * bands + band) * LOW
            inner += jnp.where(band_lane == band, part[start : start + LOW], 0.0)
        own = (row_slot == slot) & (row_band == own_lane)
        outer = jnp.where(own, part[2 * bands * LOW :], 0.0)
        inners.append(inner)
        outers.append(jnp.sum(outer, axis=0, keepdims=True))
    return inners, outers


def running_sums(inner, spill, bands, bins):
    high_count = bins // LOW
    dates = len(inner)
    used = bands * high_count
    column = [jnp.sum(inner[d], axis=0, keepdims=True) + spill[d] for d in range(dates)]
    rows = column + spill
    left = jnp.zeros((SUBLANES, LANES), jnp.float32)
    row_of = iota((SUBLANES, LANES), 0)
    for i, row in enumerate(rows):
        left = jnp.where(row_of == i, row, left)
    src, dst = iota((LANES, LANES), 0), iota((LANES, LANES), 1)
    same = (src // high_count == dst // high_count) & (dst < used)
    before = jnp.where((same & (src < dst)) | (dst == used + src // high_count), 1.0, 0.0)
    shift = jnp.where(same & (src + 1 == dst), 0.5, 0.0)
    before = jnp.where(src < used, before, 0.0)
    shift = jnp.where(src < used, shift, 0.0)
    parts = [part.astype(jnp.float32) for part in three_parts(left)] + [jnp.zeros_like(left)]
    moved = jnp.dot(
        jnp.concatenate(parts, axis=0).astype(jnp.bfloat16),
        jnp.concatenate([before, shift], axis=1).astype(jnp.bfloat16),
        preferred_element_type=jnp.float32,
    )
    moved = sum(moved[i * SUBLANES : (i + 1) * SUBLANES] for i in range(3))
    out_row, in_row = iota((LOW, 3 * LOW), 0), iota((LOW, 3 * LOW), 1) % LOW
    lower = jnp.where(in_row < out_row, 1.0, jnp.where(in_row == out_row, 0.5, 0.0))
    within = jnp.dot(
        lower.astype(jnp.bfloat16),
        jnp.concatenate(three_parts(jnp.concatenate(inner, axis=1)), axis=0),
        preferred_element_type=jnp.float32,
    )
    first = iota((LOW, LANES), 0) == 0
    sums = []
    for d in range(dates):
        part = within[:, d * LANES : (d + 1) * LANES] + moved[d : d + 1, :LANES]
        back = moved[dates + d : dates + d + 1, LANES:]
        sums.append(part - jnp.where(first, back, 0.0))
    return sums


def flat_tables(sums, bands, bins):
    high_count = bins // LOW
    used = bands * high_count
    lane = iota((SUBLANES, LANES), 1)
    total_lane = jnp.minimum(used + lane // high_count, LANES - 1)
    band_lane = iota((LOW, LANES), 1) // high_count
    wide = []
    for part in sums:
        total = jnp.take_along_axis(part[:SUBLANES], total_lane, axis=1)[:1]
        cumulative = (part / jnp.maximum(total, 1.0)).astype(jnp.bfloat16).astype(jnp.float32)
        wide += [jnp.where(band_lane == band, cumulative, 0.0) for band in range(bands)]
    src, dst = iota((LANES, bins), 0), iota((LANES, bins), 1)
    spread = jnp.where((src % high_count == dst // LOW) & (src < used), 1.0, 0.0)
    placed = jnp.dot(
        jnp.concatenate(wide, axis=0).astype(jnp.bfloat16),
        spread.astype(jnp.bfloat16),
        preferred_element_type=jnp.float32,
    )
    rows, cols = iota(placed.shape, 0), iota(placed.shape, 1)
    placed = jnp.where(rows % LOW == cols % LOW, placed, 0.0).astype(jnp.bfloat16)
    shape = (2 * SUBLANES, 2 * bands * LOW)
    slot, band = row_slot_band(iota(shape, 0), bands)
    pick = jnp.where((iota(shape, 1) // LOW == slot * bands + band) & (band < bands), 1.0, 0.0)
    tables = jnp.dot(pick.astype(jnp.bfloat16), placed, preferred_element_type=jnp.float32)
    return tables[:SUBLANES], tables[SUBLANES:]


def gather_lanes(table, index):
    parts = table.shape[1] // LANES
    inner = index % LANES
    out = jnp.take_along_axis(table[:, :LANES], inner, axis=1)
    for part in range(1, parts):
        other = jnp.take_along_axis(table[:, part * LANES : (part + 1) * LANES], inner, axis=1)
        out = jnp.where(index >= part * LANES, other, out)
    return out


def interpolate(table, position, bins):
    low = jnp.floor(position)
    first = low.astype(jnp.int32)
    second = jnp.minimum(first + 1, bins - 1)
    low_weight = rounded(1.0 - jnp.abs(position - low))
    high_weight = rounded(jnp.maximum(0.0, 1.0 - jnp.abs(position - (low + 1.0))))
    return low_weight * gather_lanes(table, first) + high_weight * gather_lanes(table, second)


def own_fit_rows(live_ref, day_ref, date_slots, dates, first_date):
    size = max(dates, SUBLANES)
    rows, cols = iota((size, size), 0), iota((size, size), 1)

    def place(t, carry):
        day_r, day_c, live_r, live_c = carry
        day = day_ref[t]
        live = (lax.rem(t, date_slots) < live_ref[lax.div(t, date_slots)]).astype(jnp.int32)
        return (
            jnp.where(rows == t, day, day_r),
            jnp.where(cols == t, day, day_c),
            jnp.where(rows == t, live, live_r),
            jnp.where(cols == t, live, live_c),
        )

    zero = jnp.zeros((size, size), jnp.int32)
    day_r, day_c, live_r, live_c = lax.fori_loop(
        0, dates, place, (zero, zero, zero, zero), unroll=dates <= 16
    )
    base = jnp.cos((2.0 * math.pi / YEAR) * (day_r - day_c).astype(jnp.float32))
    older, newer = jnp.ones_like(base), base
    total = older + newer
    for _ in range(HARMONICS - 1):
        older, newer = newer, 2.0 * base * newer - older
        total = total + newer
    eye = jnp.where(rows == cols, 1.0, 0.0)
    work = jnp.where((live_r * live_c) == 1, total, 0.0) + RIDGE * eye
    inverse = eye
    for k in range(dates):
        pivot = work[k : k + 1, k : k + 1]
        row_w, row_i = work[k : k + 1, :] / pivot, inverse[k : k + 1, :] / pivot
        column = work[:, k : k + 1]
        work = jnp.where(rows == k, row_w, work - column * row_w)
        inverse = jnp.where(rows == k, row_i, inverse - column * row_i)
    return [
        jnp.sum(jnp.where(rows == first_date + d, inverse, 0.0), axis=0, keepdims=True)
        for d in range(date_slots)
    ]


def kernel(
    groups,
    spaces,
    live_hbm,
    day_hbm,
    reflect_hbm,
    clear_hbm,
    quantile_hbm,
    out_ref,
    live_ref,
    day_ref,
    reflect_ref,
    clear_ref,
    quantile_ref,
    in_sems,
    late_raw,
    quant,
    hist_own,
    hist_all,
    mask_all,
    raw_all,
    table_all,
    early_all,
    late_all,
    hist_send,
    hist_recv,
    mask_send,
    mask_recv,
    raw_send,
    raw_recv,
    table_send,
    table_recv,
    late_send,
    late_recv,
):
    bands, date_slots, pixels = reflect_ref.shape
    bins = quantile_ref.shape[1]
    dates = date_slots * groups
    rest = 2 * bands - SUBLANES
    my_date, my_space = lax.axis_index("date"), lax.axis_index("space")
    space_peers = [lax.rem(my_space + i, spaces) for i in range(1, spaces)]

    def each_date_peer(body):
        def step(i, carry):
            body(lax.rem(my_date + i, groups))
            return carry

        if groups <= 8:
            for i in range(1, groups):
                step(i, 0)
        else:
            lax.fori_loop(1, groups, step, 0)

    def to_date(src, dst, send, recv, peer):
        return pltpu.make_async_remote_copy(
            src_ref=src,
            dst_ref=dst,
            send_sem=send,
            recv_sem=recv,
            device_id={"date": peer},
            device_id_type=MESH,
        )

    def mask_copy(peer, slot):
        return to_date(
            mask_all.at[slot], mask_all.at[slot], mask_send.at[peer], mask_recv.at[slot], peer
        )

    def raw_copy(peer, slot):
        return to_date(
            raw_all.at[slot], raw_all.at[slot], raw_send.at[peer], raw_recv.at[slot], peer
        )

    def table_copy(peer, slot):
        return to_date(
            table_all.at[slot], table_all.at[slot], table_send.at[peer], table_recv.at[slot], peer
        )

    def late_copy(peer, slot):
        return to_date(
            late_all.at[slot], late_all.at[slot], late_send.at[peer], late_recv.at[slot], peer
        )

    loads = [
        pltpu.make_async_copy(src, dst, in_sems.at[i])
        for i, (src, dst) in enumerate(
            (
                (reflect_hbm, reflect_ref),
                (clear_hbm, clear_ref),
                (live_hbm, live_ref),
                (day_hbm, day_ref),
                (quantile_hbm, quantile_ref),
            )
        )
    ]
    for load in loads:
        load.start()

    barrier = pltpu.get_barrier_semaphore()
    for peer in space_peers:
        pl.semaphore_signal(barrier, inc=1, device_id={"space": peer}, device_id_type=MESH)
    each_date_peer(
        lambda peer: pl.semaphore_signal(
            barrier, inc=1, device_id={"date": peer}, device_id_type=MESH
        )
    )

    late_raw[...] = jnp.zeros_like(late_raw)
    for load in loads[:3]:
        load.wait()
    for d in range(date_slots):
        for b in range(bands):
            group, row = find_row(d, b, bands)
            values = reflect_ref[b, d : d + 1, :]
            if group == 0:
                raw_all[my_date, row : row + 1, :] = values
            else:
                late_raw[row : row + 1, :] = values

    for d in range(date_slots):
        live = lax.rem(jnp.int32(d), date_slots) < live_ref[my_date]
        valid = clear_ref[d : d + 1, :] * live.astype(jnp.int32)
        mask_all[my_date, d : d + 1, :] = valid.astype(jnp.float32)

    def row_mask(slot, span):
        size = span.stop - span.start
        slots, _ = row_slot_band(iota((SUBLANES, size), 0), bands)
        return jnp.where(slots == 0, mask_all[slot, 0:1, span], mask_all[slot, 1:2, span])

    everything = slice(0, pixels)
    inner, spill = block_histograms(
        (raw_all[my_date], late_raw[...]),
        (
            row_mask(my_date, everything),
            jnp.broadcast_to(mask_all[my_date, 1:2, :], (SUBLANES, pixels)),
        ),
        bands,
        bins,
    )
    sums = running_sums(inner, spill, bands, bins)
    for d in range(date_slots):
        hist_own[d] = sums[d]

    pl.semaphore_wait(barrier, groups + spaces - 2)

    hist_copies = []
    for peer in space_peers:
        copy = pltpu.make_async_remote_copy(
            src_ref=hist_own,
            dst_ref=hist_all.at[my_space],
            send_sem=hist_send.at[peer],
            recv_sem=hist_recv.at[my_space],
            device_id={"space": peer},
            device_id_type=MESH,
        )
        copy.start()
        hist_copies.append(copy)
    each_date_peer(lambda peer: raw_copy(peer, my_date).start())
    each_date_peer(lambda peer: mask_copy(peer, my_date).start())

    for load in loads[3:]:
        load.wait()
    quant[...] = jnp.zeros_like(quant)
    for d in range(date_slots):
        for b in range(bands):
            group, row = find_row(d, b, bands)
            quant[group, row : row + 1, :] = rounded(quantile_ref[b : b + 1, :])
    fit_rows = own_fit_rows(live_ref, day_ref, date_slots, dates, my_date * date_slots)

    total = [hist_own[d] for d in range(date_slots)]
    for peer in space_peers:
        pltpu.make_async_remote_copy(
            src_ref=hist_own,
            dst_ref=hist_all.at[peer],
            send_sem=hist_send.at[peer],
            recv_sem=hist_recv.at[peer],
            device_id={"space": peer},
            device_id_type=MESH,
        ).wait_recv()
        for d in range(date_slots):
            total[d] = total[d] + hist_all[peer, d]

    early_table, late_table = flat_tables(total, bands, bins)
    table_all[my_date] = early_table
    each_date_peer(lambda peer: table_copy(peer, my_date).start())

    def match(table, values, group):
        position = jnp.clip(bins * values - 0.5, 0.0, bins - 1.0)
        level = interpolate(table, position, bins)
        level = jnp.clip(bins * level - 0.5, 0.0, bins - 1.0)
        return interpolate(quant[group], level, bins)

    def match_early(slot):
        for start in range(0, pixels, LANES):
            span = slice(start, start + LANES)
            matched = match(table_all[slot], raw_all[slot, :, span], 0)
            early_all[slot, :, span] = matched * row_mask(slot, span)

    for start in range(0, pixels, LANES):
        span = slice(start, start + LANES)
        matched = match(late_table, late_raw[:, span], 1)[:rest]
        late_all[my_date, :, span] = matched * mask_all[my_date, 1:2, span]
    each_date_peer(lambda peer: late_copy(peer, my_date).start())

    match_early(my_date)

    def arrived(peer):
        mask_copy(peer, peer).wait_recv()
        raw_copy(peer, peer).wait_recv()
        table_copy(peer, peer).wait_recv()
        match_early(peer)

    each_date_peer(arrived)

    row_slot, _ = row_slot_band(iota((SUBLANES, 1), 0), bands)
    count = jnp.zeros((1, pixels), jnp.float32)
    gaps = [jnp.zeros((1, pixels), jnp.float32) for _ in range(date_slots)]
    summed = jnp.zeros((SUBLANES, pixels), jnp.float32)
    fits = [jnp.zeros((SUBLANES, pixels), jnp.float32) for _ in range(date_slots)]
    for g in range(groups):
        series = early_all[g]
        summed += series
        for d in range(date_slots):
            first, second = (fit_rows[d][:, 2 * g + s : 2 * g + s + 1] for s in range(2))
            fits[d] += jnp.where(row_slot == 0, first, second) * series
        for s in range(date_slots):
            mask = mask_all[g, s : s + 1, :]
            count += mask
            for d in range(date_slots):
                gaps[d] += fit_rows[d][:, 2 * g + s : 2 * g + s + 1] * (1.0 - mask)
    share = 1.0 / jnp.maximum(count, 1.0)
    gaps = [gap * share for gap in gaps]

    def finish(d, row, value):
        out_ref[row, d : d + 1, :] = value

    for b in range(rest, bands):
        other = bands + b - rest
        mean = summed[b : b + 1] + summed[other : other + 1]
        for d in range(date_slots):
            fit = fits[d][b : b + 1] + fits[d][other : other + 1] + gaps[d] * mean
            finish(d, b, mask_all[my_date, d : d + 1, :] * fit)

    each_date_peer(lambda peer: late_copy(peer, peer).wait_recv())
    summed = summed[:rest]
    fits = [fit[:rest] for fit in fits]
    for g in range(groups):
        series = late_all[g]
        summed += series
        for d in range(date_slots):
            fits[d] += fit_rows[d][:, 2 * g + 1 : 2 * g + 2] * series
    for d in range(date_slots):
        left = mask_all[my_date, d : d + 1, :] * (fits[d] + gaps[d] * summed)
        for b in range(rest):
            finish(d, b, left[b : b + 1])

    for copy in hist_copies:
        copy.wait_send()

    def sent(peer):
        raw_copy(peer, my_date).wait_send()
        mask_copy(peer, my_date).wait_send()
        table_copy(peer, my_date).wait_send()
        late_copy(peer, my_date).wait_send()

    each_date_peer(sent)


def per_device(groups, spaces, reflect, clear_sky, live_dates, day_of_year, ref_quantile):
    date_slots, bands, pixels = reflect.shape
    bins = ref_quantile.shape[1]
    rest = 2 * bands - SUBLANES
    by_band = jnp.transpose(reflect, (1, 0, 2))
    residual = pl.pallas_call(
        functools.partial(kernel, groups, spaces),
        out_shape=jax.ShapeDtypeStruct(by_band.shape, jnp.float32),
        in_specs=[pl.BlockSpec(memory_space=pltpu.HBM)] * 5,
        out_specs=pl.BlockSpec(memory_space=pltpu.VMEM),
        scratch_shapes=[
            pltpu.SMEM(live_dates.shape, jnp.int32),
            pltpu.SMEM(day_of_year.shape, jnp.int32),
            pltpu.VMEM(by_band.shape, jnp.float32),
            pltpu.VMEM(clear_sky.shape, jnp.int32),
            pltpu.VMEM(ref_quantile.shape, jnp.float32),
            pltpu.SemaphoreType.DMA((5,)),
            pltpu.VMEM((SUBLANES, pixels), jnp.float32),
            pltpu.VMEM((2, SUBLANES, bins), jnp.float32),
            pltpu.VMEM((date_slots, LOW, LANES), jnp.float32),
            pltpu.VMEM((spaces, date_slots, LOW, LANES), jnp.float32),
            pltpu.VMEM((groups, date_slots, pixels), jnp.float32),
            pltpu.VMEM((groups, SUBLANES, pixels), jnp.float32),
            pltpu.VMEM((groups, SUBLANES, bins), jnp.float32),
            pltpu.VMEM((groups, SUBLANES, pixels), jnp.float32),
            pltpu.VMEM((groups, rest, pixels), jnp.float32),
            pltpu.SemaphoreType.DMA((spaces,)),
            pltpu.SemaphoreType.DMA((spaces,)),
            pltpu.SemaphoreType.DMA((groups,)),
            pltpu.SemaphoreType.DMA((groups,)),
            pltpu.SemaphoreType.DMA((groups,)),
            pltpu.SemaphoreType.DMA((groups,)),
            pltpu.SemaphoreType.DMA((groups,)),
            pltpu.SemaphoreType.DMA((groups,)),
            pltpu.SemaphoreType.DMA((groups,)),
            pltpu.SemaphoreType.DMA((groups,)),
        ],
        compiler_params=pltpu.CompilerParams(
            collective_id=0, has_side_effects=True, vmem_limit_bytes=16 * 2**20
        ),
    )(
        *(
            pltpu.with_memory_space_constraint(x, pltpu.HBM)
            for x in (live_dates, day_of_year, by_band, clear_sky, ref_quantile)
        )
    )
    return jnp.transpose(residual, (1, 0, 2))


def solution(mesh):
    return jax.shard_map(
        functools.partial(per_device, mesh.shape["date"], mesh.shape["space"]),
        mesh=mesh,
        in_specs=(
            P("date", None, ("tiles", "space")),
            P("date", ("tiles", "space")),
            P(),
            P(),
            P(),
        ),
        out_specs=P("date", None, ("tiles", "space")),
        check_vma=False,
    )
```

```python
import functools
import math

import jax
import jax.numpy as jnp
from jax import lax
from jax.experimental import pallas as pl
from jax.experimental.pallas import tpu as pltpu
from jax.sharding import PartitionSpec as P

MESH = pl.DeviceIdType.MESH
HARMONICS = 7
RIDGE = 1.0
YEAR = 365
LOW = 16
LANES = 128
SUBLANES = 8


def iota(shape, dim):
    return lax.broadcasted_iota(jnp.int32, shape, dim)


def rounded(x):
    return x.astype(jnp.bfloat16).astype(jnp.float32)


def three_parts(x):
    first = x.astype(jnp.bfloat16)
    rest = x - first.astype(jnp.float32)
    second = rest.astype(jnp.bfloat16)
    return first, second, (rest - second.astype(jnp.float32)).astype(jnp.bfloat16)


def row_slot_band(row, bands):
    whole = SUBLANES - bands
    slot = (row >= bands).astype(jnp.int32)
    band = jnp.where(
        row < bands, row, jnp.where(row < SUBLANES, row - bands + (bands - whole), row - SUBLANES)
    )
    return slot, band


def find_row(slot, band, bands):
    rest = 2 * bands - SUBLANES
    if slot == 0:
        return 0, band
    return (1, band) if band < rest else (0, bands + band - rest)


def block_histograms(values, valid, bands, bins):
    high_count = bins // LOW
    pixels = values[0].shape[1]
    high_iota = iota((high_count, pixels), 0).astype(jnp.float32)
    low_iota = iota((LOW, pixels), 0).astype(jnp.float32)
    marked, local, spill = [], [], []
    for group in range(2):
        position = jnp.clip(bins * values[group] - 0.5, 0.0, bins - 1.0)
        high = jnp.floor(position * (1.0 / LOW))
        local.append(position - LOW * high)
        marked.append(jnp.where(valid[group] > 0.5, high, -1.0))
        spill.append(jnp.maximum(0.0, 1.0 - jnp.abs(local[group] - LOW)))
    spill = jnp.concatenate(spill, axis=0).astype(jnp.bfloat16)
    band_lane = iota((LOW, LANES), 1) // high_count
    row_slot, row_band = row_slot_band(iota((2 * SUBLANES, LANES), 0), bands)
    own_lane = iota((2 * SUBLANES, LANES), 1) // high_count
    hot, tents = [], []
    for slot in range(2):
        for band in range(bands):
            group, row = find_row(slot, band, bands)
            one = marked[group][row : row + 1]
            hot.append(jnp.where(high_iota == one, 1.0, 0.0).astype(jnp.bfloat16))
            near = 1.0 - jnp.abs(local[group][row : row + 1] - low_iota)
            tents.append(jnp.maximum(0.0, near).astype(jnp.bfloat16))
        hot.append(jnp.zeros((LANES - bands * high_count, pixels), jnp.bfloat16))
    counts = lax.dot_general(
        jnp.concatenate(tents + [spill], axis=0),
        jnp.concatenate(hot, axis=0),
        (((1,), (1,)), ((), ())),
        preferred_element_type=jnp.float32,
    )
    inners, outers = [], []
    for slot in range(2):
        part = counts[:, slot * LANES : (slot + 1) * LANES]
        inner = jnp.zeros((LOW, LANES), jnp.float32)
        for band in range(bands):
            start = (slot * bands + band) * LOW
            inner += jnp.where(band_lane == band, part[start : start + LOW], 0.0)
        own = (row_slot == slot) & (row_band == own_lane)
        outer = jnp.where(own, part[2 * bands * LOW :], 0.0)
        inners.append(inner)
        outers.append(jnp.sum(outer, axis=0, keepdims=True))
    return inners, outers


def running_sums(inner, spill, bands, bins):
    high_count = bins // LOW
    dates = len(inner)
    used = bands * high_count
    column = [jnp.sum(inner[d], axis=0, keepdims=True) + spill[d] for d in range(dates)]
    rows = column + spill
    left = jnp.zeros((SUBLANES, LANES), jnp.float32)
    row_of = iota((SUBLANES, LANES), 0)
    for i, row in enumerate(rows):
        left = jnp.where(row_of == i, row, left)
    src, dst = iota((LANES, LANES), 0), iota((LANES, LANES), 1)
    same = (src // high_count == dst // high_count) & (dst < used)
    before = jnp.where((same & (src < dst)) | (dst == used + src // high_count), 1.0, 0.0)
    shift = jnp.where(same & (src + 1 == dst), 0.5, 0.0)
    before = jnp.where(src < used, before, 0.0)
    shift = jnp.where(src < used, shift, 0.0)
    parts = [part.astype(jnp.float32) for part in three_parts(left)] + [jnp.zeros_like(left)]
    moved = jnp.dot(
        jnp.concatenate(parts, axis=0).astype(jnp.bfloat16),
        jnp.concatenate([before, shift], axis=1).astype(jnp.bfloat16),
        preferred_element_type=jnp.float32,
    )
    moved = sum(moved[i * SUBLANES : (i + 1) * SUBLANES] for i in range(3))
    out_row, in_row = iota((LOW, 3 * LOW), 0), iota((LOW, 3 * LOW), 1) % LOW
    lower = jnp.where(in_row < out_row, 1.0, jnp.where(in_row == out_row, 0.5, 0.0))
    within = jnp.dot(
        lower.astype(jnp.bfloat16),
        jnp.concatenate(three_parts(jnp.concatenate(inner, axis=1)), axis=0),
        preferred_element_type=jnp.float32,
    )
    first = iota((LOW, LANES), 0) == 0
    sums = []
    for d in range(dates):
        part = within[:, d * LANES : (d + 1) * LANES] + moved[d : d + 1, :LANES]
        back = moved[dates + d : dates + d + 1, LANES:]
        sums.append(part - jnp.where(first, back, 0.0))
    return sums


def flat_tables(sums, bands, bins):
    high_count = bins // LOW
    used = bands * high_count
    lane = iota((SUBLANES, LANES), 1)
    total_lane = jnp.minimum(used + lane // high_count, LANES - 1)
    band_lane = iota((LOW, LANES), 1) // high_count
    wide = []
    for part in sums:
        total = jnp.take_along_axis(part[:SUBLANES], total_lane, axis=1)[:1]
        cumulative = (part / jnp.maximum(total, 1.0)).astype(jnp.bfloat16).astype(jnp.float32)
        wide += [jnp.where(band_lane == band, cumulative, 0.0) for band in range(bands)]
    src, dst = iota((LANES, bins), 0), iota((LANES, bins), 1)
    spread = jnp.where((src % high_count == dst // LOW) & (src < used), 1.0, 0.0)
    placed = jnp.dot(
        jnp.concatenate(wide, axis=0).astype(jnp.bfloat16),
        spread.astype(jnp.bfloat16),
        preferred_element_type=jnp.float32,
    )
    rows, cols = iota(placed.shape, 0), iota(placed.shape, 1)
    placed = jnp.where(rows % LOW == cols % LOW, placed, 0.0).astype(jnp.bfloat16)
    shape = (2 * SUBLANES, 2 * bands * LOW)
    slot, band = row_slot_band(iota(shape, 0), bands)
    pick = jnp.where((iota(shape, 1) // LOW == slot * bands + band) & (band < bands), 1.0, 0.0)
    tables = jnp.dot(pick.astype(jnp.bfloat16), placed, preferred_element_type=jnp.float32)
    return tables[:SUBLANES], tables[SUBLANES:]


def gather_lanes(table, index):
    parts = table.shape[1] // LANES
    inner = index % LANES
    out = jnp.take_along_axis(table[:, :LANES], inner, axis=1)
    for part in range(1, parts):
        other = jnp.take_along_axis(table[:, part * LANES : (part + 1) * LANES], inner, axis=1)
        out = jnp.where(index >= part * LANES, other, out)
    return out


def interpolate(table, position, bins):
    low = jnp.floor(position)
    first = low.astype(jnp.int32)
    second = jnp.minimum(first + 1, bins - 1)
    low_weight = rounded(1.0 - jnp.abs(position - low))
    high_weight = rounded(jnp.maximum(0.0, 1.0 - jnp.abs(position - (low + 1.0))))
    return low_weight * gather_lanes(table, first) + high_weight * gather_lanes(table, second)


def own_fit_rows(live_ref, day_ref, date_slots, dates, first_date):
    size = max(dates, SUBLANES)
    rows, cols = iota((size, size), 0), iota((size, size), 1)

    def place(t, carry):
        day_r, day_c, live_r, live_c = carry
        day = day_ref[t]
        live = (lax.rem(t, date_slots) < live_ref[lax.div(t, date_slots)]).astype(jnp.int32)
        return (
            jnp.where(rows == t, day, day_r),
            jnp.where(cols == t, day, day_c),
            jnp.where(rows == t, live, live_r),
            jnp.where(cols == t, live, live_c),
        )

    zero = jnp.zeros((size, size), jnp.int32)
    day_r, day_c, live_r, live_c = lax.fori_loop(
        0, dates, place, (zero, zero, zero, zero), unroll=dates <= 16
    )
    base = jnp.cos((2.0 * math.pi / YEAR) * (day_r - day_c).astype(jnp.float32))
    older, newer = jnp.ones_like(base), base
    total = older + newer
    for _ in range(HARMONICS - 1):
        older, newer = newer, 2.0 * base * newer - older
        total = total + newer
    eye = jnp.where(rows == cols, 1.0, 0.0)
    work = jnp.where((live_r * live_c) == 1, total, 0.0) + RIDGE * eye
    inverse = eye
    for k in range(dates):
        pivot = work[k : k + 1, k : k + 1]
        row_w, row_i = work[k : k + 1, :] / pivot, inverse[k : k + 1, :] / pivot
        column = work[:, k : k + 1]
        work = jnp.where(rows == k, row_w, work - column * row_w)
        inverse = jnp.where(rows == k, row_i, inverse - column * row_i)
    return [
        jnp.sum(jnp.where(rows == first_date + d, inverse, 0.0), axis=0, keepdims=True)
        for d in range(date_slots)
    ]


def kernel(
    groups,
    spaces,
    live_hbm,
    day_hbm,
    reflect_hbm,
    clear_hbm,
    quantile_hbm,
    out_ref,
    live_ref,
    day_ref,
    reflect_ref,
    clear_ref,
    quantile_ref,
    in_sems,
    late_raw,
    quant,
    hist_own,
    hist_all,
    mask_all,
    raw_all,
    table_all,
    early_all,
    late_all,
    hist_send,
    hist_recv,
    mask_send,
    mask_recv,
    raw_send,
    raw_recv,
    table_send,
    table_recv,
    late_send,
    late_recv,
):
    bands, date_slots, pixels = reflect_ref.shape
    bins = quantile_ref.shape[1]
    dates = date_slots * groups
    rest = 2 * bands - SUBLANES
    my_date, my_space = lax.axis_index("date"), lax.axis_index("space")
    space_peers = [lax.rem(my_space + i, spaces) for i in range(1, spaces)]

    def each_date_peer(body):
        def step(i, carry):
            body(i + jnp.where(my_date <= i, 1, 0))
            return carry

        if groups <= 8:
            for i in range(groups - 1):
                step(i, 0)
        else:
            lax.fori_loop(0, groups - 1, step, 0)

    def to_date(src, dst, send, recv, peer):
        return pltpu.make_async_remote_copy(
            src_ref=src,
            dst_ref=dst,
            send_sem=send,
            recv_sem=recv,
            device_id={"date": peer},
            device_id_type=MESH,
        )

    def mask_copy(peer, slot):
        return to_date(
            mask_all.at[slot], mask_all.at[slot], mask_send.at[peer], mask_recv.at[slot], peer
        )

    def raw_copy(peer, slot):
        return to_date(
            raw_all.at[slot], raw_all.at[slot], raw_send.at[peer], raw_recv.at[slot], peer
        )

    def table_copy(peer, slot):
        return to_date(
            table_all.at[slot], table_all.at[slot], table_send.at[peer], table_recv.at[slot], peer
        )

    def late_copy(peer, slot):
        return to_date(
            late_all.at[slot], late_all.at[slot], late_send.at[peer], late_recv.at[slot], peer
        )

    loads = [
        pltpu.make_async_copy(src, dst, in_sems.at[i])
        for i, (src, dst) in enumerate(
            (
                (reflect_hbm, reflect_ref),
                (clear_hbm, clear_ref),
                (live_hbm, live_ref),
                (day_hbm, day_ref),
                (quantile_hbm, quantile_ref),
            )
        )
    ]
    for load in loads:
        load.start()

    barrier = pltpu.get_barrier_semaphore()
    for peer in space_peers:
        pl.semaphore_signal(barrier, inc=1, device_id={"space": peer}, device_id_type=MESH)
    each_date_peer(
        lambda peer: pl.semaphore_signal(
            barrier, inc=1, device_id={"date": peer}, device_id_type=MESH
        )
    )

    late_raw[...] = jnp.zeros_like(late_raw)
    for load in loads[:3]:
        load.wait()
    for d in range(date_slots):
        for b in range(bands):
            group, row = find_row(d, b, bands)
            values = reflect_ref[b, d : d + 1, :]
            if group == 0:
                raw_all[my_date, row : row + 1, :] = values
            else:
                late_raw[row : row + 1, :] = values

    for d in range(date_slots):
        live = lax.rem(jnp.int32(d), date_slots) < live_ref[my_date]
        valid = clear_ref[d : d + 1, :] * live.astype(jnp.int32)
        mask_all[my_date, d : d + 1, :] = valid.astype(jnp.float32)

    def row_mask(slot, span):
        size = span.stop - span.start
        slots, _ = row_slot_band(iota((SUBLANES, size), 0), bands)
        return jnp.where(slots == 0, mask_all[slot, 0:1, span], mask_all[slot, 1:2, span])

    everything = slice(0, pixels)
    inner, spill = block_histograms(
        (raw_all[my_date], late_raw[...]),
        (
            row_mask(my_date, everything),
            jnp.broadcast_to(mask_all[my_date, 1:2, :], (SUBLANES, pixels)),
        ),
        bands,
        bins,
    )
    sums = running_sums(inner, spill, bands, bins)
    for d in range(date_slots):
        hist_own[d] = sums[d]

    pl.semaphore_wait(barrier, groups + spaces - 2)

    hist_copies = []
    for peer in space_peers:
        copy = pltpu.make_async_remote_copy(
            src_ref=hist_own,
            dst_ref=hist_all.at[my_space],
            send_sem=hist_send.at[peer],
            recv_sem=hist_recv.at[my_space],
            device_id={"space": peer},
            device_id_type=MESH,
        )
        copy.start()
        hist_copies.append(copy)

    def send_raw(peer):
        raw_copy(peer, my_date).start()
        mask_copy(peer, my_date).start()

    each_date_peer(send_raw)

    for load in loads[3:]:
        load.wait()
    quant[...] = jnp.zeros_like(quant)
    for d in range(date_slots):
        for b in range(bands):
            group, row = find_row(d, b, bands)
            quant[group, row : row + 1, :] = rounded(quantile_ref[b : b + 1, :])
    fit_rows = own_fit_rows(live_ref, day_ref, date_slots, dates, my_date * date_slots)

    total = [hist_own[d] for d in range(date_slots)]
    for peer in space_peers:
        pltpu.make_async_remote_copy(
            src_ref=hist_own,
            dst_ref=hist_all.at[peer],
            send_sem=hist_send.at[peer],
            recv_sem=hist_recv.at[peer],
            device_id={"space": peer},
            device_id_type=MESH,
        ).wait_recv()
        for d in range(date_slots):
            total[d] = total[d] + hist_all[peer, d]

    early_table, late_table = flat_tables(total, bands, bins)
    table_all[my_date] = early_table
    each_date_peer(lambda peer: table_copy(peer, my_date).start())

    def match(table, values, group):
        position = jnp.clip(bins * values - 0.5, 0.0, bins - 1.0)
        level = interpolate(table, position, bins)
        level = jnp.clip(bins * level - 0.5, 0.0, bins - 1.0)
        return interpolate(quant[group], level, bins)

    def match_early(slot):
        for start in range(0, pixels, LANES):
            span = slice(start, start + LANES)
            matched = match(table_all[slot], raw_all[slot, :, span], 0)
            early_all[slot, :, span] = matched * row_mask(slot, span)

    for start in range(0, pixels, LANES):
        span = slice(start, start + LANES)
        matched = match(late_table, late_raw[:, span], 1)[:rest]
        late_all[my_date, :, span] = matched * mask_all[my_date, 1:2, span]
    each_date_peer(lambda peer: late_copy(peer, my_date).start())

    match_early(my_date)

    def arrived(peer):
        mask_copy(peer, peer).wait_recv()
        raw_copy(peer, peer).wait_recv()
        table_copy(peer, peer).wait_recv()
        match_early(peer)

    each_date_peer(arrived)

    row_slot, _ = row_slot_band(iota((SUBLANES, 1), 0), bands)
    count = jnp.zeros((1, pixels), jnp.float32)
    gaps = [jnp.zeros((1, pixels), jnp.float32) for _ in range(date_slots)]
    summed = jnp.zeros((SUBLANES, pixels), jnp.float32)
    fits = [jnp.zeros((SUBLANES, pixels), jnp.float32) for _ in range(date_slots)]
    for g in range(groups):
        series = early_all[g]
        summed += series
        for d in range(date_slots):
            first, second = (fit_rows[d][:, 2 * g + s : 2 * g + s + 1] for s in range(2))
            fits[d] += jnp.where(row_slot == 0, first, second) * series
        for s in range(date_slots):
            mask = mask_all[g, s : s + 1, :]
            count += mask
            for d in range(date_slots):
                gaps[d] += fit_rows[d][:, 2 * g + s : 2 * g + s + 1] * (1.0 - mask)
    share = 1.0 / jnp.maximum(count, 1.0)
    gaps = [gap * share for gap in gaps]

    def finish(d, row, value):
        out_ref[row, d : d + 1, :] = value

    for b in range(rest, bands):
        other = bands + b - rest
        mean = summed[b : b + 1] + summed[other : other + 1]
        for d in range(date_slots):
            fit = fits[d][b : b + 1] + fits[d][other : other + 1] + gaps[d] * mean
            finish(d, b, mask_all[my_date, d : d + 1, :] * fit)

    each_date_peer(lambda peer: late_copy(peer, peer).wait_recv())
    summed = summed[:rest]
    fits = [fit[:rest] for fit in fits]
    for g in range(groups):
        series = late_all[g]
        summed += series
        for d in range(date_slots):
            fits[d] += fit_rows[d][:, 2 * g + 1 : 2 * g + 2] * series
    for d in range(date_slots):
        left = mask_all[my_date, d : d + 1, :] * (fits[d] + gaps[d] * summed)
        for b in range(rest):
            finish(d, b, left[b : b + 1])

    for copy in hist_copies:
        copy.wait_send()

    def sent(peer):
        raw_copy(peer, my_date).wait_send()
        mask_copy(peer, my_date).wait_send()
        table_copy(peer, my_date).wait_send()
        late_copy(peer, my_date).wait_send()

    each_date_peer(sent)


def per_device(groups, spaces, reflect, clear_sky, live_dates, day_of_year, ref_quantile):
    date_slots, bands, pixels = reflect.shape
    bins = ref_quantile.shape[1]
    rest = 2 * bands - SUBLANES
    by_band = jnp.transpose(reflect, (1, 0, 2))
    residual = pl.pallas_call(
        functools.partial(kernel, groups, spaces),
        out_shape=jax.ShapeDtypeStruct(by_band.shape, jnp.float32),
        in_specs=[pl.BlockSpec(memory_space=pltpu.HBM)] * 5,
        out_specs=pl.BlockSpec(memory_space=pltpu.VMEM),
        scratch_shapes=[
            pltpu.SMEM(live_dates.shape, jnp.int32),
            pltpu.SMEM(day_of_year.shape, jnp.int32),
            pltpu.VMEM(by_band.shape, jnp.float32),
            pltpu.VMEM(clear_sky.shape, jnp.int32),
            pltpu.VMEM(ref_quantile.shape, jnp.float32),
            pltpu.SemaphoreType.DMA((5,)),
            pltpu.VMEM((SUBLANES, pixels), jnp.float32),
            pltpu.VMEM((2, SUBLANES, bins), jnp.float32),
            pltpu.VMEM((date_slots, LOW, LANES), jnp.float32),
            pltpu.VMEM((spaces, date_slots, LOW, LANES), jnp.float32),
            pltpu.VMEM((groups, date_slots, pixels), jnp.float32),
            pltpu.VMEM((groups, SUBLANES, pixels), jnp.float32),
            pltpu.VMEM((groups, SUBLANES, bins), jnp.float32),
            pltpu.VMEM((groups, SUBLANES, pixels), jnp.float32),
            pltpu.VMEM((groups, rest, pixels), jnp.float32),
            pltpu.SemaphoreType.DMA((spaces,)),
            pltpu.SemaphoreType.DMA((spaces,)),
            pltpu.SemaphoreType.DMA((groups,)),
            pltpu.SemaphoreType.DMA((groups,)),
            pltpu.SemaphoreType.DMA((groups,)),
            pltpu.SemaphoreType.DMA((groups,)),
            pltpu.SemaphoreType.DMA((groups,)),
            pltpu.SemaphoreType.DMA((groups,)),
            pltpu.SemaphoreType.DMA((groups,)),
            pltpu.SemaphoreType.DMA((groups,)),
        ],
        compiler_params=pltpu.CompilerParams(
            collective_id=0, has_side_effects=True, vmem_limit_bytes=16 * 2**20
        ),
    )(
        *(
            pltpu.with_memory_space_constraint(x, pltpu.HBM)
            for x in (live_dates, day_of_year, by_band, clear_sky, ref_quantile)
        )
    )
    return jnp.transpose(residual, (1, 0, 2))


def solution(mesh):
    return jax.shard_map(
        functools.partial(per_device, mesh.shape["date"], mesh.shape["space"]),
        mesh=mesh,
        in_specs=(
            P("date", None, ("tiles", "space")),
            P("date", ("tiles", "space")),
            P(),
            P(),
            P(),
        ),
        out_specs=P("date", None, ("tiles", "space")),
        check_vma=False,
    )
```

```python
import functools
import math

import jax
import jax.numpy as jnp
from jax import lax
from jax.experimental import pallas as pl
from jax.experimental.pallas import tpu as pltpu
from jax.sharding import PartitionSpec as P

MESH = pl.DeviceIdType.MESH
HARMONICS = 7
RIDGE = 1.0
YEAR = 365
LOW = 16
LANES = 128
SUBLANES = 8


def iota(shape, dim):
    return lax.broadcasted_iota(jnp.int32, shape, dim)


def rounded(x):
    return x.astype(jnp.bfloat16).astype(jnp.float32)


def three_parts(x):
    first = x.astype(jnp.bfloat16)
    rest = x - first.astype(jnp.float32)
    second = rest.astype(jnp.bfloat16)
    return first, second, (rest - second.astype(jnp.float32)).astype(jnp.bfloat16)


def row_slot_band(row, bands):
    whole = SUBLANES - bands
    slot = (row >= bands).astype(jnp.int32)
    band = jnp.where(
        row < bands, row, jnp.where(row < SUBLANES, row - bands + (bands - whole), row - SUBLANES)
    )
    return slot, band


def find_row(slot, band, bands):
    rest = 2 * bands - SUBLANES
    if slot == 0:
        return 0, band
    return (1, band) if band < rest else (0, bands + band - rest)


def block_histograms(values, valid, bands, bins):
    high_count = bins // LOW
    pixels = values[0].shape[1]
    high_iota = iota((high_count, pixels), 0).astype(jnp.float32)
    low_iota = iota((LOW, pixels), 0).astype(jnp.float32)
    marked, local, spill = [], [], []
    for group in range(2):
        position = jnp.clip(bins * values[group] - 0.5, 0.0, bins - 1.0)
        high = jnp.floor(position * (1.0 / LOW))
        local.append(position - LOW * high)
        marked.append(jnp.where(valid[group] > 0.5, high, -1.0))
        spill.append(jnp.maximum(0.0, 1.0 - jnp.abs(local[group] - LOW)))
    spill = jnp.concatenate(spill, axis=0).astype(jnp.bfloat16)
    band_lane = iota((LOW, LANES), 1) // high_count
    row_slot, row_band = row_slot_band(iota((2 * SUBLANES, LANES), 0), bands)
    own_lane = iota((2 * SUBLANES, LANES), 1) // high_count
    hot, tents = [], []
    for slot in range(2):
        for band in range(bands):
            group, row = find_row(slot, band, bands)
            one = marked[group][row : row + 1]
            hot.append(jnp.where(high_iota == one, 1.0, 0.0).astype(jnp.bfloat16))
            near = 1.0 - jnp.abs(local[group][row : row + 1] - low_iota)
            tents.append(jnp.maximum(0.0, near).astype(jnp.bfloat16))
        hot.append(jnp.zeros((LANES - bands * high_count, pixels), jnp.bfloat16))
    counts = lax.dot_general(
        jnp.concatenate(tents + [spill], axis=0),
        jnp.concatenate(hot, axis=0),
        (((1,), (1,)), ((), ())),
        preferred_element_type=jnp.float32,
    )
    inners, outers = [], []
    for slot in range(2):
        part = counts[:, slot * LANES : (slot + 1) * LANES]
        inner = jnp.zeros((LOW, LANES), jnp.float32)
        for band in range(bands):
            start = (slot * bands + band) * LOW
            inner += jnp.where(band_lane == band, part[start : start + LOW], 0.0)
        own = (row_slot == slot) & (row_band == own_lane)
        outer = jnp.where(own, part[2 * bands * LOW :], 0.0)
        inners.append(inner)
        outers.append(jnp.sum(outer, axis=0, keepdims=True))
    return inners, outers


def running_sums(inner, spill, bands, bins):
    high_count = bins // LOW
    dates = len(inner)
    used = bands * high_count
    column = [jnp.sum(inner[d], axis=0, keepdims=True) + spill[d] for d in range(dates)]
    rows = column + spill
    left = jnp.zeros((SUBLANES, LANES), jnp.float32)
    row_of = iota((SUBLANES, LANES), 0)
    for i, row in enumerate(rows):
        left = jnp.where(row_of == i, row, left)
    src, dst = iota((LANES, LANES), 0), iota((LANES, LANES), 1)
    same = (src // high_count == dst // high_count) & (dst < used)
    before = jnp.where((same & (src < dst)) | (dst == used + src // high_count), 1.0, 0.0)
    shift = jnp.where(same & (src + 1 == dst), 0.5, 0.0)
    before = jnp.where(src < used, before, 0.0)
    shift = jnp.where(src < used, shift, 0.0)
    parts = [part.astype(jnp.float32) for part in three_parts(left)] + [jnp.zeros_like(left)]
    moved = jnp.dot(
        jnp.concatenate(parts, axis=0).astype(jnp.bfloat16),
        jnp.concatenate([before, shift], axis=1).astype(jnp.bfloat16),
        preferred_element_type=jnp.float32,
    )
    moved = sum(moved[i * SUBLANES : (i + 1) * SUBLANES] for i in range(3))
    out_row, in_row = iota((LOW, 3 * LOW), 0), iota((LOW, 3 * LOW), 1) % LOW
    lower = jnp.where(in_row < out_row, 1.0, jnp.where(in_row == out_row, 0.5, 0.0))
    within = jnp.dot(
        lower.astype(jnp.bfloat16),
        jnp.concatenate(three_parts(jnp.concatenate(inner, axis=1)), axis=0),
        preferred_element_type=jnp.float32,
    )
    first = iota((LOW, LANES), 0) == 0
    sums = []
    for d in range(dates):
        part = within[:, d * LANES : (d + 1) * LANES] + moved[d : d + 1, :LANES]
        back = moved[dates + d : dates + d + 1, LANES:]
        sums.append(part - jnp.where(first, back, 0.0))
    return sums


def flat_tables(sums, bands, bins):
    high_count = bins // LOW
    used = bands * high_count
    lane = iota((SUBLANES, LANES), 1)
    total_lane = jnp.minimum(used + lane // high_count, LANES - 1)
    band_lane = iota((LOW, LANES), 1) // high_count
    wide = []
    for part in sums:
        total = jnp.take_along_axis(part[:SUBLANES], total_lane, axis=1)[:1]
        cumulative = (part / jnp.maximum(total, 1.0)).astype(jnp.bfloat16).astype(jnp.float32)
        wide += [jnp.where(band_lane == band, cumulative, 0.0) for band in range(bands)]
    src, dst = iota((LANES, bins), 0), iota((LANES, bins), 1)
    spread = jnp.where((src % high_count == dst // LOW) & (src < used), 1.0, 0.0)
    placed = jnp.dot(
        jnp.concatenate(wide, axis=0).astype(jnp.bfloat16),
        spread.astype(jnp.bfloat16),
        preferred_element_type=jnp.float32,
    )
    rows, cols = iota(placed.shape, 0), iota(placed.shape, 1)
    placed = jnp.where(rows % LOW == cols % LOW, placed, 0.0).astype(jnp.bfloat16)
    shape = (2 * SUBLANES, 2 * bands * LOW)
    slot, band = row_slot_band(iota(shape, 0), bands)
    pick = jnp.where((iota(shape, 1) // LOW == slot * bands + band) & (band < bands), 1.0, 0.0)
    tables = jnp.dot(pick.astype(jnp.bfloat16), placed, preferred_element_type=jnp.float32)
    return tables[:SUBLANES], tables[SUBLANES:]


def gather_lanes(table, index):
    parts = table.shape[1] // LANES
    inner = index % LANES
    out = jnp.take_along_axis(table[:, :LANES], inner, axis=1)
    for part in range(1, parts):
        other = jnp.take_along_axis(table[:, part * LANES : (part + 1) * LANES], inner, axis=1)
        out = jnp.where(index >= part * LANES, other, out)
    return out


def interpolate(table, position, bins):
    low = jnp.floor(position)
    first = low.astype(jnp.int32)
    second = jnp.minimum(first + 1, bins - 1)
    low_weight = rounded(1.0 - jnp.abs(position - low))
    high_weight = rounded(jnp.maximum(0.0, 1.0 - jnp.abs(position - (low + 1.0))))
    return low_weight * gather_lanes(table, first) + high_weight * gather_lanes(table, second)


def own_fit_rows(live_ref, day_ref, date_slots, dates, first_date):
    size = max(dates, SUBLANES)
    rows, cols = iota((size, size), 0), iota((size, size), 1)

    def place(t, carry):
        day_r, day_c, live_r, live_c = carry
        day = day_ref[t]
        live = (lax.rem(t, date_slots) < live_ref[lax.div(t, date_slots)]).astype(jnp.int32)
        return (
            jnp.where(rows == t, day, day_r),
            jnp.where(cols == t, day, day_c),
            jnp.where(rows == t, live, live_r),
            jnp.where(cols == t, live, live_c),
        )

    zero = jnp.zeros((size, size), jnp.int32)
    day_r, day_c, live_r, live_c = lax.fori_loop(
        0, dates, place, (zero, zero, zero, zero), unroll=dates <= 16
    )
    base = jnp.cos((2.0 * math.pi / YEAR) * (day_r - day_c).astype(jnp.float32))
    older, newer = jnp.ones_like(base), base
    total = older + newer
    for _ in range(HARMONICS - 1):
        older, newer = newer, 2.0 * base * newer - older
        total = total + newer
    eye = jnp.where(rows == cols, 1.0, 0.0)
    work = jnp.where((live_r * live_c) == 1, total, 0.0) + RIDGE * eye
    inverse = eye
    for k in range(dates):
        pivot = work[k : k + 1, k : k + 1]
        row_w, row_i = work[k : k + 1, :] / pivot, inverse[k : k + 1, :] / pivot
        column = work[:, k : k + 1]
        work = jnp.where(rows == k, row_w, work - column * row_w)
        inverse = jnp.where(rows == k, row_i, inverse - column * row_i)
    return [
        jnp.sum(jnp.where(rows == first_date + d, inverse, 0.0), axis=0, keepdims=True)
        for d in range(date_slots)
    ]


def kernel(
    groups,
    spaces,
    live_hbm,
    day_hbm,
    reflect_hbm,
    clear_hbm,
    quantile_hbm,
    out_ref,
    live_ref,
    day_ref,
    reflect_ref,
    clear_ref,
    quantile_ref,
    in_sems,
    late_raw,
    quant,
    hist_own,
    hist_all,
    mask_all,
    raw_all,
    table_all,
    early_all,
    late_all,
    hist_send,
    hist_recv,
    mask_send,
    mask_recv,
    raw_send,
    raw_recv,
    table_send,
    table_recv,
    late_send,
    late_recv,
):
    bands, date_slots, pixels = reflect_ref.shape
    bins = quantile_ref.shape[1]
    dates = date_slots * groups
    rest = 2 * bands - SUBLANES
    my_date, my_space = lax.axis_index("date"), lax.axis_index("space")
    space_peers = [lax.rem(my_space + i, spaces) for i in range(1, spaces)]

    def each_date_peer(body):
        def step(i, carry):
            body(i + jnp.where(my_date <= i, 1, 0))
            return carry

        if groups <= 8:
            for i in range(groups - 1):
                step(i, 0)
        else:
            lax.fori_loop(0, groups - 1, step, 0)

    def to_date(src, dst, send, recv, peer):
        return pltpu.make_async_remote_copy(
            src_ref=src,
            dst_ref=dst,
            send_sem=send,
            recv_sem=recv,
            device_id={"date": peer},
            device_id_type=MESH,
        )

    def mask_copy(peer, slot):
        return to_date(
            mask_all.at[slot], mask_all.at[slot], mask_send.at[peer], mask_recv.at[slot], peer
        )

    def raw_copy(peer, slot):
        return to_date(
            raw_all.at[slot], raw_all.at[slot], raw_send.at[peer], raw_recv.at[slot], peer
        )

    def table_copy(peer, slot):
        return to_date(
            table_all.at[slot], table_all.at[slot], table_send.at[peer], table_recv.at[slot], peer
        )

    def late_copy(peer, slot):
        return to_date(
            late_all.at[slot], late_all.at[slot], late_send.at[peer], late_recv.at[slot], peer
        )

    loads = [
        pltpu.make_async_copy(src, dst, in_sems.at[i])
        for i, (src, dst) in enumerate(
            (
                (reflect_hbm, reflect_ref),
                (clear_hbm, clear_ref),
                (live_hbm, live_ref),
                (day_hbm, day_ref),
                (quantile_hbm, quantile_ref),
            )
        )
    ]
    for load in loads:
        load.start()

    barrier = pltpu.get_barrier_semaphore()
    for peer in space_peers:
        pl.semaphore_signal(barrier, inc=1, device_id={"space": peer}, device_id_type=MESH)
    each_date_peer(
        lambda peer: pl.semaphore_signal(
            barrier, inc=1, device_id={"date": peer}, device_id_type=MESH
        )
    )

    late_raw[...] = jnp.zeros_like(late_raw)
    for load in loads[:3]:
        load.wait()
    for d in range(date_slots):
        for b in range(bands):
            group, row = find_row(d, b, bands)
            values = reflect_ref[b, d : d + 1, :]
            if group == 0:
                raw_all[my_date, row : row + 1, :] = values
            else:
                late_raw[row : row + 1, :] = values

    for d in range(date_slots):
        live = lax.rem(jnp.int32(d), date_slots) < live_ref[my_date]
        valid = clear_ref[d : d + 1, :] * live.astype(jnp.int32)
        mask_all[my_date, d : d + 1, :] = valid.astype(jnp.float32)

    def send_raw(peer):
        raw_copy(peer, my_date).start()
        mask_copy(peer, my_date).start()

    @pl.when(my_date >= groups // 2)
    def _():
        pl.semaphore_wait(barrier, groups + spaces - 2)
        each_date_peer(send_raw)

    def row_mask(slot, span):
        size = span.stop - span.start
        slots, _ = row_slot_band(iota((SUBLANES, size), 0), bands)
        return jnp.where(slots == 0, mask_all[slot, 0:1, span], mask_all[slot, 1:2, span])

    everything = slice(0, pixels)
    inner, spill = block_histograms(
        (raw_all[my_date], late_raw[...]),
        (
            row_mask(my_date, everything),
            jnp.broadcast_to(mask_all[my_date, 1:2, :], (SUBLANES, pixels)),
        ),
        bands,
        bins,
    )
    sums = running_sums(inner, spill, bands, bins)
    for d in range(date_slots):
        hist_own[d] = sums[d]

    @pl.when(my_date < groups // 2)
    def _():
        pl.semaphore_wait(barrier, groups + spaces - 2)

    hist_copies = []
    for peer in space_peers:
        copy = pltpu.make_async_remote_copy(
            src_ref=hist_own,
            dst_ref=hist_all.at[my_space],
            send_sem=hist_send.at[peer],
            recv_sem=hist_recv.at[my_space],
            device_id={"space": peer},
            device_id_type=MESH,
        )
        copy.start()
        hist_copies.append(copy)

    @pl.when(my_date < groups // 2)
    def _():
        each_date_peer(send_raw)

    for load in loads[3:]:
        load.wait()
    quant[...] = jnp.zeros_like(quant)
    for d in range(date_slots):
        for b in range(bands):
            group, row = find_row(d, b, bands)
            quant[group, row : row + 1, :] = rounded(quantile_ref[b : b + 1, :])
    fit_rows = own_fit_rows(live_ref, day_ref, date_slots, dates, my_date * date_slots)

    total = [hist_own[d] for d in range(date_slots)]
    for peer in space_peers:
        pltpu.make_async_remote_copy(
            src_ref=hist_own,
            dst_ref=hist_all.at[peer],
            send_sem=hist_send.at[peer],
            recv_sem=hist_recv.at[peer],
            device_id={"space": peer},
            device_id_type=MESH,
        ).wait_recv()
        for d in range(date_slots):
            total[d] = total[d] + hist_all[peer, d]

    early_table, late_table = flat_tables(total, bands, bins)
    table_all[my_date] = early_table
    each_date_peer(lambda peer: table_copy(peer, my_date).start())

    def match(table, values, group):
        position = jnp.clip(bins * values - 0.5, 0.0, bins - 1.0)
        level = interpolate(table, position, bins)
        level = jnp.clip(bins * level - 0.5, 0.0, bins - 1.0)
        return interpolate(quant[group], level, bins)

    def match_early(slot):
        for start in range(0, pixels, LANES):
            span = slice(start, start + LANES)
            matched = match(table_all[slot], raw_all[slot, :, span], 0)
            early_all[slot, :, span] = matched * row_mask(slot, span)

    for start in range(0, pixels, LANES):
        span = slice(start, start + LANES)
        matched = match(late_table, late_raw[:, span], 1)[:rest]
        late_all[my_date, :, span] = matched * mask_all[my_date, 1:2, span]
    each_date_peer(lambda peer: late_copy(peer, my_date).start())

    match_early(my_date)

    def arrived(peer):
        mask_copy(peer, peer).wait_recv()
        raw_copy(peer, peer).wait_recv()
        table_copy(peer, peer).wait_recv()
        match_early(peer)

    each_date_peer(arrived)

    row_slot, _ = row_slot_band(iota((SUBLANES, 1), 0), bands)
    count = jnp.zeros((1, pixels), jnp.float32)
    gaps = [jnp.zeros((1, pixels), jnp.float32) for _ in range(date_slots)]
    summed = jnp.zeros((SUBLANES, pixels), jnp.float32)
    fits = [jnp.zeros((SUBLANES, pixels), jnp.float32) for _ in range(date_slots)]
    for g in range(groups):
        series = early_all[g]
        summed += series
        for d in range(date_slots):
            first, second = (fit_rows[d][:, 2 * g + s : 2 * g + s + 1] for s in range(2))
            fits[d] += jnp.where(row_slot == 0, first, second) * series
        for s in range(date_slots):
            mask = mask_all[g, s : s + 1, :]
            count += mask
            for d in range(date_slots):
                gaps[d] += fit_rows[d][:, 2 * g + s : 2 * g + s + 1] * (1.0 - mask)
    share = 1.0 / jnp.maximum(count, 1.0)
    gaps = [gap * share for gap in gaps]

    def finish(d, row, value):
        out_ref[row, d : d + 1, :] = value

    for b in range(rest, bands):
        other = bands + b - rest
        mean = summed[b : b + 1] + summed[other : other + 1]
        for d in range(date_slots):
            fit = fits[d][b : b + 1] + fits[d][other : other + 1] + gaps[d] * mean
            finish(d, b, mask_all[my_date, d : d + 1, :] * fit)

    each_date_peer(lambda peer: late_copy(peer, peer).wait_recv())
    summed = summed[:rest]
    fits = [fit[:rest] for fit in fits]
    for g in range(groups):
        series = late_all[g]
        summed += series
        for d in range(date_slots):
            fits[d] += fit_rows[d][:, 2 * g + 1 : 2 * g + 2] * series
    for d in range(date_slots):
        left = mask_all[my_date, d : d + 1, :] * (fits[d] + gaps[d] * summed)
        for b in range(rest):
            finish(d, b, left[b : b + 1])

    for copy in hist_copies:
        copy.wait_send()

    def sent(peer):
        raw_copy(peer, my_date).wait_send()
        mask_copy(peer, my_date).wait_send()
        table_copy(peer, my_date).wait_send()
        late_copy(peer, my_date).wait_send()

    each_date_peer(sent)


def per_device(groups, spaces, reflect, clear_sky, live_dates, day_of_year, ref_quantile):
    date_slots, bands, pixels = reflect.shape
    bins = ref_quantile.shape[1]
    rest = 2 * bands - SUBLANES
    by_band = jnp.transpose(reflect, (1, 0, 2))
    residual = pl.pallas_call(
        functools.partial(kernel, groups, spaces),
        out_shape=jax.ShapeDtypeStruct(by_band.shape, jnp.float32),
        in_specs=[pl.BlockSpec(memory_space=pltpu.HBM)] * 5,
        out_specs=pl.BlockSpec(memory_space=pltpu.VMEM),
        scratch_shapes=[
            pltpu.SMEM(live_dates.shape, jnp.int32),
            pltpu.SMEM(day_of_year.shape, jnp.int32),
            pltpu.VMEM(by_band.shape, jnp.float32),
            pltpu.VMEM(clear_sky.shape, jnp.int32),
            pltpu.VMEM(ref_quantile.shape, jnp.float32),
            pltpu.SemaphoreType.DMA((5,)),
            pltpu.VMEM((SUBLANES, pixels), jnp.float32),
            pltpu.VMEM((2, SUBLANES, bins), jnp.float32),
            pltpu.VMEM((date_slots, LOW, LANES), jnp.float32),
            pltpu.VMEM((spaces, date_slots, LOW, LANES), jnp.float32),
            pltpu.VMEM((groups, date_slots, pixels), jnp.float32),
            pltpu.VMEM((groups, SUBLANES, pixels), jnp.float32),
            pltpu.VMEM((groups, SUBLANES, bins), jnp.float32),
            pltpu.VMEM((groups, SUBLANES, pixels), jnp.float32),
            pltpu.VMEM((groups, rest, pixels), jnp.float32),
            pltpu.SemaphoreType.DMA((spaces,)),
            pltpu.SemaphoreType.DMA((spaces,)),
            pltpu.SemaphoreType.DMA((groups,)),
            pltpu.SemaphoreType.DMA((groups,)),
            pltpu.SemaphoreType.DMA((groups,)),
            pltpu.SemaphoreType.DMA((groups,)),
            pltpu.SemaphoreType.DMA((groups,)),
            pltpu.SemaphoreType.DMA((groups,)),
            pltpu.SemaphoreType.DMA((groups,)),
            pltpu.SemaphoreType.DMA((groups,)),
        ],
        compiler_params=pltpu.CompilerParams(
            collective_id=0, has_side_effects=True, vmem_limit_bytes=16 * 2**20
        ),
    )(
        *(
            pltpu.with_memory_space_constraint(x, pltpu.HBM)
            for x in (live_dates, day_of_year, by_band, clear_sky, ref_quantile)
        )
    )
    return jnp.transpose(residual, (1, 0, 2))


def solution(mesh):
    return jax.shard_map(
        functools.partial(per_device, mesh.shape["date"], mesh.shape["space"]),
        mesh=mesh,
        in_specs=(
            P("date", None, ("tiles", "space")),
            P("date", ("tiles", "space")),
            P(),
            P(),
            P(),
        ),
        out_specs=P("date", None, ("tiles", "space")),
        check_vma=False,
    )
```
